256 devices in a mesh: src: 16 (over y_hi, x, core), tgt: 16 (over z, y_lo).
Axes of the slice: x: 4, y: 4 (y_hi: 2, y_lo: 2; y = y_hi * 2 + y_lo), z: 8, core: 2. Of those that a mesh axis runs over, the one named last changes fastest.
Arguments:
- source_cells: bfloat16 [32, 524288], P(None, 'src'), may hold values from -4 to 4
- target_cells: bfloat16 [32, 524288], P(None, 'tgt'), may hold values from -4 to 4
- source_mass: float32 [524288], P('src'), may hold values from 0.5 to 2
- target_mass: float32 [524288], P('tgt'), may hold values from 0.5 to 2
- source_count: int32 [2048], P('src'), may hold values from 1 to 256, 393216 in all
- target_count: int32 [2048], P('tgt'), may hold values from 1 to 256, 393216 in all
- pair_lists: int32 [2048, 8], P('src'), may hold values from 0 to 2047, as said below
Outputs:
- source_potential: float32 [524288], P('src')
- target_potential: float32 [524288], P('tgt')
- mapped: float32 [32, 524288], P(None, ('src', 'tgt'))
The draws below stay inside these ranges and needn't reach their ends.
Inputs may be any that keep to these rules, and one draw needn't show every extreme that they name: `pair_lists`: each row names 8 different target clusters, and every target cluster is named by some row. Within the rows of one index of src, the target clusters of one index of tgt are named 128 times in all, those of the next index of tgt (wrapping around) never, and those of every other index of tgt 128 // 2 times.
All inputs are finite; a program needn't handle non-finite values. No bound on the sum of `source_count` or of `target_count` on one device may be relied on, other than what follows from the above.
Results may differ from the reference program's by a relative error of at most 0.0003.
Values may be sent and summed in bfloat16 or wider, within the bound.
A program may use at most 64 MiB of HBM per device.

```python
import math
import jax
import jax.numpy as jnp
import numpy as np
from jax import lax

D = 32
TILE = 256
LIST = 8
ITERS = 2
CS_DEV = 128
CT_DEV = 128
NCS = 2048
NCT = 2048
N_SRC = 16
N_TGT = 16


def draw_source_cells(key, part):
    key = jax.random.fold_in(key, 5)
    key_values = jax.random.fold_in(key, 0)
    values = jnp.clip(0.5 * jax.random.normal(key_values, (D, NCS * TILE), jnp.float32), -3.0, 3.0)
    return values.astype(jnp.bfloat16)


def draw_target_cells(key, part):
    key = jax.random.fold_in(key, 7)
    key_values = jax.random.fold_in(key, 0)
    values = jnp.clip(0.5 * jax.random.normal(key_values, (D, NCT * TILE), jnp.float32), -3.0, 3.0)
    return values.astype(jnp.bfloat16)


def draw_pair_lists(key, part):
    key = jax.random.fold_in(key, 9)
    key_rotation, key_order = jax.random.split(key)
    slot_count = CS_DEV * LIST
    spread_count = slot_count // N_TGT
    rotation = jax.random.randint(key_rotation, (), 0, N_TGT)
    src_blocks = jnp.arange(N_SRC, dtype=jnp.int32)
    tgt_blocks = jnp.arange(N_TGT, dtype=jnp.int32)
    busy_block = (src_blocks + rotation) % N_TGT
    quiet_block = (busy_block + 1) % N_TGT
    block_loads = jnp.where(tgt_blocks[None, :] == busy_block[:, None], 2 * spread_count, spread_count)
    block_loads = jnp.where(tgt_blocks[None, :] == quiet_block[:, None], 0, block_loads).astype(jnp.int32)
    bounds = jnp.cumsum(block_loads, axis=1)
    orders = jax.vmap(lambda sub_key: jax.random.permutation(sub_key, slot_count))(jax.random.split(key_order, N_SRC))
    owners = jnp.sum((orders[:, :, None] >= bounds[:, None, :]).astype(jnp.int32), axis=2)
    onehot = (owners[:, :, None] == tgt_blocks[None, None, :]).astype(jnp.int32)
    slot_ranks = jnp.sum((jnp.cumsum(onehot, axis=1) - onehot) * onehot, axis=2)
    offsets = jnp.cumsum(block_loads, axis=0) - block_loads
    first_cluster = jnp.sum(offsets[:, None, :] * onehot, axis=2)
    cluster = (first_cluster + slot_ranks) % CT_DEV
    return (owners * CT_DEV + cluster).reshape(N_SRC * CS_DEV, LIST).astype(jnp.int32)


def levels(key, extent, pieces, low, largest):
    level = 1.0
    for axis_at, parts in pieces:
        draws = jax.random.uniform(jax.random.fold_in(jax.random.fold_in(key, 6), axis_at), (parts,), jnp.float32, low / len(pieces), largest / len(pieces))
        level = level * jnp.repeat(jnp.exp(draws), extent[axis_at] // parts).reshape((-1,) + (1,) * (len(extent) - 1 - axis_at))
    return level


def profile(number_of, total, most, slope):
    portions = [(1 << 20) // math.isqrt(grade ** slope) + 1 for grade in range(2, number_of + 1)]
    spare, holding = total - most - (number_of - 1), [1] * (number_of - 1)
    while spare > 0:
        candidates = [i for i in range(number_of - 1) if holding[i] < most]
        mass, left = sum([portions[i] for i in candidates]), spare
        for i in candidates:
            extra = min(most - holding[i], max(1, left * portions[i] // mass), spare)
            holding[i] = holding[i] + extra
            spare = spare - extra
    return np.array([most] + holding)


def uneven_parts(own_key, number_of, total, reach, lean):
    if number_of == 2:
        one = jax.random.randint(own_key, (), max(1, total - reach), min(reach, total - 1) + 1)
        return jnp.stack([one, total - one])
    tallies = jnp.asarray(profile(number_of, total, reach, lean), jnp.int32)
    pairs = (number_of - 1) // 2
    donor, sink = tallies[1:1 + 2 * pairs:2], tallies[2:2 + 2 * pairs:2]
    slack = jnp.minimum(donor - 1, reach - sink)
    shifted = jax.random.randint(jax.random.fold_in(own_key, 1), (pairs,), 0, 1 << 20) % (slack + 1)
    tallies = tallies.at[1:1 + 2 * pairs:2].set(donor - shifted).at[2:2 + 2 * pairs:2].set(sink + shifted)
    return tallies[jax.random.permutation(jax.random.fold_in(own_key, 2), number_of)]


def setup_inputs(seed: int = 0) -> dict:
    splits = jax.random.split(jax.random.key(seed), 8)
    return {
        "source_cells": draw_source_cells(jax.random.fold_in(splits[7], 71), 0),
        "target_cells": draw_target_cells(jax.random.fold_in(splits[7], 71), 0),
        "source_mass": jnp.clip(jnp.exp(math.log(2.0) - 1.3862944 * jax.random.uniform(splits[2], (NCS * TILE,), jnp.float32) ** levels(splits[2], (NCS * TILE,), ((0, 16),), -0.2, 0.2)), 0.5, 2.0),
        "target_mass": jnp.clip(jnp.exp(math.log(2.0) - 1.3862944 * jax.random.uniform(splits[3], (NCT * TILE,), jnp.float32) ** levels(splits[3], (NCT * TILE,), ((0, 16),), -0.2, 0.2)), 0.5, 2.0),
        "source_count": uneven_parts(splits[4], NCS, 3 * NCS * TILE // 4, TILE, 0).astype(jnp.int32),
        "target_count": uneven_parts(splits[5], NCT, 3 * NCT * TILE // 4, TILE, 0).astype(jnp.int32),
        "pair_lists": draw_pair_lists(jax.random.fold_in(splits[7], 71), 0),
    }


entropy_blur = 0.5
empty_peak = -1.0e30


def squared_norms(cells):
    widened = cells.astype(jnp.float32)
    return jnp.sum(widened * widened, axis=0)


def potential(logmass, usable, highest, totals):
    safe_totals = jnp.where(usable, totals, 1.0)
    return jnp.where(usable, entropy_blur * logmass - entropy_blur * (highest + jnp.log(safe_totals)), 0.0)


def reference(source_cells, target_cells, source_mass, target_mass, source_count, target_count, pair_lists):
    features = source_cells.shape[0]
    src_tiles = jnp.transpose(source_cells.reshape(features, NCS, TILE), (1, 0, 2))
    tgt_tiles = jnp.transpose(target_cells.reshape(features, NCT, TILE), (1, 0, 2))
    src_norm = squared_norms(source_cells).reshape(NCS, TILE)
    tgt_norm = squared_norms(target_cells).reshape(NCT, TILE)
    position = jnp.arange(TILE, dtype=jnp.int32)
    src_usable = position[None, :] < source_count[:, None]
    tgt_usable = position[None, :] < target_count[:, None]
    src_logmass = jnp.log(source_mass).reshape(NCS, TILE)
    tgt_logmass = jnp.log(target_mass).reshape(NCT, TILE)
    cluster_ids = jnp.arange(NCS, dtype=jnp.int32)

    def distances(cluster):
        target_ids = pair_lists[cluster]
        src_block = src_tiles[cluster].astype(jnp.float32)
        tgt_block = tgt_tiles[target_ids].astype(jnp.float32)
        cross_term = jnp.einsum("di,kdj->ikj", src_block, tgt_block, precision=lax.Precision.HIGHEST)
        distance = src_norm[cluster][:, None, None] + tgt_norm[target_ids][None, :, :] - 2.0 * cross_term
        return target_ids, tgt_block, distance

    def row_weights(cluster, target_pot):
        target_ids, tgt_block, distance = distances(cluster)
        usable = tgt_usable[target_ids][None, :, :]
        scores = jnp.where(usable, (target_pot[target_ids][None, :, :] - distance) / entropy_blur, empty_peak)
        highest = jnp.max(scores, axis=(1, 2))
        weight = jnp.where(usable, jnp.exp(scores - highest[:, None, None]), 0.0)
        return tgt_block, highest, weight

    def source_update(target_pot):
        def per_cluster(cluster):
            tgt_block, highest, weight = row_weights(cluster, target_pot)
            return highest, jnp.sum(weight, axis=(1, 2))

        highest, totals = lax.map(per_cluster, cluster_ids)
        return potential(src_logmass, src_usable, highest, totals)

    def target_update(source_pot):
        def per_cluster(cluster):
            target_ids, tgt_block, distance = distances(cluster)
            usable = src_usable[cluster][:, None, None]
            scores = jnp.where(usable, (source_pot[cluster][:, None, None] - distance) / entropy_blur, empty_peak)
            highest = jnp.max(scores, axis=0)
            totals = jnp.sum(jnp.where(usable, jnp.exp(scores - highest[None]), 0.0), axis=0)
            return highest, totals

        highest, totals = lax.map(per_cluster, cluster_ids)
        flat_ids = pair_lists.reshape(-1)
        highest = highest.reshape(-1, TILE)
        totals = totals.reshape(-1, TILE)
        column_max = jnp.full((NCT, TILE), empty_peak, jnp.float32).at[flat_ids].max(highest)
        rescaled = totals * jnp.exp(highest - column_max[flat_ids])
        column_sum = jnp.zeros((NCT, TILE), jnp.float32).at[flat_ids].add(rescaled)
        return potential(tgt_logmass, tgt_usable, column_max, column_sum)

    def barycentre(target_pot):
        def per_cluster(cluster):
            tgt_block, highest, weight = row_weights(cluster, target_pot)
            totals = jnp.sum(weight, axis=(1, 2))
            numerator = jnp.einsum("ikj,kdj->di", weight, tgt_block, precision=lax.Precision.HIGHEST)
            usable = src_usable[cluster]
            return jnp.where(usable[None, :], numerator / jnp.where(usable, totals, 1.0)[None, :], 0.0)

        mapped = lax.map(per_cluster, cluster_ids)
        return jnp.transpose(mapped, (1, 0, 2)).reshape(features, NCS * TILE)

    target_pot = jnp.zeros((NCT, TILE), jnp.float32)
    source_pot = jnp.zeros((NCS, TILE), jnp.float32)
    for sweep_index in range(ITERS):
        source_pot = source_update(target_pot)
        target_pot = target_update(source_pot)
    mapped = barycentre(target_pot)
    return source_pot.reshape(-1), target_pot.reshape(-1), mapped
```

```python
import functools

import jax
import jax.numpy as jnp
from jax import lax
from jax.experimental import pallas as pl
from jax.experimental.pallas import tpu as pltpu
from jax.sharding import PartitionSpec as P

ITERS = 2
MESH = pl.DeviceIdType.MESH
EMPTY = -1e30
TILE = 256
SUB = 8
AUX = 16
MAPROWS = 40
MIB = 1 << 20


def split3(row):
    high = row.astype(jnp.bfloat16).astype(jnp.float32)
    rest = row - high
    mid = rest.astype(jnp.bfloat16).astype(jnp.float32)
    low = rest - mid
    return high, mid, low


def cluster_row(ref, cluster):
    first = ref[pl.ds(2 * cluster, 1), :]
    second = ref[pl.ds(2 * cluster + 1, 1), :]
    return jnp.concatenate([first, second], axis=1)


def aux_rows(row, offset, other):
    at = lax.broadcasted_iota(jnp.int32, (AUX, TILE), 0)
    high, mid, low = split3(row)
    out = jnp.where((at >= other) & (at < other + 3), 1.0, 0.0)
    out = jnp.where(at == offset, high, out)
    out = jnp.where(at == offset + 1, mid, out)
    out = jnp.where(at == offset + 2, low, out)
    return out.astype(jnp.bfloat16)


def cells_of(ref, cluster):
    return ref[:, pl.ds(pl.multiple_of(cluster * TILE, TILE), TILE)]


def sweep_kernel(kind, sub_ids, lane_ids, count, sub_cells, lane_cells, sub_pot, lane_pot, out, *scratch):
    clusters = lane_cells.shape[1] // TILE
    if kind == "max":
        top, total = scratch
        top[...] = jnp.full(top.shape, EMPTY, jnp.float32)
        total[...] = jnp.zeros(total.shape, jnp.float32)
    elif kind == "sum":
        (total,) = scratch
        total[...] = jnp.zeros(total.shape, jnp.float32)
    else:
        out[...] = jnp.zeros(out.shape, jnp.float32)

    def tile(p):
        a, b = sub_ids[p], lane_ids[p]
        sub = cells_of(sub_cells, a)
        lane = cells_of(lane_cells, b)
        sub_aux = aux_rows(cluster_row(sub_pot, a), 0, 3)
        lane_aux = aux_rows(cluster_row(lane_pot, b), 3, 0)
        left = jnp.concatenate([sub, sub_aux], axis=0)
        right = jnp.concatenate([lane * jnp.bfloat16(4.0), lane_aux], axis=0)
        score = lax.dot_general(left, right, (((0,), (0,)), ((), ())), preferred_element_type=jnp.float32)
        if kind == "max":
            score = score.reshape(TILE // SUB, SUB, TILE)
            old = top[b]
            new = jnp.maximum(old, jnp.max(score, axis=0))
            part = jnp.sum(jnp.exp(score - new[None]), axis=0)
            total[b] = total[b] * jnp.exp(old - new) + part
            top[b] = new
        elif kind == "sum":
            weight = jnp.exp(score).reshape(TILE // SUB, SUB, TILE)
            total[b] = total[b] + jnp.sum(weight, axis=0)
        else:
            weight = jnp.exp(score)
            high = weight.astype(jnp.bfloat16)
            low = (weight - high.astype(jnp.float32)).astype(jnp.bfloat16)
            ones = jnp.where(lax.broadcasted_iota(jnp.int32, (AUX, TILE), 0) == 0, 1.0, 0.0).astype(jnp.bfloat16)
            cells = jnp.concatenate([sub, ones], axis=0)
            moved = jnp.dot(cells, high, preferred_element_type=jnp.float32)
            moved = moved + jnp.dot(cells, low, preferred_element_type=jnp.float32)
            out[b] = out[b] + moved[:MAPROWS]

    pl.loop(0, count[0])(tile)

    if kind == "map":
        return

    per = out.shape[2] // 2

    def finish(c):
        shard, at = c // per, c % per
        if kind == "max":
            best = jnp.max(top[c], axis=0, keepdims=True)
            row = jnp.sum(total[c] * jnp.exp(top[c] - best), axis=0, keepdims=True)
            rows = (best, row)
        else:
            rows = (jnp.sum(total[c], axis=0, keepdims=True),)
        for q, value in enumerate(rows):
            out[shard, q, pl.ds(2 * at, 1), :] = value[:, :128]
            out[shard, q, pl.ds(2 * at + 1, 1), :] = value[:, 128:]

    pl.loop(0, clusters)(finish)


def sweep(kind, shards, sub_ids, lane_ids, count, sub_cells, lane_cells, sub_pot, lane_pot):
    clusters = lane_cells.shape[1] // TILE
    if kind == "map":
        out = jax.ShapeDtypeStruct((clusters, MAPROWS, TILE), jnp.float32)
        scratch = []
    else:
        many = 2 if kind == "max" else 1
        out = jax.ShapeDtypeStruct((shards, many, 2 * clusters // shards, 128), jnp.float32)
        scratch = [pltpu.VMEM((clusters, SUB, TILE), jnp.float32)] * many
    smem = pl.BlockSpec(memory_space=pltpu.SMEM)
    vmem = pl.BlockSpec(memory_space=pltpu.VMEM)
    return pl.pallas_call(
        functools.partial(sweep_kernel, kind),
        out_shape=out,
        in_specs=[smem] * 3 + [vmem] * 4,
        out_specs=vmem,
        scratch_shapes=scratch,
        compiler_params=pltpu.CompilerParams(vmem_limit_bytes=48 * MIB),
        name="sweep_" + kind,
    )(sub_ids, lane_ids, count, sub_cells, lane_cells, sub_pot, lane_pot)


def greet(axis, n):
    me = lax.axis_index(axis)
    barrier = pltpu.get_barrier_semaphore()
    for k in range(1, n):
        pl.semaphore_signal(barrier, inc=1, device_id={axis: lax.rem(me + k, n)}, device_id_type=MESH)
    pl.semaphore_wait(barrier, n - 1)
    return me


def reduce_kernel(kind, axis, n, part, old, logmass, out, held, send1, recv1, send2, recv2):
    me = greet(axis, n)
    rows = old.shape[0] // n
    copies = []
    for k in range(1, n):
        peer = lax.rem(me + k, n)
        copy = pltpu.make_async_remote_copy(
            src_ref=part.at[peer], dst_ref=held.at[k], send_sem=send1.at[k], recv_sem=recv1.at[k],
            device_id={axis: peer}, device_id_type=MESH)
        copy.start()
        copies.append(copy)
    for copy in copies:
        copy.wait()
    mine = pl.ds(pl.multiple_of(me * rows, rows), rows)
    if kind == "max":
        best = part[me, 0]
        for k in range(1, n):
            best = jnp.maximum(best, held[k, 0])
        total = part[me, 1] * jnp.exp(part[me, 0] - best)
        for k in range(1, n):
            total = total + held[k, 1] * jnp.exp(held[k, 0] - best)
        lse = best + jnp.log(total)
    else:
        total = part[me, 0]
        for k in range(1, n):
            total = total + held[k, 0]
        lse = jnp.log(jnp.where(total > 0.0, total, 1.0))
    mass = logmass[mine, :]
    out[mine, :] = jnp.where(mass > 0.5 * EMPTY, old[mine, :] + mass - lse, EMPTY)
    copies = []
    for k in range(1, n):
        peer = lax.rem(me + k, n)
        copy = pltpu.make_async_remote_copy(
            src_ref=out.at[mine], dst_ref=out.at[mine], send_sem=send2.at[k], recv_sem=recv2.at[k],
            device_id={axis: peer}, device_id_type=MESH)
        copy.start()
        copies.append(copy)
    for copy in copies:
        copy.wait()


def reduce(kind, axis, ident, part, old, logmass):
    n = part.shape[0]
    vmem = pl.BlockSpec(memory_space=pltpu.VMEM)
    return pl.pallas_call(
        functools.partial(reduce_kernel, kind, axis, n),
        out_shape=jax.ShapeDtypeStruct(old.shape, jnp.float32),
        in_specs=[vmem] * 3,
        out_specs=vmem,
        scratch_shapes=[pltpu.VMEM(part.shape, jnp.float32)] + [pltpu.SemaphoreType.DMA((n,))] * 4,
        compiler_params=pltpu.CompilerParams(collective_id=ident, has_side_effects=True, vmem_limit_bytes=32 * MIB),
        name="reduce_" + kind + "_" + axis,
    )(part, old, logmass)


def scatter_kernel(axis, n, moved, out, held, send, recv, own):
    me = greet(axis, n)
    per = moved.shape[0] // n
    copies = []
    for k in range(1, n):
        peer = lax.rem(me + k, n)
        copy = pltpu.make_async_remote_copy(
            src_ref=moved.at[pl.ds(peer * per, per)], dst_ref=held.at[k], send_sem=send.at[k], recv_sem=recv.at[k],
            device_id={axis: peer}, device_id_type=MESH)
        copy.start()
        copies.append(copy)
    local = pltpu.make_async_copy(moved.at[pl.ds(me * per, per)], held.at[0], own)
    local.start()
    local.wait()
    for copy in copies:
        copy.wait()

    features = out.shape[0]

    def one(c):
        total = held[0, c]
        for k in range(1, n):
            total = total + held[k, c]
        weight = total[features:features + 1]
        weight = jnp.where(weight > 0.0, weight, 1.0)
        out[:, pl.ds(pl.multiple_of(c * TILE, TILE), TILE)] = total[:features] / weight

    pl.loop(0, per)(one)


def scatter(axis, ident, n, features, moved):
    clusters = moved.shape[0]
    per = clusters // n
    return pl.pallas_call(
        functools.partial(scatter_kernel, axis, n),
        out_shape=jax.ShapeDtypeStruct((features, per * TILE), jnp.float32),
        in_specs=[pl.BlockSpec(memory_space=pl.ANY)],
        out_specs=pl.BlockSpec(memory_space=pltpu.VMEM),
        scratch_shapes=[
            pltpu.VMEM((n, per) + moved.shape[1:], jnp.float32),
            pltpu.SemaphoreType.DMA((n,)),
            pltpu.SemaphoreType.DMA((n,)),
            pltpu.SemaphoreType.DMA,
        ],
        compiler_params=pltpu.CompilerParams(collective_id=ident, has_side_effects=True, vmem_limit_bytes=48 * MIB),
        name="scatter",
    )(moved)


def pair_table(pair_lists, tgt_block, per_block, capacity):
    width = pair_lists.shape[1]
    flat = pair_lists.reshape(-1)
    chosen = flat // per_block == tgt_block
    rank = jnp.cumsum(chosen.astype(jnp.int32)) - 1
    slots = jnp.arange(capacity, dtype=jnp.int32)
    matches = (rank[None, :] == slots[:, None]) & chosen[None, :]
    sources = jnp.arange(flat.shape[0], dtype=jnp.int32) // width
    pair_src = jnp.sum(jnp.where(matches, sources[None, :], 0), axis=1)
    pair_tgt = jnp.sum(jnp.where(matches, (flat % per_block)[None, :], 0), axis=1)
    return pair_src, pair_tgt, jnp.sum(chosen.astype(jnp.int32)).reshape(1)


def side(cells, mass, count):
    clusters = count.shape[0]
    wide = cells.astype(jnp.float32)
    norm = jnp.sum(wide * wide, axis=0).reshape(2 * clusters, 128)
    place = jnp.arange(2, dtype=jnp.int32)[None, :, None] * 128 + jnp.arange(128, dtype=jnp.int32)[None, None, :]
    live = (place < count[:, None, None]).reshape(2 * clusters, 128)
    logmass = jnp.where(live, jnp.log(mass).reshape(2 * clusters, 128), EMPTY)
    return norm, live, logmass


def shards(source_cells, target_cells, source_mass, target_mass, source_count, target_count, pair_lists):
    features = source_cells.shape[0]
    n_src, n_tgt = lax.axis_size("src"), lax.axis_size("tgt")
    capacity = 2 * pair_lists.size // n_tgt
    own_src, own_tgt, own = pair_table(pair_lists, lax.axis_index("tgt"), target_count.shape[0], capacity)
    src_norm, src_live, src_logmass = side(source_cells, source_mass, source_count)
    tgt_norm, tgt_live, tgt_logmass = side(target_cells, target_mass, target_count)
    u = -2.0 * src_norm
    v = jnp.where(tgt_live, -2.0 * tgt_norm, EMPTY)
    for step in range(ITERS):
        kind = "max" if step == 0 else "sum"
        part = sweep(kind, n_tgt, own_tgt, own_src, own, target_cells, source_cells, v, u)
        u = reduce(kind, "tgt", 2 * step, part, u, src_logmass)
        part = sweep(kind, n_src, own_src, own_tgt, own, source_cells, target_cells, u, v)
        v = reduce(kind, "src", 2 * step + 1, part, v, tgt_logmass)
    moved = sweep("map", n_tgt, own_tgt, own_src, own, target_cells, source_cells, v, u)
    mapped = scatter("tgt", 2 * ITERS, n_tgt, features, moved)
    source_pot = jnp.where(src_live, 0.5 * u + src_norm, 0.0)
    target_pot = jnp.where(tgt_live, 0.5 * v + tgt_norm, 0.0)
    return source_pot.reshape(-1), target_pot.reshape(-1), mapped


def solution(mesh):
    return jax.shard_map(
        shards,
        mesh=mesh,
        in_specs=(P(None, "src"), P(None, "tgt"), P("src"), P("tgt"), P("src"), P("tgt"), P("src", None)),
        out_specs=(P("src"), P("tgt"), P(None, ("src", "tgt"))),
        check_vma=False,
    )
```

```python
import functools
import math

import jax
import jax.numpy as jnp
from jax import lax
from jax.experimental import pallas as pl
from jax.experimental.pallas import tpu as pltpu
from jax.sharding import PartitionSpec as P

ITERS = 2
MESH = pl.DeviceIdType.MESH
EMPTY = -1e30
TILE = 256
SUB = 8
AUX = 16
MAPROWS = 40
MIB = 1 << 20


def split3(row):
    high = row.astype(jnp.bfloat16).astype(jnp.float32)
    rest = row - high
    mid = rest.astype(jnp.bfloat16).astype(jnp.float32)
    low = rest - mid
    return high, mid, low


def cluster_row(ref, cluster):
    first = ref[pl.ds(2 * cluster, 1), :]
    second = ref[pl.ds(2 * cluster + 1, 1), :]
    return jnp.concatenate([first, second], axis=1)


def aux_rows(row, offset, other):
    at = lax.broadcasted_iota(jnp.int32, (AUX, TILE), 0)
    high, mid, low = split3(row)
    out = jnp.where((at >= other) & (at < other + 3), 1.0, 0.0)
    out = jnp.where(at == offset, high, out)
    out = jnp.where(at == offset + 1, mid, out)
    out = jnp.where(at == offset + 2, low, out)
    return out.astype(jnp.bfloat16)


def cells_of(ref, cluster):
    return ref[:, pl.ds(pl.multiple_of(cluster * TILE, TILE), TILE)]


def sweep_kernel(kind, step, sub_ids, lane_ids, count, sub_cells, lane_cells, sub_pot, lane_pot, out, *scratch):
    clusters = lane_cells.shape[1] // TILE
    if kind == "max":
        top, total = scratch
        top[...] = jnp.full(top.shape, EMPTY, jnp.float32)
        total[...] = jnp.zeros(total.shape, jnp.float32)
    elif kind == "sum":
        (total,) = scratch
        total[...] = jnp.zeros(total.shape, jnp.float32)
    else:
        out[...] = jnp.zeros(out.shape, jnp.float32)

    def tile(p):
        a, b = sub_ids[p], lane_ids[p]
        sub = cells_of(sub_cells, a)
        lane = cells_of(lane_cells, b)
        sub_aux = aux_rows(cluster_row(sub_pot, a), 0, 3)
        lane_aux = aux_rows(cluster_row(lane_pot, b), 3, 0)
        left = jnp.concatenate([sub, sub_aux], axis=0)
        right = jnp.concatenate([lane * jnp.bfloat16(4.0), lane_aux], axis=0)
        score = lax.dot_general(left, right, (((0,), (0,)), ((), ())), preferred_element_type=jnp.float32)
        if kind == "max":
            score = score.reshape(TILE // SUB, SUB, TILE)
            old = top[b]
            new = jnp.maximum(old, jnp.max(score, axis=0))
            part = jnp.sum(jnp.exp(score - new[None]), axis=0)
            total[b] = total[b] * jnp.exp(old - new) + part
            top[b] = new
        elif kind == "sum":
            weight = jnp.exp(score).reshape(TILE // SUB, SUB, TILE)
            total[b] = total[b] + jnp.sum(weight, axis=0)
        else:
            weight = jnp.exp(score)
            high = weight.astype(jnp.bfloat16)
            low = (weight - high.astype(jnp.float32)).astype(jnp.bfloat16)
            ones = jnp.where(lax.broadcasted_iota(jnp.int32, (AUX, TILE), 0) == 0, 1.0, 0.0).astype(jnp.bfloat16)
            cells = jnp.concatenate([sub, ones], axis=0)
            moved = jnp.dot(cells, high, preferred_element_type=jnp.float32)
            moved = moved + jnp.dot(cells, low, preferred_element_type=jnp.float32)
            out[b] = out[b] + moved[:MAPROWS]

    def group(g):
        for r in range(step):
            tile(g * step + r)

    pl.loop(0, count[0] // step)(group)

    if kind == "map":
        return

    per = out.shape[1] // 2

    def finish(c):
        shard, at = c // per, c % per
        if kind == "max":
            best = jnp.max(top[c], axis=0, keepdims=True)
            row = jnp.sum(total[c] * jnp.exp(top[c] - best), axis=0, keepdims=True)
            value = best + jnp.log(jnp.where(row > 0.0, row, 1.0))
        else:
            value = jnp.sum(total[c], axis=0, keepdims=True)
        out[shard, pl.ds(2 * at, 1), :] = value[:, :128]
        out[shard, pl.ds(2 * at + 1, 1), :] = value[:, 128:]

    def finish_group(g):
        for r in range(8):
            finish(g * 8 + r)

    pl.loop(0, clusters // 8)(finish_group)


def sweep(kind, shards, sub_ids, lane_ids, count, sub_cells, lane_cells, sub_pot, lane_pot):
    clusters = lane_cells.shape[1] // TILE
    if kind == "map":
        out = jax.ShapeDtypeStruct((clusters, MAPROWS, TILE), jnp.float32)
        scratch = []
    else:
        many = 2 if kind == "max" else 1
        out = jax.ShapeDtypeStruct((shards, 2 * clusters // shards, 128), jnp.float32)
        scratch = [pltpu.VMEM((clusters, SUB, TILE), jnp.float32)] * many
    smem = pl.BlockSpec(memory_space=pltpu.SMEM)
    vmem = pl.BlockSpec(memory_space=pltpu.VMEM)
    return pl.pallas_call(
        functools.partial(sweep_kernel, kind, math.gcd(sub_ids.shape[0] // 2, 16)),
        out_shape=out,
        in_specs=[smem] * 3 + [vmem] * 4,
        out_specs=vmem,
        scratch_shapes=scratch,
        compiler_params=pltpu.CompilerParams(vmem_limit_bytes=48 * MIB),
        name="sweep_" + kind,
    )(sub_ids, lane_ids, count, sub_cells, lane_cells, sub_pot, lane_pot)


def greet(axis, n):
    me = lax.axis_index(axis)
    barrier = pltpu.get_barrier_semaphore()
    for k in range(1, n):
        pl.semaphore_signal(barrier, inc=1, device_id={axis: lax.rem(me + k, n)}, device_id_type=MESH)
    pl.semaphore_wait(barrier, n - 1)
    return me


def reduce_kernel(kind, axis, n, part, old, logmass, out, held, send1, recv1, send2, recv2):
    me = greet(axis, n)
    rows = old.shape[0] // n
    copies = []
    for k in range(1, n):
        peer = lax.rem(me + k, n)
        copy = pltpu.make_async_remote_copy(
            src_ref=part.at[peer], dst_ref=held.at[k], send_sem=send1.at[k], recv_sem=recv1.at[k],
            device_id={axis: peer}, device_id_type=MESH)
        copy.start()
        copies.append(copy)
    for copy in copies:
        copy.wait()
    mine = pl.ds(pl.multiple_of(me * rows, rows), rows)
    if kind == "max":
        best = part[me]
        for k in range(1, n):
            best = jnp.maximum(best, held[k])
        total = jnp.exp(part[me] - best)
        for k in range(1, n):
            total = total + jnp.exp(held[k] - best)
        lse = best + jnp.log(total)
    else:
        total = part[me]
        for k in range(1, n):
            total = total + held[k]
        lse = jnp.log(jnp.where(total > 0.0, total, 1.0))
    mass = logmass[mine, :]
    out[mine, :] = jnp.where(mass > 0.5 * EMPTY, old[mine, :] + mass - lse, EMPTY)
    copies = []
    for k in range(1, n):
        peer = lax.rem(me + k, n)
        copy = pltpu.make_async_remote_copy(
            src_ref=out.at[mine], dst_ref=out.at[mine], send_sem=send2.at[k], recv_sem=recv2.at[k],
            device_id={axis: peer}, device_id_type=MESH)
        copy.start()
        copies.append(copy)
    for copy in copies:
        copy.wait()


def reduce(kind, axis, ident, part, old, logmass):
    n = part.shape[0]
    vmem = pl.BlockSpec(memory_space=pltpu.VMEM)
    return pl.pallas_call(
        functools.partial(reduce_kernel, kind, axis, n),
        out_shape=jax.ShapeDtypeStruct(old.shape, jnp.float32),
        in_specs=[vmem] * 3,
        out_specs=vmem,
        scratch_shapes=[pltpu.VMEM(part.shape, jnp.float32)] + [pltpu.SemaphoreType.DMA((n,))] * 4,
        compiler_params=pltpu.CompilerParams(collective_id=ident, has_side_effects=True, vmem_limit_bytes=32 * MIB),
        name="reduce_" + kind + "_" + axis,
    )(part, old, logmass)


def scatter_kernel(axis, n, moved, out, held, send, recv, own):
    me = greet(axis, n)
    per = moved.shape[0] // n
    copies = []
    for k in range(1, n):
        peer = lax.rem(me + k, n)
        copy = pltpu.make_async_remote_copy(
            src_ref=moved.at[pl.ds(peer * per, per)], dst_ref=held.at[k], send_sem=send.at[k], recv_sem=recv.at[k],
            device_id={axis: peer}, device_id_type=MESH)
        copy.start()
        copies.append(copy)
    local = pltpu.make_async_copy(moved.at[pl.ds(me * per, per)], held.at[0], own)
    local.start()
    local.wait()
    for copy in copies:
        copy.wait()

    features = out.shape[0]

    def one(c):
        total = held[0, c]
        for k in range(1, n):
            total = total + held[k, c]
        weight = total[features:features + 1]
        weight = jnp.where(weight > 0.0, weight, 1.0)
        out[:, pl.ds(pl.multiple_of(c * TILE, TILE), TILE)] = total[:features] / weight

    pl.loop(0, per)(one)


def scatter(axis, ident, n, features, moved):
    clusters = moved.shape[0]
    per = clusters // n
    return pl.pallas_call(
        functools.partial(scatter_kernel, axis, n),
        out_shape=jax.ShapeDtypeStruct((features, per * TILE), jnp.float32),
        in_specs=[pl.BlockSpec(memory_space=pl.ANY)],
        out_specs=pl.BlockSpec(memory_space=pltpu.VMEM),
        scratch_shapes=[
            pltpu.VMEM((n, per) + moved.shape[1:], jnp.float32),
            pltpu.SemaphoreType.DMA((n,)),
            pltpu.SemaphoreType.DMA((n,)),
            pltpu.SemaphoreType.DMA,
        ],
        compiler_params=pltpu.CompilerParams(collective_id=ident, has_side_effects=True, vmem_limit_bytes=48 * MIB),
        name="scatter",
    )(moved)


def pair_table(pair_lists, tgt_block, per_block, capacity):
    width = pair_lists.shape[1]
    flat = pair_lists.reshape(-1)
    chosen = flat // per_block == tgt_block
    rank = jnp.cumsum(chosen.astype(jnp.int32)) - 1
    slots = jnp.arange(capacity, dtype=jnp.int32)
    matches = (rank[None, :] == slots[:, None]) & chosen[None, :]
    sources = jnp.arange(flat.shape[0], dtype=jnp.int32) // width
    pair_src = jnp.sum(jnp.where(matches, sources[None, :], 0), axis=1)
    pair_tgt = jnp.sum(jnp.where(matches, (flat % per_block)[None, :], 0), axis=1)
    return pair_src, pair_tgt, jnp.sum(chosen.astype(jnp.int32)).reshape(1)


def side(cells, mass, count):
    clusters = count.shape[0]
    wide = cells.astype(jnp.float32)
    norm = jnp.sum(wide * wide, axis=0).reshape(2 * clusters, 128)
    place = jnp.arange(2, dtype=jnp.int32)[None, :, None] * 128 + jnp.arange(128, dtype=jnp.int32)[None, None, :]
    live = (place < count[:, None, None]).reshape(2 * clusters, 128)
    logmass = jnp.where(live, jnp.log(mass).reshape(2 * clusters, 128), EMPTY)
    return norm, live, logmass


def shards(source_cells, target_cells, source_mass, target_mass, source_count, target_count, pair_lists):
    features = source_cells.shape[0]
    n_src, n_tgt = lax.axis_size("src"), lax.axis_size("tgt")
    capacity = 2 * pair_lists.size // n_tgt
    own_src, own_tgt, own = pair_table(pair_lists, lax.axis_index("tgt"), target_count.shape[0], capacity)
    src_norm, src_live, src_logmass = side(source_cells, source_mass, source_count)
    tgt_norm, tgt_live, tgt_logmass = side(target_cells, target_mass, target_count)
    u = -2.0 * src_norm
    v = jnp.where(tgt_live, -2.0 * tgt_norm, EMPTY)
    for step in range(ITERS):
        kind = "max" if step == 0 else "sum"
        part = sweep(kind, n_tgt, own_tgt, own_src, own, target_cells, source_cells, v, u)
        u = reduce(kind, "tgt", 2 * step, part, u, src_logmass)
        part = sweep(kind, n_src, own_src, own_tgt, own, source_cells, target_cells, u, v)
        v = reduce(kind, "src", 2 * step + 1, part, v, tgt_logmass)
    moved = sweep("map", n_tgt, own_tgt, own_src, own, target_cells, source_cells, v, u)
    mapped = scatter("tgt", 2 * ITERS, n_tgt, features, moved)
    source_pot = jnp.where(src_live, 0.5 * u + src_norm, 0.0)
    target_pot = jnp.where(tgt_live, 0.5 * v + tgt_norm, 0.0)
    return source_pot.reshape(-1), target_pot.reshape(-1), mapped


def solution(mesh):
    return jax.shard_map(
        shards,
        mesh=mesh,
        in_specs=(P(None, "src"), P(None, "tgt"), P("src"), P("tgt"), P("src"), P("tgt"), P("src", None)),
        out_specs=(P("src"), P("tgt"), P(None, ("src", "tgt"))),
        check_vma=False,
    )
```

```python
import functools
import math

import jax
import jax.numpy as jnp
from jax import lax
from jax.experimental import pallas as pl
from jax.experimental.pallas import tpu as pltpu
from jax.sharding import PartitionSpec as P

ITERS = 2
MESH = pl.DeviceIdType.MESH
EMPTY = -1e30
TILE = 256
SUB = 8
AUX = 16
MIB = 1 << 20


def split3(row):
    high = row.astype(jnp.bfloat16).astype(jnp.float32)
    rest = row - high
    mid = rest.astype(jnp.bfloat16).astype(jnp.float32)
    low = rest - mid
    return high, mid, low


def cluster_row(ref, cluster):
    first = ref[pl.ds(2 * cluster, 1), :]
    second = ref[pl.ds(2 * cluster + 1, 1), :]
    return jnp.concatenate([first, second], axis=1)


def aux_rows(row, offset, other):
    at = lax.broadcasted_iota(jnp.int32, (AUX, TILE), 0)
    high, mid, low = split3(row)
    out = jnp.where((at >= other) & (at < other + 3), 1.0, 0.0)
    out = jnp.where(at == offset, high, out)
    out = jnp.where(at == offset + 1, mid, out)
    out = jnp.where(at == offset + 2, low, out)
    return out.astype(jnp.bfloat16)


def cells_of(ref, cluster):
    return ref[:, pl.ds(pl.multiple_of(cluster * TILE, TILE), TILE)]


def sweep_kernel(kind, step, sub_ids, lane_ids, count, sub_cells, lane_cells, sub_pot, lane_pot, out, *scratch):
    clusters = lane_cells.shape[1] // TILE
    if kind == "max":
        top, total = scratch
        top[...] = jnp.full(top.shape, EMPTY, jnp.float32)
        total[...] = jnp.zeros(total.shape, jnp.float32)
    elif kind == "sum":
        (total,) = scratch
        total[...] = jnp.zeros(total.shape, jnp.float32)
    else:
        (den,) = scratch
        features, per = out.shape[1], den.shape[1]
        out[...] = jnp.zeros(out.shape, jnp.float32)
        den[...] = jnp.zeros(den.shape, jnp.float32)

    def tile(p):
        a, b = sub_ids[p], lane_ids[p]
        sub = cells_of(sub_cells, a)
        lane = cells_of(lane_cells, b)
        sub_aux = aux_rows(cluster_row(sub_pot, a), 0, 3)
        lane_aux = aux_rows(cluster_row(lane_pot, b), 3, 0)
        left = jnp.concatenate([sub, sub_aux], axis=0)
        right = jnp.concatenate([lane * jnp.bfloat16(4.0), lane_aux], axis=0)
        score = lax.dot_general(left, right, (((0,), (0,)), ((), ())), preferred_element_type=jnp.float32)
        if kind == "max":
            score = score.reshape(TILE // SUB, SUB, TILE)
            old = top[b]
            new = jnp.maximum(old, jnp.max(score, axis=0))
            part = jnp.sum(jnp.exp(score - new[None]), axis=0)
            total[b] = total[b] * jnp.exp(old - new) + part
            top[b] = new
        elif kind == "sum":
            weight = jnp.exp(score).reshape(TILE // SUB, SUB, TILE)
            total[b] = total[b] + jnp.sum(weight, axis=0)
        else:
            weight = jnp.exp(score)
            high = weight.astype(jnp.bfloat16)
            low = (weight - high.astype(jnp.float32)).astype(jnp.bfloat16)
            ones = jnp.where(lax.broadcasted_iota(jnp.int32, (AUX, TILE), 0) == 0, 1.0, 0.0).astype(jnp.bfloat16)
            cells = jnp.concatenate([sub, ones], axis=0)
            moved = jnp.dot(cells, high, preferred_element_type=jnp.float32)
            moved = moved + jnp.dot(cells, low, preferred_element_type=jnp.float32)
            out[b] = out[b] + moved[:features]
            place = (b // per, pl.ds(b % per, 1))
            den[place] = den[place] + moved[features:features + 1]

    def group(g):
        for r in range(step):
            tile(g * step + r)

    pl.loop(0, count[0] // step)(group)

    if kind == "map":
        return

    per = out.shape[1] // 2

    def finish(c):
        shard, at = c // per, c % per
        if kind == "max":
            best = jnp.max(top[c], axis=0, keepdims=True)
            row = jnp.sum(total[c] * jnp.exp(top[c] - best), axis=0, keepdims=True)
            value = best + jnp.log(jnp.where(row > 0.0, row, 1.0))
        else:
            value = jnp.sum(total[c], axis=0, keepdims=True)
        out[shard, pl.ds(2 * at, 1), :] = value[:, :128]
        out[shard, pl.ds(2 * at + 1, 1), :] = value[:, 128:]

    def finish_group(g):
        for r in range(8):
            finish(g * 8 + r)

    pl.loop(0, clusters // 8)(finish_group)


def sweep(kind, shards, sub_ids, lane_ids, count, sub_cells, lane_cells, sub_pot, lane_pot):
    clusters = lane_cells.shape[1] // TILE
    if kind == "map":
        out = (
            jax.ShapeDtypeStruct((clusters, lane_cells.shape[0], TILE), jnp.float32),
            jax.ShapeDtypeStruct((shards, clusters // shards, TILE), jnp.float32),
        )
        scratch = []
    else:
        many = 2 if kind == "max" else 1
        out = jax.ShapeDtypeStruct((shards, 2 * clusters // shards, 128), jnp.float32)
        scratch = [pltpu.VMEM((clusters, SUB, TILE), jnp.float32)] * many
    smem = pl.BlockSpec(memory_space=pltpu.SMEM)
    vmem = pl.BlockSpec(memory_space=pltpu.VMEM)
    return pl.pallas_call(
        functools.partial(sweep_kernel, kind, math.gcd(sub_ids.shape[0] // 2, 16)),
        out_shape=out,
        in_specs=[smem] * 3 + [vmem] * 4,
        out_specs=(vmem, vmem) if kind == "map" else vmem,
        scratch_shapes=scratch,
        compiler_params=pltpu.CompilerParams(vmem_limit_bytes=48 * MIB),
        name="sweep_" + kind,
    )(sub_ids, lane_ids, count, sub_cells, lane_cells, sub_pot, lane_pot)


def greet(axis, n):
    me = lax.axis_index(axis)
    barrier = pltpu.get_barrier_semaphore()
    for k in range(1, n):
        pl.semaphore_signal(barrier, inc=1, device_id={axis: lax.rem(me + k, n)}, device_id_type=MESH)
    pl.semaphore_wait(barrier, n - 1)
    return me


def reduce_kernel(kind, axis, n, part, old, logmass, out, held, send1, recv1, send2, recv2):
    me = greet(axis, n)
    rows = old.shape[0] // n
    copies = []
    for k in range(1, n):
        peer = lax.rem(me + k, n)
        copy = pltpu.make_async_remote_copy(
            src_ref=part.at[peer], dst_ref=held.at[k], send_sem=send1.at[k], recv_sem=recv1.at[k],
            device_id={axis: peer}, device_id_type=MESH)
        copy.start()
        copies.append(copy)
    for copy in copies:
        copy.wait()
    mine = pl.ds(pl.multiple_of(me * rows, rows), rows)
    if kind == "max":
        best = part[me]
        for k in range(1, n):
            best = jnp.maximum(best, held[k])
        total = jnp.exp(part[me] - best)
        for k in range(1, n):
            total = total + jnp.exp(held[k] - best)
        lse = best + jnp.log(total)
    else:
        total = part[me]
        for k in range(1, n):
            total = total + held[k]
        lse = jnp.log(jnp.where(total > 0.0, total, 1.0))
    mass = logmass[mine, :]
    out[mine, :] = jnp.where(mass > 0.5 * EMPTY, old[mine, :] + mass - lse, EMPTY)
    copies = []
    for k in range(1, n):
        peer = lax.rem(me + k, n)
        copy = pltpu.make_async_remote_copy(
            src_ref=out.at[mine], dst_ref=out.at[mine], send_sem=send2.at[k], recv_sem=recv2.at[k],
            device_id={axis: peer}, device_id_type=MESH)
        copy.start()
        copies.append(copy)
    for copy in copies:
        copy.wait()


def reduce(kind, axis, ident, part, old, logmass):
    n = part.shape[0]
    vmem = pl.BlockSpec(memory_space=pltpu.VMEM)
    return pl.pallas_call(
        functools.partial(reduce_kernel, kind, axis, n),
        out_shape=jax.ShapeDtypeStruct(old.shape, jnp.float32),
        in_specs=[vmem] * 3,
        out_specs=vmem,
        scratch_shapes=[pltpu.VMEM(part.shape, jnp.float32)] + [pltpu.SemaphoreType.DMA((n,))] * 4,
        compiler_params=pltpu.CompilerParams(collective_id=ident, has_side_effects=True, vmem_limit_bytes=32 * MIB),
        name="reduce_" + kind + "_" + axis,
    )(part, old, logmass)


def scatter_kernel(axis, n, ny, num, den, out, first_y, ring_a, ring_b, last_y, held, *sems):
    nz = n // ny
    me = greet(axis, n)
    z, y = me // ny, lax.rem(me, ny)
    per, features = num.shape[2], num.shape[3]
    half = per // 4
    other = ny - 1 - y

    def device(at):
        return lax.rem(at + nz, nz) * ny + y

    def copy(src, dst, sem, k, peer):
        made = pltpu.make_async_remote_copy(
            src_ref=src, dst_ref=dst, send_sem=sems[2 * sem].at[k], recv_sem=sems[2 * sem + 1].at[k],
            device_id={axis: peer}, device_id_type=MESH)
        made.start()
        return made

    partner = z * ny + other
    sign = (1, -1)

    def block(d, step):
        return lax.rem(z - sign[d] * (1 + step) + 2 * nz, nz)

    def group(d, base):
        return pl.ds(base + d * half, half)

    over_y = [[None] * nz for _ in sign]
    over_a = [[None] * nz for _ in sign]
    over_b = [[None] * nz for _ in sign]
    for d in range(2):
        at = block(d, 0)
        over_a[d][0] = copy(num.at[at, :, group(d, 0)], ring_a.at[d, 0], 1, d * nz, device(z + sign[d]))
    for step in range(nz):
        for d in range(2):
            at = block(d, step)
            over_y[d][step] = copy(num.at[at, other, group(d, 2 * half)], first_y.at[d, step], 0, d * nz + step, partner)
    others = []
    for k in range(1, n):
        peer = lax.rem(me + k, n)
        others.append(copy(den.at[peer], held.at[k], 4, k, peer))
    for step in range(nz):
        at = [block(d, step) for d in range(2)]
        for d in range(2):
            over_y[d][step].wait_recv()
            first_y[d, step] += num[at[d], y, group(d, 2 * half)]
            if step > 0:
                over_b[d][step - 1].wait_recv()
                first_y[d, step] += ring_b[d, step - 1]
            if step < nz - 1:
                over_b[d][step] = copy(first_y.at[d, step], ring_b.at[d, step], 2, d * nz + step, device(z + sign[d]))
            if step > 0:
                over_a[d][step - 1].wait_recv()
                ring_a[d, step - 1] += num[at[d], :, group(d, 0)]
            if 0 < step < nz - 1:
                over_a[d][step] = copy(ring_a.at[d, step - 1], ring_a.at[d, step], 1, d * nz + step, device(z + sign[d]))
    over_last = [copy(ring_a.at[d, nz - 2, other], last_y.at[d], 3, d, partner) for d in range(2)]
    for made in others:
        made.wait_recv()
    total = den[me]
    for k in range(1, n):
        total = total + held[k]
    total = jnp.where(total > 0.0, total, 1.0)

    def put(c, value):
        out[:, c * TILE:(c + 1) * TILE] = value / total[c:c + 1]

    for d in range(2):
        for c in range(half):
            put(2 * half + d * half + c, first_y[d, nz - 1, c])
    for d in range(2):
        over_last[d].wait_recv()
        for c in range(half):
            put(d * half + c, ring_a[d, nz - 2, y, c] + last_y[d, c])
    for made in others + over_last:
        made.wait_send()
    for d in range(2):
        for step in range(nz):
            over_y[d][step].wait_send()
        for step in range(nz - 1):
            over_a[d][step].wait_send()
            over_b[d][step].wait_send()


def scatter(axis, ident, n, ny, num, den):
    clusters, features, width = num.shape
    per, nz = clusters // n, n // ny
    quarter = per // 4
    vmem = pl.BlockSpec(memory_space=pltpu.VMEM)
    sems = []
    for many in (2 * nz, 2 * nz, 2 * nz, 2, n):
        sems += [pltpu.SemaphoreType.DMA((many,))] * 2
    return pl.pallas_call(
        functools.partial(scatter_kernel, axis, n, ny),
        out_shape=jax.ShapeDtypeStruct((features, per * width), jnp.float32),
        in_specs=[vmem, vmem],
        out_specs=vmem,
        scratch_shapes=[
            pltpu.VMEM((2, nz, quarter, features, width), jnp.float32),
            pltpu.VMEM((2, nz - 1, ny, quarter, features, width), jnp.float32),
            pltpu.VMEM((2, nz - 1, quarter, features, width), jnp.float32),
            pltpu.VMEM((2, quarter, features, width), jnp.float32),
            pltpu.VMEM((n, per, width), jnp.float32),
        ] + sems,
        compiler_params=pltpu.CompilerParams(collective_id=ident, has_side_effects=True, vmem_limit_bytes=32 * MIB),
        name="scatter",
    )(num.reshape(nz, ny, per, features, width), den)


def pair_table(pair_lists, tgt_block, per_block, capacity):
    width = pair_lists.shape[1]
    flat = pair_lists.reshape(-1)
    chosen = flat // per_block == tgt_block
    rank = jnp.cumsum(chosen.astype(jnp.int32)) - 1
    slots = jnp.arange(capacity, dtype=jnp.int32)
    matches = (rank[None, :] == slots[:, None]) & chosen[None, :]
    sources = jnp.arange(flat.shape[0], dtype=jnp.int32) // width
    pair_src = jnp.sum(jnp.where(matches, sources[None, :], 0), axis=1)
    pair_tgt = jnp.sum(jnp.where(matches, (flat % per_block)[None, :], 0), axis=1)
    return pair_src, pair_tgt, jnp.sum(chosen.astype(jnp.int32)).reshape(1)


def side(cells, mass, count):
    clusters = count.shape[0]
    wide = cells.astype(jnp.float32)
    norm = jnp.sum(wide * wide, axis=0).reshape(2 * clusters, 128)
    place = jnp.arange(2, dtype=jnp.int32)[None, :, None] * 128 + jnp.arange(128, dtype=jnp.int32)[None, None, :]
    live = (place < count[:, None, None]).reshape(2 * clusters, 128)
    logmass = jnp.where(live, jnp.log(mass).reshape(2 * clusters, 128), EMPTY)
    return norm, live, logmass


def shards(source_cells, target_cells, source_mass, target_mass, source_count, target_count, pair_lists):
    n_src, n_tgt = lax.axis_size("src"), lax.axis_size("tgt")
    capacity = 2 * pair_lists.size // n_tgt
    own_src, own_tgt, own = pair_table(pair_lists, lax.axis_index("tgt"), target_count.shape[0], capacity)
    src_norm, src_live, src_logmass = side(source_cells, source_mass, source_count)
    tgt_norm, tgt_live, tgt_logmass = side(target_cells, target_mass, target_count)
    u = -2.0 * src_norm
    v = jnp.where(tgt_live, -2.0 * tgt_norm, EMPTY)
    for step in range(ITERS):
        kind = "max" if step == 0 else "sum"
        part = sweep(kind, n_tgt, own_tgt, own_src, own, target_cells, source_cells, v, u)
        u = reduce(kind, "tgt", 2 * step, part, u, src_logmass)
        part = sweep(kind, n_src, own_src, own_tgt, own, source_cells, target_cells, u, v)
        v = reduce(kind, "src", 2 * step + 1, part, v, tgt_logmass)
    num, den = sweep("map", n_tgt, own_tgt, own_src, own, target_cells, source_cells, v, u)
    mapped = scatter("tgt", 2 * ITERS, n_tgt, 2, num, den)
    source_pot = jnp.where(src_live, 0.5 * u + src_norm, 0.0)
    target_pot = jnp.where(tgt_live, 0.5 * v + tgt_norm, 0.0)
    return source_pot.reshape(-1), target_pot.reshape(-1), mapped


def solution(mesh):
    return jax.shard_map(
        shards,
        mesh=mesh,
        in_specs=(P(None, "src"), P(None, "tgt"), P("src"), P("tgt"), P("src"), P("tgt"), P("src", None)),
        out_specs=(P("src"), P("tgt"), P(None, ("src", "tgt"))),
        check_vma=False,
    )
```

```python
import functools
import math

import jax
import jax.numpy as jnp
from jax import lax
from jax.experimental import pallas as pl
from jax.experimental.pallas import tpu as pltpu
from jax.sharding import PartitionSpec as P

MESH = pl.DeviceIdType.MESH
EMPTY = -1e30
TILE = 256
SUB = 8
AUX = 16
NY = 2
MIB = 1 << 20
ROW_SUB, ROW_LANE, ROW_KEEP, ROW_LAST, COL_SUB, COL_LANE, COL_KEEP, COL_LAST = range(8)


def split3(row):
    high = row.astype(jnp.bfloat16).astype(jnp.float32)
    rest = row - high
    mid = rest.astype(jnp.bfloat16).astype(jnp.float32)
    low = rest - mid
    return high, mid, low


def cluster_row(ref, cluster):
    first = ref[pl.ds(2 * cluster, 1), :]
    second = ref[pl.ds(2 * cluster + 1, 1), :]
    return jnp.concatenate([first, second], axis=1)


def aux_rows(row, offset, other):
    at = lax.broadcasted_iota(jnp.int32, (AUX, TILE), 0)
    high, mid, low = split3(row)
    out = jnp.where((at >= other) & (at < other + 3), 1.0, 0.0)
    out = jnp.where(at == offset, high, out)
    out = jnp.where(at == offset + 1, mid, out)
    out = jnp.where(at == offset + 2, low, out)
    return out.astype(jnp.bfloat16)


def kernel(
    sizes, table, x_cells, y_cells, u0, v0, x_mass, y_mass, u_out, v_out, out,
    xs, ys, u1, v1, parts, helds, slot_m, slot_s, slot_n, slot_d, send_a, send_y, den, held_d,
    first_y, ring_a, ring_b, last_y, *sems,
):
    n_src, n_tgt, slots = sizes
    step = math.gcd(slots, 16)
    features = x_cells.shape[0]
    me_src, me_tgt = lax.axis_index("src"), lax.axis_index("tgt")
    barrier = pltpu.get_barrier_semaphore()
    for axis, me, n in (("tgt", me_tgt, n_tgt), ("src", me_src, n_src)):
        for k in range(1, n):
            pl.semaphore_signal(barrier, inc=1, device_id={axis: lax.rem(me + k, n)}, device_id_type=MESH)

    slot_m[slots] = jnp.full((SUB, TILE), EMPTY, jnp.float32)
    slot_s[slots] = jnp.zeros((SUB, TILE), jnp.float32)
    slot_n[slots] = jnp.zeros((features, TILE), jnp.float32)
    slot_d[pl.ds(slots, SUB), :] = jnp.zeros((SUB, TILE), jnp.float32)

    def entry(which, p):
        return table[which * slots + p]

    def sweep(kind, first, sub_cells, lane_cells, sub_pot, lane_pot):
        def tile(p, carry):
            a, b, keep = entry(first, p), entry(first + 1, p), entry(first + 2, p)
            sub, lane = sub_cells[a], lane_cells[b]
            left = jnp.concatenate([sub, aux_rows(cluster_row(sub_pot, a), 0, 3)], axis=0)
            right = jnp.concatenate([lane, aux_rows(cluster_row(lane_pot, b), 3, 0)], axis=0)
            score = lax.dot_general(left, right, (((0,), (0,)), ((), ())), preferred_element_type=jnp.float32)
            hold = keep.astype(jnp.float32)
            if kind == "max":
                score = score.reshape(TILE // SUB, SUB, TILE)
                best = jnp.max(score, axis=0)
                part = jnp.sum(jnp.exp(score - best[None]), axis=0)
                old = carry[0] * hold + (1.0 - hold) * EMPTY
                new = jnp.maximum(old, best)
                total = carry[1] * hold * jnp.exp(old - new) + part * jnp.exp(best - new)
                slot_m[p] = new
                slot_s[p] = total
                return new, total
            weight = jnp.exp(score)
            if kind == "sum":
                total = carry[0] * hold + jnp.sum(weight.reshape(TILE // SUB, SUB, TILE), axis=0)
                slot_s[p] = total
                return (total,)
            high = weight.astype(jnp.bfloat16)
            low = (weight - high.astype(jnp.float32)).astype(jnp.bfloat16)
            ones = jnp.where(lax.broadcasted_iota(jnp.int32, (AUX, TILE), 0) == 0, 1.0, 0.0).astype(jnp.bfloat16)
            cells = jnp.concatenate([sub, ones], axis=0)
            moved = jnp.dot(cells, high, preferred_element_type=jnp.float32)
            moved = moved + jnp.dot(cells, low, preferred_element_type=jnp.float32)
            total = carry[0] * hold + moved[:features]
            weights = carry[1] * hold + moved[features:features + 1]
            slot_n[p] = total
            slot_d[pl.ds(p, 1), :] = weights
            return total, weights

        def group(g, carry):
            for r in range(step):
                carry = tile(g * step + r, carry)
            return carry

        empty = jnp.zeros((SUB, TILE), jnp.float32)
        if kind == "max":
            start = (empty + EMPTY, empty)
        elif kind == "sum":
            start = (empty,)
        else:
            start = (jnp.zeros((features, TILE), jnp.float32), jnp.zeros((1, TILE), jnp.float32))
        lax.fori_loop(0, slots // step, group, start)

    def reduce(kind, which, axis, me, n, last, old, mass, new):
        part, held = parts.at[which], helds.at[which]
        rows = old.shape[0] // n
        per = rows // 2

        def finish(c):
            at = entry(last, c)
            if kind == "max":
                best = jnp.max(slot_m[at], axis=0, keepdims=True)
                row = jnp.sum(slot_s[at] * jnp.exp(slot_m[at] - best), axis=0, keepdims=True)
                value = best + jnp.log(jnp.where(row > 0.0, row, 1.0))
            else:
                value = jnp.sum(slot_s[at], axis=0, keepdims=True)
            part[pl.ds(2 * c, 1), :] = value[:, :128]
            part[pl.ds(2 * c + 1, 1), :] = value[:, 128:]

        def finish_group(g):
            for r in range(per):
                finish(g * per + r)

        pl.loop(0, n)(finish_group)
        if which == 0:
            pl.semaphore_wait(barrier, n_src + n_tgt - 2)
        mine = pl.ds(pl.multiple_of(me * rows, rows), rows)

        def share(src_ref, dst_ref, phase):
            made = []
            for k in range(1, n):
                peer = lax.rem(me + k, n)
                copy = pltpu.make_async_remote_copy(
                    src_ref=src_ref(peer), dst_ref=dst_ref(k),
                    send_sem=sems[2 * phase].at[which, k], recv_sem=sems[2 * phase + 1].at[which, k],
                    device_id={axis: peer}, device_id_type=MESH)
                copy.start()
                made.append(copy)
            return made

        made = share(lambda peer: part.at[pl.ds(pl.multiple_of(peer * rows, rows), rows)],
                     lambda k: held.at[pl.ds(k * rows, rows)], 0)
        for copy in made:
            copy.wait_recv()
        own = part[mine, :]
        if kind == "max":
            best = own
            for k in range(1, n):
                best = jnp.maximum(best, held[k * rows:(k + 1) * rows])
            total = jnp.exp(own - best)
            for k in range(1, n):
                total = total + jnp.exp(held[k * rows:(k + 1) * rows] - best)
            lse = best + jnp.log(total)
        else:
            total = own
            for k in range(1, n):
                total = total + held[k * rows:(k + 1) * rows]
            lse = jnp.log(jnp.where(total > 0.0, total, 1.0))
        logmass = mass[mine, :]
        new[mine, :] = jnp.where(logmass > 0.5 * EMPTY, old[mine, :] + logmass - lse, EMPTY)
        sent = share(lambda peer: new.at[mine], lambda k: new.at[mine], 1)
        for copy in made:
            copy.wait_send()
        for copy in sent:
            copy.wait()

    def arrange(c):
        lanes = pl.ds(pl.multiple_of(c * TILE, TILE), TILE)
        xs[c] = x_cells[:, lanes] * jnp.bfloat16(4.0)
        ys[c] = y_cells[:, lanes]

    pl.loop(0, x_cells.shape[1] // TILE)(arrange)
    sweep("max", ROW_SUB, ys, xs, v0, u0)
    reduce("max", 0, "tgt", me_tgt, n_tgt, ROW_LAST, u0, x_mass, u1)
    sweep("max", COL_SUB, xs, ys, u1, v0)
    reduce("max", 1, "src", me_src, n_src, COL_LAST, v0, y_mass, v1)
    sweep("sum", ROW_SUB, ys, xs, v1, u1)
    reduce("sum", 2, "tgt", me_tgt, n_tgt, ROW_LAST, u1, x_mass, u_out)
    sweep("sum", COL_SUB, xs, ys, u_out, v1)
    reduce("sum", 3, "src", me_src, n_src, COL_LAST, v1, y_mass, v_out)
    sweep("map", ROW_SUB, ys, xs, v_out, u_out)

    n, nz = n_tgt, n_tgt // NY
    z, y = me_tgt // NY, lax.rem(me_tgt, NY)
    other = NY - 1 - y
    per = out.shape[1] // TILE
    half = per // 4
    sign = (1, -1)

    def device(at):
        return lax.rem(at + nz, nz) * NY + y

    def block(d, hop):
        return lax.rem(z - sign[d] * (1 + hop) + 2 * nz, nz)

    def own(at, side, base, c):
        return slot_n[entry(ROW_LAST, (at * NY + side) * per + base + c)]

    def copy(src, dst, sem, k, peer):
        made = pltpu.make_async_remote_copy(
            src_ref=src, dst_ref=dst, send_sem=sems[2 * sem].at[k], recv_sem=sems[2 * sem + 1].at[k],
            device_id={"tgt": peer}, device_id_type=MESH)
        made.start()
        return made

    partner = z * NY + other
    over_y = [[None] * nz for _ in sign]
    over_a = [[None] * nz for _ in sign]
    over_b = [[None] * nz for _ in sign]
    for d in range(2):
        for side in range(NY):
            for c in range(half):
                send_a[d, side, c] = own(block(d, 0), side, d * half, c)
        over_a[d][0] = copy(send_a.at[d], ring_a.at[d, 0], 3, d * nz, device(z + sign[d]))
    for hop in range(nz):
        for d in range(2):
            for c in range(half):
                send_y[d, hop, c] = own(block(d, hop), other, (2 + d) * half, c)
            over_y[d][hop] = copy(send_y.at[d, hop], first_y.at[d, hop], 2, d * nz + hop, partner)

    def gather(t):
        for c in range(per):
            den[t, pl.ds(c, 1), :] = slot_d[pl.ds(entry(ROW_LAST, t * per + c), 1), :]

    pl.loop(0, n)(gather)
    others = []
    for k in range(1, n):
        peer = lax.rem(me_tgt + k, n)
        others.append(copy(den.at[peer], held_d.at[k], 6, k, peer))
    for hop in range(nz):
        at = [block(d, hop) for d in range(2)]
        for d in range(2):
            over_y[d][hop].wait_recv()
            if hop > 0:
                over_b[d][hop - 1].wait_recv()
            for c in range(half):
                value = first_y[d, hop, c] + own(at[d], y, (2 + d) * half, c)
                if hop > 0:
                    value = value + ring_b[d, hop - 1, c]
                first_y[d, hop, c] = value
            if hop < nz - 1:
                over_b[d][hop] = copy(first_y.at[d, hop], ring_b.at[d, hop], 4, d * nz + hop, device(z + sign[d]))
            if hop > 0:
                over_a[d][hop - 1].wait_recv()
                for side in range(NY):
                    for c in range(half):
                        ring_a[d, hop - 1, side, c] += own(at[d], side, d * half, c)
            if 0 < hop < nz - 1:
                over_a[d][hop] = copy(ring_a.at[d, hop - 1], ring_a.at[d, hop], 3, d * nz + hop, device(z + sign[d]))
    over_last = [copy(ring_a.at[d, nz - 2, other], last_y.at[d], 5, d, partner) for d in range(2)]
    for made in others:
        made.wait_recv()
    total = den[me_tgt]
    for k in range(1, n):
        total = total + held_d[k]
    total = jnp.where(total > 0.0, total, 1.0)

    def put(c, value):
        out[:, c * TILE:(c + 1) * TILE] = value / total[c:c + 1]

    for d in range(2):
        for c in range(half):
            put((2 + d) * half + c, first_y[d, nz - 1, c])
    for d in range(2):
        over_last[d].wait_recv()
        for c in range(half):
            put(d * half + c, ring_a[d, nz - 2, y, c] + last_y[d, c])
    for made in others + over_last:
        made.wait_send()
    for d in range(2):
        for hop in range(nz):
            over_y[d][hop].wait_send()
        for hop in range(nz - 1):
            over_a[d][hop].wait_send()
            over_b[d][hop].wait_send()


def transport(n_src, n_tgt, slots, table, x_cells, y_cells, u0, v0, x_mass, y_mass):
    features = x_cells.shape[0]
    clusters = x_cells.shape[1] // TILE
    per, nz = clusters // n_tgt, n_tgt // NY
    quarter = per // 4
    f32 = jnp.float32
    vmem = pl.BlockSpec(memory_space=pltpu.VMEM)
    dma = pltpu.SemaphoreType.DMA
    most = max(n_src, n_tgt)
    sems = [dma((4, most))] * 4
    for many in (2 * nz, 2 * nz, 2 * nz, 2, n_tgt):
        sems += [dma((many,))] * 2
    scratch = [
        pltpu.VMEM((clusters, features, TILE), jnp.bfloat16),
        pltpu.VMEM((clusters, features, TILE), jnp.bfloat16),
        pltpu.VMEM(u0.shape, f32),
        pltpu.VMEM(v0.shape, f32),
        pltpu.VMEM((4,) + u0.shape, f32),
        pltpu.VMEM((4,) + u0.shape, f32),
        pltpu.VMEM((slots + 1, SUB, TILE), f32),
        pltpu.VMEM((slots + 1, SUB, TILE), f32),
        pltpu.VMEM((slots + 1, features, TILE), f32),
        pltpu.VMEM((slots + SUB, TILE), f32),
        pltpu.VMEM((2, NY, quarter, features, TILE), f32),
        pltpu.VMEM((2, nz, quarter, features, TILE), f32),
        pltpu.VMEM((n_tgt, per, TILE), f32),
        pltpu.VMEM((n_tgt, per, TILE), f32),
        pltpu.VMEM((2, nz, quarter, features, TILE), f32),
        pltpu.VMEM((2, nz - 1, NY, quarter, features, TILE), f32),
        pltpu.VMEM((2, nz - 1, quarter, features, TILE), f32),
        pltpu.VMEM((2, quarter, features, TILE), f32),
    ]
    return pl.pallas_call(
        functools.partial(kernel, (n_src, n_tgt, slots)),
        out_shape=(
            jax.ShapeDtypeStruct(u0.shape, f32),
            jax.ShapeDtypeStruct(v0.shape, f32),
            jax.ShapeDtypeStruct((features, per * TILE), f32),
        ),
        in_specs=[pl.BlockSpec(memory_space=pltpu.SMEM)] + [vmem] * 6,
        out_specs=(vmem, vmem, vmem),
        scratch_shapes=scratch + sems,
        compiler_params=pltpu.CompilerParams(collective_id=0, has_side_effects=True, vmem_limit_bytes=40 * MIB),
        name="transport",
    )(table, x_cells, y_cells, u0, v0, x_mass, y_mass)


def pair_tables(pair_lists, tgt_block, per_block, slots):
    width = pair_lists.shape[1]
    flat = pair_lists.reshape(-1)
    chosen = flat // per_block == tgt_block
    targets = flat % per_block
    sources = jnp.arange(flat.shape[0], dtype=jnp.int32) // width
    places = jnp.arange(slots, dtype=jnp.int32)
    rank = jnp.cumsum(chosen.astype(jnp.int32)) - 1
    matches = (rank[None, :] == places[:, None]) & chosen[None, :]
    row_src = jnp.sum(jnp.where(matches, sources[None, :], 0), axis=1)
    row_tgt = jnp.sum(jnp.where(matches, targets[None, :], 0), axis=1)
    live = places < jnp.sum(chosen.astype(jnp.int32))
    before = (row_tgt[None, :] < row_tgt[:, None]) | (
        (row_tgt[None, :] == row_tgt[:, None]) & (places[None, :] < places[:, None]))
    order = jnp.where(live, jnp.sum((before & live[None, :]).astype(jnp.int32), axis=1), places)
    moves = order[None, :] == places[:, None]
    col_src = jnp.sum(jnp.where(moves, row_src[None, :], 0), axis=1)
    col_tgt = jnp.sum(jnp.where(moves, row_tgt[None, :], 0), axis=1)

    def ends(kept):
        same = jnp.concatenate([jnp.zeros((1,), jnp.int32), (kept[1:] == kept[:-1]).astype(jnp.int32)])
        found = (kept[None, :] == places[:, None]) & live[None, :]
        last = jnp.max(jnp.where(found, places[None, :], -1), axis=1)
        return same, jnp.where(last < 0, slots, last)

    row_keep, row_last = ends(row_src)
    col_keep, col_last = ends(col_tgt)
    return jnp.concatenate([row_tgt, row_src, row_keep, row_last, col_src, col_tgt, col_keep, col_last])


def side(cells, mass, count):
    clusters = count.shape[0]
    wide = cells.astype(jnp.float32)
    norm = jnp.sum(wide * wide, axis=0).reshape(2 * clusters, 128)
    place = jnp.arange(2, dtype=jnp.int32)[None, :, None] * 128 + jnp.arange(128, dtype=jnp.int32)[None, None, :]
    live = (place < count[:, None, None]).reshape(2 * clusters, 128)
    logmass = jnp.where(live, jnp.log(mass).reshape(2 * clusters, 128), EMPTY)
    return norm, live, logmass


def shards(source_cells, target_cells, source_mass, target_mass, source_count, target_count, pair_lists):
    n_src, n_tgt = lax.axis_size("src"), lax.axis_size("tgt")
    slots = 2 * pair_lists.size // n_tgt
    table = pair_tables(pair_lists, lax.axis_index("tgt"), target_count.shape[0], slots)
    src_norm, src_live, src_logmass = side(source_cells, source_mass, source_count)
    tgt_norm, tgt_live, tgt_logmass = side(target_cells, target_mass, target_count)
    u0 = -2.0 * src_norm
    v0 = jnp.where(tgt_live, -2.0 * tgt_norm, EMPTY)
    u, v, mapped = transport(
        n_src, n_tgt, slots, table, source_cells, target_cells, u0, v0, src_logmass, tgt_logmass)
    source_pot = jnp.where(src_live, 0.5 * u + src_norm, 0.0)
    target_pot = jnp.where(tgt_live, 0.5 * v + tgt_norm, 0.0)
    return source_pot.reshape(-1), target_pot.reshape(-1), mapped


def solution(mesh):
    return jax.shard_map(
        shards,
        mesh=mesh,
        in_specs=(P(None, "src"), P(None, "tgt"), P("src"), P("tgt"), P("src"), P("tgt"), P("src", None)),
        out_specs=(P("src"), P("tgt"), P(None, ("src", "tgt"))),
        check_vma=False,
    )
```

```python
import functools
import math

import jax
import jax.numpy as jnp
from jax import lax
from jax.experimental import pallas as pl
from jax.experimental.pallas import tpu as pltpu
from jax.sharding import PartitionSpec as P

MESH = pl.DeviceIdType.MESH
EMPTY = -1e30
TILE = 256
SUB = 8
AUX = 16
CHUNKS = 8
NY = 2
MIB = 1 << 20
ROW_SUB, ROW_LANE, ROW_KEEP, ROW_LAST, COL_SUB, COL_LANE, COL_KEEP, COL_LAST = range(8)


def split3(row):
    high = row.astype(jnp.bfloat16).astype(jnp.float32)
    rest = row - high
    mid = rest.astype(jnp.bfloat16).astype(jnp.float32)
    low = rest - mid
    return high, mid, low


def cluster_row(ref, cluster):
    return ref[pl.ds(cluster, 1), :]


def halves_row(ref, cluster):
    first = ref[pl.ds(2 * cluster, 1), :]
    second = ref[pl.ds(2 * cluster + 1, 1), :]
    return jnp.concatenate([first, second], axis=1)


def put_halves(ref, cluster, row):
    ref[pl.ds(2 * cluster, 1), :] = row[:, :128]
    ref[pl.ds(2 * cluster + 1, 1), :] = row[:, 128:]


def squared_norm(cells):
    wide = cells.astype(jnp.float32)
    return jnp.sum(wide * wide, axis=0, keepdims=True)


def far_offset(axis, j, n):
    if axis == "tgt":
        return n // 2 + lax.div(j + 1, 2) * (1 - 2 * lax.rem(j, 2))
    i = lax.div(j, 2)
    near = n // 4 + lax.div(i + 1, 2) * (2 * lax.rem(i, 2) - 1)
    return near + lax.rem(j, 2) * (n - 2 * near)


def aux_rows(row, offset, other):
    at = lax.broadcasted_iota(jnp.int32, (AUX, TILE), 0)
    high, mid, low = split3(row)
    out = jnp.where((at >= other) & (at < other + 3), 1.0, 0.0)
    out = jnp.where(at == offset, high, out)
    out = jnp.where(at == offset + 1, mid, out)
    out = jnp.where(at == offset + 2, low, out)
    return out.astype(jnp.bfloat16)


def kernel(
    sizes, table, x_count, y_count, x_cells, y_cells, x_mass, y_mass, u_out, v_out, x_norm_out, y_norm_out, out,
    xs, ys, x_norm, u0, v0, u1, v1, u2, v2, parts, helds, slot_m, slot_s, slot_n, slot_d, send_a, send_y, den, held_d,
    first_y, ring_a, ring_b, last_y, *sems,
):
    n_src, n_tgt, slots = sizes
    step = math.gcd(slots, 16)
    features = x_cells.shape[0]
    clusters = x_cells.shape[1] // TILE
    me_src, me_tgt = lax.axis_index("src"), lax.axis_index("tgt")
    barrier = pltpu.get_barrier_semaphore()
    for axis, me, n in (("tgt", me_tgt, n_tgt), ("src", me_src, n_src)):
        for k in range(1, n):
            pl.semaphore_signal(barrier, inc=1, device_id={axis: lax.rem(me + k, n)}, device_id_type=MESH)

    slot_m[slots] = jnp.full((SUB, TILE), EMPTY, jnp.float32)
    slot_s[slots] = jnp.zeros((SUB, TILE), jnp.float32)
    slot_n[slots] = jnp.zeros((features, TILE), jnp.float32)
    slot_d[pl.ds(slots, SUB), :] = jnp.zeros((SUB, TILE), jnp.float32)

    def entry(which, p):
        return table[which * slots + p]

    def sweep(kind, first, sub_cells, lane_cells, sub_pot, lane_pot):
        def tile(p, carry):
            a, b, keep = entry(first, p), entry(first + 1, p), entry(first + 2, p)
            sub, lane = sub_cells[a], lane_cells[b]
            left = jnp.concatenate([sub, aux_rows(cluster_row(sub_pot, a), 0, 3)], axis=0)
            right = jnp.concatenate([lane, aux_rows(cluster_row(lane_pot, b), 3, 0)], axis=0)
            score = lax.dot_general(left, right, (((0,), (0,)), ((), ())), preferred_element_type=jnp.float32)
            hold = keep.astype(jnp.float32)
            if kind == "max":
                score = score.reshape(CHUNKS, TILE // SUB // CHUNKS, SUB, TILE)
                best = [jnp.max(score[q], axis=0) for q in range(CHUNKS)]
                old = carry[0] * hold + (1.0 - hold) * EMPTY
                new = functools.reduce(jnp.maximum, best, old)
                total = carry[1] * hold * jnp.exp(old - new)
                for q in range(CHUNKS):
                    total = total + jnp.sum(jnp.exp(score[q] - best[q][None]), axis=0) * jnp.exp(best[q] - new)
                slot_m[p] = new
                slot_s[p] = total
                return new, total
            weight = jnp.exp(score)
            if kind == "sum":
                total = carry[0] * hold + jnp.sum(weight.reshape(TILE // SUB, SUB, TILE), axis=0)
                slot_s[p] = total
                return (total,)
            high = weight.astype(jnp.bfloat16)
            low = (weight - high.astype(jnp.float32)).astype(jnp.bfloat16)
            ones = jnp.where(lax.broadcasted_iota(jnp.int32, (AUX, TILE), 0) == 0, 1.0, 0.0).astype(jnp.bfloat16)
            cells = jnp.concatenate([sub, ones], axis=0)
            moved = jnp.dot(cells, high, preferred_element_type=jnp.float32)
            moved = moved + jnp.dot(cells, low, preferred_element_type=jnp.float32)
            total = carry[0] * hold + moved[:features]
            weights = carry[1] * hold + moved[features:features + 1]
            slot_n[p] = total
            slot_d[pl.ds(p, 1), :] = weights
            return total, weights

        def group(g, carry):
            for r in range(step):
                carry = tile(g * step + r, carry)
            return carry

        empty = jnp.zeros((SUB, TILE), jnp.float32)
        if kind == "max":
            start = (empty + EMPTY, empty)
        elif kind == "sum":
            start = (empty,)
        else:
            start = (jnp.zeros((features, TILE), jnp.float32), jnp.zeros((1, TILE), jnp.float32))
        lax.fori_loop(0, slots // step, group, start)

    def reduce(kind, which, axis, me, n, last, old, mass, count, new, meanwhile):
        part, held = parts.at[which], helds.at[which]
        per = clusters // n
        lanes = lax.broadcasted_iota(jnp.int32, (1, TILE), 1)

        def shard(peer):
            return pl.ds(pl.multiple_of(peer * per, per), per)

        def finish(peer):
            rows = []
            for r in range(per):
                at = entry(last, peer * per + r)
                if kind == "max":
                    best = jnp.max(slot_m[at], axis=0, keepdims=True)
                    row = jnp.sum(slot_s[at] * jnp.exp(slot_m[at] - best), axis=0, keepdims=True)
                    rows.append(best + jnp.log(jnp.where(row > 0.0, row, 1.0)))
                else:
                    rows.append(jnp.sum(slot_s[at], axis=0, keepdims=True))
            part[shard(peer), :] = jnp.concatenate(rows, axis=0)

        def copy(j, phase):
            k = far_offset(axis, j, n)
            peer = lax.rem(me + k, n)
            mine = shard(me)
            src_ref, dst_ref = (part.at[shard(peer)], held.at[k]) if phase == 0 else (new.at[mine], new.at[mine])
            return pltpu.make_async_remote_copy(
                src_ref=src_ref, dst_ref=dst_ref,
                send_sem=sems[2 * phase].at[which, k], recv_sem=sems[2 * phase + 1].at[which, k],
                device_id={axis: peer}, device_id_type=MESH)

        if which == 0:
            pl.semaphore_wait(barrier, n_src + n_tgt - 2)

        @pl.loop(0, n - 1)
        def _(j):
            finish(lax.rem(me + far_offset(axis, j, n), n))
            copy(j, 0).start()

        finish(me)
        meanwhile()
        rows = []
        for r in range(per):
            c = me * per + r
            rows.append(jnp.where(lanes < count[c], jnp.log(halves_row(mass, c)), EMPTY))
        logmass = jnp.concatenate(rows, axis=0)

        @pl.loop(0, n - 1)
        def _(j):
            copy(j, 0).wait_recv()

        mine = shard(me)
        own = part[mine, :]
        if kind == "max":
            best = own
            for k in range(1, n):
                best = jnp.maximum(best, held[k])
            total = jnp.exp(own - best)
            for k in range(1, n):
                total = total + jnp.exp(held[k] - best)
            lse = best + jnp.log(total)
        else:
            total = own
            for k in range(1, n):
                total = total + held[k]
            lse = jnp.log(jnp.where(total > 0.0, total, 1.0))
        new[mine, :] = jnp.where(logmass > 0.5 * EMPTY, old[mine, :] + logmass - lse, EMPTY)

        @pl.loop(0, n - 1)
        def _(j):
            copy(j, 1).start()

        @pl.loop(0, n - 1)
        def _(j):
            copy(j, 0).wait_send()

        @pl.loop(0, n - 1)
        def _(j):
            copy(j, 1).wait()

    lane = lax.broadcasted_iota(jnp.int32, (1, TILE), 1)
    u0[...] = jnp.zeros(u0.shape, jnp.float32)

    @pl.loop(0, clusters // SUB)
    def _(g):
        rows = []
        for r in range(SUB):
            c = g * SUB + r
            at = pl.ds(pl.multiple_of(c * TILE, TILE), TILE)
            xs[c] = x_cells[:, at] * jnp.bfloat16(4.0)
            cells = y_cells[:, at]
            ys[c] = cells
            rows.append(jnp.where(lane < y_count[c], -2.0 * squared_norm(cells), EMPTY))
        v0[pl.ds(pl.multiple_of(g * SUB, SUB), SUB), :] = jnp.concatenate(rows, axis=0)

    def norms():
        @pl.loop(0, clusters // SUB)
        def _(g):
            for r in range(SUB):
                c = g * SUB + r
                put_halves(x_norm_out, c, squared_norm(xs[c]) * 0.0625)
                put_halves(y_norm_out, c, -0.5 * cluster_row(v0, c))

    def nothing():
        pass

    def write_u():
        @pl.loop(0, clusters // SUB)
        def _(g):
            for r in range(SUB):
                put_halves(u_out, g * SUB + r, cluster_row(u2, g * SUB + r))

    sweep("max", ROW_SUB, ys, xs, v0, u0)
    reduce("max", 0, "tgt", me_tgt, n_tgt, ROW_LAST, u0, x_mass, x_count, u1, nothing)
    sweep("max", COL_SUB, xs, ys, u1, v0)
    reduce("max", 1, "src", me_src, n_src, COL_LAST, v0, y_mass, y_count, v1, norms)
    sweep("sum", ROW_SUB, ys, xs, v1, u1)
    reduce("sum", 2, "tgt", me_tgt, n_tgt, ROW_LAST, u1, x_mass, x_count, u2, nothing)
    sweep("sum", COL_SUB, xs, ys, u2, v1)
    reduce("sum", 3, "src", me_src, n_src, COL_LAST, v1, y_mass, y_count, v2, write_u)
    sweep("map", ROW_SUB, ys, xs, v2, u2)

    n, nz = n_tgt, n_tgt // NY
    z, y = me_tgt // NY, lax.rem(me_tgt, NY)
    other = NY - 1 - y
    per = out.shape[1] // TILE
    half = per // 4
    sign = (1, -1)

    def device(at):
        return lax.rem(at + nz, nz) * NY + y

    def block(d, hop):
        return lax.rem(z - sign[d] * (1 + hop) + 2 * nz, nz)

    def own(at, side, base, c):
        return slot_n[entry(ROW_LAST, (at * NY + side) * per + base + c)]

    def copy(src, dst, sem, k, peer):
        made = pltpu.make_async_remote_copy(
            src_ref=src, dst_ref=dst, send_sem=sems[2 * sem].at[k], recv_sem=sems[2 * sem + 1].at[k],
            device_id={"tgt": peer}, device_id_type=MESH)
        made.start()
        return made

    partner = z * NY + other
    over_y = [[None] * nz for _ in sign]
    over_a = [[[None] * nz for _ in range(NY)] for _ in sign]
    over_b = [[None] * nz for _ in sign]
    sides = (other, y)
    for s in range(NY):
        for d in range(2):
            for c in range(half):
                send_a[d, s, c] = own(block(d, 0), sides[s], d * half, c)
            over_a[d][s][0] = copy(send_a.at[d, s], ring_a.at[d, 0, s], 3, (d * NY + s) * nz, device(z + sign[d]))
    for hop in range(nz):
        for d in range(2):
            for c in range(half):
                send_y[d, hop, c] = own(block(d, hop), other, (2 + d) * half, c)
            over_y[d][hop] = copy(send_y.at[d, hop], first_y.at[d, hop], 2, d * nz + hop, partner)

    def gather(t):
        for c in range(per):
            den[t, pl.ds(c, 1), :] = slot_d[pl.ds(entry(ROW_LAST, t * per + c), 1), :]

    pl.loop(0, n)(gather)
    others = []
    for k in range(1, n):
        peer = lax.rem(me_tgt + k, n)
        others.append(copy(den.at[peer], held_d.at[k], 6, k, peer))
    over_last = []
    for hop in range(nz):
        at = [block(d, hop) for d in range(2)]
        for d in range(2):
            over_y[d][hop].wait_recv()
            if hop > 0:
                over_b[d][hop - 1].wait_recv()
            for c in range(half):
                value = first_y[d, hop, c] + own(at[d], y, (2 + d) * half, c)
                if hop > 0:
                    value = value + ring_b[d, hop - 1, c]
                first_y[d, hop, c] = value
            if hop < nz - 1:
                over_b[d][hop] = copy(first_y.at[d, hop], ring_b.at[d, hop], 4, d * nz + hop, device(z + sign[d]))
        for s in range(NY):
            for d in range(2):
                if hop == 0:
                    continue
                over_a[d][s][hop - 1].wait_recv()
                for c in range(half):
                    ring_a[d, hop - 1, s, c] += own(at[d], sides[s], d * half, c)
                if hop < nz - 1:
                    over_a[d][s][hop] = copy(
                        ring_a.at[d, hop - 1, s], ring_a.at[d, hop, s], 3, (d * NY + s) * nz + hop, device(z + sign[d]))
                elif s == 0:
                    over_last.append(copy(ring_a.at[d, nz - 2, 0], last_y.at[d], 5, d, partner))

    @pl.loop(0, clusters // SUB)
    def _(g):
        for r in range(SUB):
            put_halves(v_out, g * SUB + r, cluster_row(v2, g * SUB + r))

    for made in others:
        made.wait_recv()
    total = den[me_tgt]
    for k in range(1, n):
        total = total + held_d[k]
    total = jnp.where(total > 0.0, total, 1.0)

    def put(c, value):
        out[:, c * TILE:(c + 1) * TILE] = value / total[c:c + 1]

    for d in range(2):
        for c in range(half):
            put((2 + d) * half + c, first_y[d, nz - 1, c])
    for d in range(2):
        over_last[d].wait_recv()
        for c in range(half):
            put(d * half + c, ring_a[d, nz - 2, 1, c] + last_y[d, c])
    for made in others + over_last:
        made.wait_send()
    for d in range(2):
        for hop in range(nz):
            over_y[d][hop].wait_send()
        for hop in range(nz - 1):
            for s in range(NY):
                over_a[d][s][hop].wait_send()
            over_b[d][hop].wait_send()


def transport(n_src, n_tgt, slots, table, x_count, y_count, x_cells, y_cells, x_mass, y_mass):
    features = x_cells.shape[0]
    clusters = x_cells.shape[1] // TILE
    per, nz = clusters // n_tgt, n_tgt // NY
    quarter = per // 4
    f32 = jnp.float32
    vmem = pl.BlockSpec(memory_space=pltpu.VMEM)
    smem = pl.BlockSpec(memory_space=pltpu.SMEM)
    dma = pltpu.SemaphoreType.DMA
    most = max(n_src, n_tgt)
    sems = [dma((4, most))] * 4
    for many in (2 * nz, 2 * NY * nz, 2 * nz, 2, n_tgt):
        sems += [dma((many,))] * 2
    flat = jax.ShapeDtypeStruct((2 * clusters, TILE // 2), f32)
    row = pltpu.VMEM((clusters, TILE), f32)
    cells = pltpu.VMEM((clusters, features, TILE), jnp.bfloat16)
    scratch = [cells, cells] + [row] * 7 + [
        pltpu.VMEM((4, clusters, TILE), f32),
        pltpu.VMEM((4, most, clusters // min(n_src, n_tgt), TILE), f32),
        pltpu.VMEM((slots + 1, SUB, TILE), f32),
        pltpu.VMEM((slots + 1, SUB, TILE), f32),
        pltpu.VMEM((slots + 1, features, TILE), f32),
        pltpu.VMEM((slots + SUB, TILE), f32),
        pltpu.VMEM((2, NY, quarter, features, TILE), f32),
        pltpu.VMEM((2, nz, quarter, features, TILE), f32),
        pltpu.VMEM((n_tgt, per, TILE), f32),
        pltpu.VMEM((n_tgt, per, TILE), f32),
        pltpu.VMEM((2, nz, quarter, features, TILE), f32),
        pltpu.VMEM((2, nz - 1, NY, quarter, features, TILE), f32),
        pltpu.VMEM((2, nz - 1, quarter, features, TILE), f32),
        pltpu.VMEM((2, quarter, features, TILE), f32),
    ]
    return pl.pallas_call(
        functools.partial(kernel, (n_src, n_tgt, slots)),
        out_shape=(flat,) * 4 + (jax.ShapeDtypeStruct((features, per * TILE), f32),),
        in_specs=[smem] * 3 + [vmem] * 4,
        out_specs=(vmem,) * 5,
        scratch_shapes=scratch + sems,
        compiler_params=pltpu.CompilerParams(collective_id=0, has_side_effects=True, vmem_limit_bytes=40 * MIB),
        name="transport",
    )(table, x_count, y_count, x_cells, y_cells, x_mass, y_mass)


def pair_tables(pair_lists, tgt_block, per_block, slots):
    width = pair_lists.shape[1]
    flat = pair_lists.reshape(-1)
    chosen = flat // per_block == tgt_block
    targets = flat % per_block
    sources = jnp.arange(flat.shape[0], dtype=jnp.int32) // width
    places = jnp.arange(slots, dtype=jnp.int32)
    rank = jnp.cumsum(chosen.astype(jnp.int32)) - 1
    matches = (rank[None, :] == places[:, None]) & chosen[None, :]
    row_src = jnp.sum(jnp.where(matches, sources[None, :], 0), axis=1)
    row_tgt = jnp.sum(jnp.where(matches, targets[None, :], 0), axis=1)
    live = places < jnp.sum(chosen.astype(jnp.int32))
    before = (row_tgt[None, :] < row_tgt[:, None]) | (
        (row_tgt[None, :] == row_tgt[:, None]) & (places[None, :] < places[:, None]))
    order = jnp.where(live, jnp.sum((before & live[None, :]).astype(jnp.int32), axis=1), places)
    moves = order[None, :] == places[:, None]
    col_src = jnp.sum(jnp.where(moves, row_src[None, :], 0), axis=1)
    col_tgt = jnp.sum(jnp.where(moves, row_tgt[None, :], 0), axis=1)

    def ends(kept):
        same = jnp.concatenate([jnp.zeros((1,), jnp.int32), (kept[1:] == kept[:-1]).astype(jnp.int32)])
        found = (kept[None, :] == places[:, None]) & live[None, :]
        last = jnp.max(jnp.where(found, places[None, :], -1), axis=1)
        return same, jnp.where(last < 0, slots, last)

    row_keep, row_last = ends(row_src)
    col_keep, col_last = ends(col_tgt)
    return jnp.concatenate([row_tgt, row_src, row_keep, row_last, col_src, col_tgt, col_keep, col_last])


def shards(source_cells, target_cells, source_mass, target_mass, source_count, target_count, pair_lists):
    n_src, n_tgt = lax.axis_size("src"), lax.axis_size("tgt")
    slots = 2 * pair_lists.size // n_tgt
    table = pair_tables(pair_lists, lax.axis_index("tgt"), target_count.shape[0], slots)
    u, v, x_norm, y_norm, mapped = transport(
        n_src, n_tgt, slots, table, source_count, target_count, source_cells, target_cells,
        source_mass.reshape(-1, TILE // 2), target_mass.reshape(-1, TILE // 2))
    source_pot = jnp.where(u > 0.5 * EMPTY, 0.5 * u + x_norm, 0.0)
    target_pot = jnp.where(v > 0.5 * EMPTY, 0.5 * v + y_norm, 0.0)
    return source_pot.reshape(-1), target_pot.reshape(-1), mapped


def solution(mesh):
    return jax.shard_map(
        shards,
        mesh=mesh,
        in_specs=(P(None, "src"), P(None, "tgt"), P("src"), P("tgt"), P("src"), P("tgt"), P("src", None)),
        out_specs=(P("src"), P("tgt"), P(None, ("src", "tgt"))),
        check_vma=False,
    )
```

```python
import functools
import math

import jax
import jax.numpy as jnp
from jax import lax
from jax.experimental import pallas as pl
from jax.experimental.pallas import tpu as pltpu
from jax.sharding import PartitionSpec as P

MESH = pl.DeviceIdType.MESH
EMPTY = -1e30
TILE = 256
SUB = 8
AUX = 16
CHUNKS = 8
CODE = 32752.0
NY = 2
MIB = 1 << 20
ROW_SUB, ROW_LANE, ROW_KEEP, ROW_LAST, COL_SUB, COL_LANE, COL_KEEP, COL_LAST, SRC_COUNT, TGT_COUNT = range(10)


def split3(row):
    high = row.astype(jnp.bfloat16).astype(jnp.float32)
    rest = row - high
    mid = rest.astype(jnp.bfloat16).astype(jnp.float32)
    low = rest - mid
    return high, mid, low


def cluster_row(ref, cluster):
    return ref[pl.ds(cluster, 1), :]


def halves_row(ref, cluster):
    first = ref[pl.ds(2 * cluster, 1), :]
    second = ref[pl.ds(2 * cluster + 1, 1), :]
    return jnp.concatenate([first, second], axis=1)


def put_halves(ref, cluster, row):
    ref[pl.ds(2 * cluster, 1), :] = row[:, :128]
    ref[pl.ds(2 * cluster + 1, 1), :] = row[:, 128:]


def squared_norm(cells):
    wide = cells.astype(jnp.float32)
    return jnp.sum(wide * wide, axis=0, keepdims=True)


def far_offset(axis, j, n):
    if axis == "tgt":
        return n // 2 + lax.div(j + 1, 2) * (1 - 2 * lax.rem(j, 2))
    i = lax.div(j, 2)
    near = n // 4 + lax.div(i + 1, 2) * (2 * lax.rem(i, 2) - 1)
    return near + lax.rem(j, 2) * (n - 2 * near)


def aux_rows(row, offset, other):
    at = lax.broadcasted_iota(jnp.int32, (AUX, TILE), 0)
    high, mid, low = split3(row)
    out = jnp.where((at >= other) & (at < other + 3), 1.0, 0.0)
    out = jnp.where(at == offset, high, out)
    out = jnp.where(at == offset + 1, mid, out)
    out = jnp.where(at == offset + 2, low, out)
    return out.astype(jnp.bfloat16)


def kernel(
    sizes, table, xs, ys, x_mass, y_mass, u_out, v_out, x_norm_out, y_norm_out, out,
    masses, u0, v0, u1, v1, u2, v2, parts, helds, slot_m, slot_s, slot_n, slot_d, send_a, send_y, den, held_d,
    first_y, ring_a, ring_b, last_y, kept, local, *sems,
):
    n_src, n_tgt, slots = sizes
    step = math.gcd(slots, 16)
    clusters, features = xs.shape[:2]
    me_src, me_tgt = lax.axis_index("src"), lax.axis_index("tgt")
    barrier = pltpu.get_barrier_semaphore()
    for axis, me, n in (("tgt", me_tgt, n_tgt), ("src", me_src, n_src)):
        for k in range(1, n):
            pl.semaphore_signal(barrier, inc=1, device_id={axis: lax.rem(me + k, n)}, device_id_type=MESH)

    fetches = []
    for i, (mass, me, n) in enumerate(((x_mass, me_tgt, n_tgt), (y_mass, me_src, n_src))):
        rows = 2 * clusters // n
        fetch = pltpu.make_async_copy(
            mass.at[pl.ds(pl.multiple_of(me * rows, rows), rows)], masses.at[i], local.at[i])
        fetch.start()
        fetches.append(fetch)
    slot_m[slots] = jnp.full((SUB, TILE), EMPTY, jnp.float32)
    slot_s[slots] = jnp.zeros((SUB, TILE), jnp.float32)
    slot_n[slots] = jnp.zeros((features, TILE), jnp.float32)
    slot_d[pl.ds(slots, SUB), :] = jnp.zeros((SUB, TILE), jnp.float32)

    def entry(which, p):
        return table[which * slots + p]

    def scaled(cells, ref):
        return cells * jnp.bfloat16(4.0) if ref is xs else cells

    def sweep(kind, first, sub_cells, lane_cells, sub_pot, lane_pot):
        def tile(p, carry):
            a, b, keep = entry(first, p), entry(first + 1, p), entry(first + 2, p)
            sub, lane = sub_cells[a], lane_cells[b]
            left = jnp.concatenate([scaled(sub, sub_cells), aux_rows(cluster_row(sub_pot, a), 0, 3)], axis=0)
            right = jnp.concatenate([scaled(lane, lane_cells), aux_rows(cluster_row(lane_pot, b), 3, 0)], axis=0)
            score = lax.dot_general(left, right, (((0,), (0,)), ((), ())), preferred_element_type=jnp.float32)
            hold = keep.astype(jnp.float32)
            if kind == "max":
                score = score.reshape(CHUNKS, TILE // SUB // CHUNKS, SUB, TILE)
                best = [jnp.max(score[q], axis=0) for q in range(CHUNKS)]
                old = carry[0] * hold + (1.0 - hold) * EMPTY
                new = functools.reduce(jnp.maximum, best, old)
                total = carry[1] * hold * jnp.exp(old - new)
                for q in range(CHUNKS):
                    total = total + jnp.sum(jnp.exp(score[q] - best[q][None]), axis=0) * jnp.exp(best[q] - new)
                slot_m[p] = new
                slot_s[p] = total
                return new, total
            weight = jnp.exp(score)
            if kind == "sum":
                total = carry[0] * hold + jnp.sum(weight.reshape(TILE // SUB, SUB, TILE), axis=0)
                slot_s[p] = total
                return (total,)
            high = weight.astype(jnp.bfloat16)
            low = (weight - high.astype(jnp.float32)).astype(jnp.bfloat16)
            ones = jnp.where(lax.broadcasted_iota(jnp.int32, (AUX, TILE), 0) == 0, 1.0, 0.0).astype(jnp.bfloat16)
            cells = jnp.concatenate([sub, ones], axis=0)
            moved = jnp.dot(cells, high, preferred_element_type=jnp.float32)
            moved = moved + jnp.dot(cells, low, preferred_element_type=jnp.float32)
            total = carry[0] * hold + moved[:features]
            weights = carry[1] * hold + moved[features:features + 1]
            slot_n[p] = total
            slot_d[pl.ds(p, 1), :] = weights
            return total, weights

        def group(g, carry):
            for r in range(step):
                carry = tile(g * step + r, carry)
            return carry

        empty = jnp.zeros((SUB, TILE), jnp.float32)
        if kind == "max":
            start = (empty + EMPTY, empty)
        elif kind == "sum":
            start = (empty,)
        else:
            start = (jnp.zeros((features, TILE), jnp.float32), jnp.zeros((1, TILE), jnp.float32))
        lax.fori_loop(0, slots // step, group, start)

    def reduce(kind, which, axis, me, n, last, old, new, meanwhile):
        part, held = parts.at[which], helds.at[which]
        per = clusters // n
        lanes = lax.broadcasted_iota(jnp.int32, (1, TILE), 1)

        def shard(peer):
            return pl.ds(pl.multiple_of(peer * per, per), per)

        def finish(peer):
            rows = []
            for r in range(per):
                at = entry(last, peer * per + r)
                if kind == "max":
                    best = jnp.max(slot_m[at], axis=0, keepdims=True)
                    row = jnp.sum(slot_s[at] * jnp.exp(slot_m[at] - best), axis=0, keepdims=True)
                    rows.append(best + jnp.log(jnp.where(row > 0.0, row, 1.0)))
                else:
                    rows.append(jnp.sum(slot_s[at], axis=0, keepdims=True))
            part[shard(peer), :] = jnp.concatenate(rows, axis=0)

        def copy(j, phase):
            k = far_offset(axis, j, n)
            peer = lax.rem(me + k, n)
            mine = shard(me)
            src_ref, dst_ref = (part.at[shard(peer)], held.at[k]) if phase == 0 else (new.at[mine], new.at[mine])
            return pltpu.make_async_remote_copy(
                src_ref=src_ref, dst_ref=dst_ref,
                send_sem=sems[2 * phase].at[which, k], recv_sem=sems[2 * phase + 1].at[which, k],
                device_id={axis: peer}, device_id_type=MESH)

        if which == 0:
            pl.semaphore_wait(barrier, n_src + n_tgt - 2)

        @pl.loop(0, n - 1)
        def _(j):
            finish(lax.rem(me + far_offset(axis, j, n), n))
            copy(j, 0).start()

        finish(me)
        meanwhile()
        if which < 2:
            fetches[which].wait()
        mass = masses.at[which % 2]
        count = (SRC_COUNT, TGT_COUNT)[which % 2]
        rows = []
        for r in range(per):
            rows.append(jnp.where(lanes < entry(count, me * per + r), jnp.log(halves_row(mass, r)), EMPTY))
        logmass = jnp.concatenate(rows, axis=0)

        @pl.loop(0, n - 1)
        def _(j):
            copy(j, 0).wait_recv()

        mine = shard(me)
        own = part[mine, :]
        if kind == "max":
            best = own
            for k in range(1, n):
                best = jnp.maximum(best, held[k])
            total = jnp.exp(own - best)
            for k in range(1, n):
                total = total + jnp.exp(held[k] - best)
            lse = best + jnp.log(total)
        else:
            total = own
            for k in range(1, n):
                total = total + held[k]
            lse = jnp.log(jnp.where(total > 0.0, total, 1.0))
        new[mine, :] = jnp.where(logmass > 0.5 * EMPTY, old[mine, :] + logmass - lse, EMPTY)

        @pl.loop(0, n - 1)
        def _(j):
            copy(j, 1).start()

        @pl.loop(0, n - 1)
        def _(j):
            copy(j, 0).wait_send()

        @pl.loop(0, n - 1)
        def _(j):
            copy(j, 1).wait()

    lane = lax.broadcasted_iota(jnp.int32, (1, TILE), 1)
    u0[...] = jnp.zeros(u0.shape, jnp.float32)

    @pl.loop(0, clusters // SUB)
    def _(g):
        rows = []
        for r in range(SUB):
            c = g * SUB + r
            rows.append(jnp.where(lane < entry(TGT_COUNT, c), -2.0 * squared_norm(ys[c]), EMPTY))
        v0[pl.ds(pl.multiple_of(g * SUB, SUB), SUB), :] = jnp.concatenate(rows, axis=0)

    def norms():
        @pl.loop(0, clusters // SUB)
        def _(g):
            for r in range(SUB):
                c = g * SUB + r
                put_halves(x_norm_out, c, squared_norm(xs[c]))
                put_halves(y_norm_out, c, -0.5 * cluster_row(v0, c))

    def nothing():
        pass

    def write_u():
        @pl.loop(0, clusters // SUB)
        def _(g):
            for r in range(SUB):
                put_halves(u_out, g * SUB + r, cluster_row(u2, g * SUB + r))

    sweep("max", ROW_SUB, ys, xs, v0, u0)
    reduce("max", 0, "tgt", me_tgt, n_tgt, ROW_LAST, u0, u1, nothing)
    sweep("max", COL_SUB, xs, ys, u1, v0)
    reduce("max", 1, "src", me_src, n_src, COL_LAST, v0, v1, norms)
    sweep("sum", ROW_SUB, ys, xs, v1, u1)
    reduce("sum", 2, "tgt", me_tgt, n_tgt, ROW_LAST, u1, u2, nothing)
    sweep("sum", COL_SUB, xs, ys, u2, v1)
    reduce("sum", 3, "src", me_src, n_src, COL_LAST, v1, v2, write_u)
    sweep("map", ROW_SUB, ys, xs, v2, u2)

    n, nz = n_tgt, n_tgt // NY
    z, y = me_tgt // NY, lax.rem(me_tgt, NY)
    other = NY - 1 - y
    sides = (other, y)
    per = out.shape[1] // TILE
    half = per // 2
    sign = (1, -1)
    far = nz // 2
    hops = ((far, nz - 1 - far), (nz - 1 - far, far))
    partner = z * NY + other

    def toward(d):
        return lax.rem(z + sign[d] + nz, nz) * NY + y

    def block(g, d, hop):
        return lax.rem(z + sign[d] * (hops[g][d] - hop) + nz, nz)

    def own(at, side, g, c):
        return slot_n[entry(ROW_LAST, (at * NY + side) * per + g * half + c)]

    def copy(src, dst, sem, k, peer):
        made = pltpu.make_async_remote_copy(
            src_ref=src, dst_ref=dst, send_sem=sems[2 * sem].at[k], recv_sem=sems[2 * sem + 1].at[k],
            device_id={"tgt": peer}, device_id_type=MESH)
        made.start()
        return made

    def encode(ref, values):
        exponents = []
        for c in range(half):
            value = values(c)
            largest = jnp.max(jnp.abs(value), axis=0, keepdims=True)
            exponent = jnp.ceil(jnp.log2(jnp.maximum(largest, 1e-30)))
            code = jnp.floor(value * (jnp.exp2(-exponent) * CODE) + 0.5)
            ref[c * features:(c + 1) * features, :] = code.astype(jnp.int32).astype(jnp.int16)
            exponents.append(exponent)
        exponents.append(jnp.zeros((AUX - half, TILE), jnp.float32))
        block = jnp.concatenate(exponents, axis=0)
        ref[half * features:half * features + AUX, :] = block.astype(jnp.int32).astype(jnp.int16)

    def decoder(ref):
        exponents = ref[half * features:half * features + AUX, :].astype(jnp.int32).astype(jnp.float32)
        scale = jnp.exp2(exponents) * (1.0 / CODE)
        return lambda c: (
            ref[c * features:(c + 1) * features, :].astype(jnp.int32).astype(jnp.float32) * scale[c:c + 1])

    pieces = [(d, hop) for hop in range(far) for d in range(2) if hop < hops[1][d]]
    over_y = {}
    over_a = {}
    over_b = {}

    def send_piece(i, at):
        encode(send_y.at[i], lambda c: own(at, other, 1, c))
        over_y[i] = copy(send_y.at[i], first_y.at[i], 2, i, partner)

    for i in range(2):
        d, hop = pieces[i]
        send_piece(i, block(1, d, hop))
        for s in range(NY):
            encode(send_a.at[i, s], lambda c: own(block(0, i, 0), sides[s], 0, c))
            over_a[i, s, 0] = copy(send_a.at[i, s], ring_a.at[i, 0, s], 3, (i * NY + s) * far, toward(i))
    for i in range(2, nz - 1):
        d, hop = pieces[i]
        send_piece(i, block(1, d, hop))
    send_piece(nz - 1, z)

    def gather(t):
        for c in range(per):
            den[t, pl.ds(c, 1), :] = slot_d[pl.ds(entry(ROW_LAST, t * per + c), 1), :]

    pl.loop(0, n)(gather)
    others = []
    for k in range(1, n):
        peer = lax.rem(me_tgt + k, n)
        others.append(copy(den.at[peer], held_d.at[k], 6, k, peer))

    def step_b(d, hop):
        i = pieces.index((d, hop))
        over_y[i].wait_recv()
        parts_of = [decoder(first_y.at[i])]
        if hop > 0:
            over_b[d, hop - 1].wait_recv()
            parts_of.append(decoder(ring_b.at[d, hop - 1]))
        at = block(1, d, hop)
        encode(first_y.at[i], lambda c: sum((part(c) for part in parts_of), own(at, y, 1, c)))
        over_b[d, hop] = copy(first_y.at[i], ring_b.at[d, hop], 4, d * far + hop, toward(d))

    def step_a(d, s, hop):
        over_a[d, s, hop - 1].wait_recv()
        held = ring_a.at[d, hop - 1, s]
        arrived = decoder(held)
        at = block(0, d, hop)
        encode(held, lambda c: arrived(c) + own(at, sides[s], 0, c))
        over_a[d, s, hop] = copy(held, ring_a.at[d, hop, s], 3, (d * NY + s) * far + hop, toward(d))

    for hop in range(far):
        for d in range(2):
            if hop < hops[1][d]:
                step_b(d, hop)
        for s in range(NY):
            for d in range(2):
                if 0 < hop < hops[0][d]:
                    step_a(d, s, hop)

    def arrived_a(s):
        both = []
        for d in range(2):
            over_a[d, s, hops[0][d] - 1].wait_recv()
            both.append(decoder(ring_a.at[d, hops[0][d] - 1, s]))
        return lambda c: both[0](c) + both[1](c) + own(z, sides[s], 0, c)

    encode(kept, arrived_a(0))
    over_last = copy(kept, last_y, 5, 0, partner)

    @pl.loop(0, clusters // SUB)
    def _(g):
        for r in range(SUB):
            put_halves(v_out, g * SUB + r, cluster_row(v2, g * SUB + r))

    for made in others:
        made.wait_recv()
    total = den[me_tgt]
    for k in range(1, n):
        total = total + held_d[k]
    total = jnp.where(total > 0.0, total, 1.0)

    def put(c, value):
        out[:, c * TILE:(c + 1) * TILE] = value / total[c:c + 1]

    over_y[nz - 1].wait_recv()
    parts_b = [decoder(first_y.at[nz - 1])]
    for d in range(2):
        over_b[d, hops[1][d] - 1].wait_recv()
        parts_b.append(decoder(ring_b.at[d, hops[1][d] - 1]))
    for c in range(half):
        put(half + c, sum((part(c) for part in parts_b), own(z, y, 1, c)))
    mine = arrived_a(1)
    over_last.wait_recv()
    last = decoder(last_y)
    for c in range(half):
        put(c, mine(c) + last(c))
    for made in others + [over_last] + list(over_y.values()) + list(over_a.values()) + list(over_b.values()):
        made.wait_send()


def transport(n_src, n_tgt, slots, table, xs, ys, x_mass, y_mass):
    clusters, features = xs.shape[:2]
    per, nz = clusters // n_tgt, n_tgt // NY
    far = nz // 2
    f32 = jnp.float32
    vmem = pl.BlockSpec(memory_space=pltpu.VMEM)
    smem = pl.BlockSpec(memory_space=pltpu.SMEM)
    hbm = pl.BlockSpec(memory_space=pl.ANY)
    dma = pltpu.SemaphoreType.DMA
    most = max(n_src, n_tgt)
    sems = [dma((4, most))] * 4
    for many in (nz, 2 * NY * far, 2 * far, 1, n_tgt):
        sems += [dma((many,))] * 2
    flat = jax.ShapeDtypeStruct((2 * clusters, TILE // 2), f32)
    row = pltpu.VMEM((clusters, TILE), f32)
    coded = (per // 2 * features + AUX, TILE)

    def codes(*many):
        return pltpu.VMEM(many + coded, jnp.int16)

    scratch = [pltpu.VMEM((2, 2 * clusters // n_tgt, TILE // 2), f32)] + [row] * 6 + [
        pltpu.VMEM((4, clusters, TILE), f32),
        pltpu.VMEM((4, most, clusters // min(n_src, n_tgt), TILE), f32),
        pltpu.VMEM((slots + 1, SUB, TILE), f32),
        pltpu.VMEM((slots + 1, SUB, TILE), f32),
        pltpu.VMEM((slots + 1, features, TILE), f32),
        pltpu.VMEM((slots + SUB, TILE), f32),
        codes(2, NY),
        codes(nz),
        pltpu.VMEM((n_tgt, per, TILE), f32),
        pltpu.VMEM((n_tgt, per, TILE), f32),
        codes(nz),
        codes(2, far, NY),
        codes(2, far),
        codes(),
        codes(),
        dma((2,)),
    ]
    return pl.pallas_call(
        functools.partial(kernel, (n_src, n_tgt, slots)),
        out_shape=(flat,) * 4 + (jax.ShapeDtypeStruct((features, per * TILE), f32),),
        in_specs=[smem, vmem, vmem, hbm, hbm],
        out_specs=(vmem,) * 5,
        scratch_shapes=scratch + sems,
        compiler_params=pltpu.CompilerParams(collective_id=0, has_side_effects=True, vmem_limit_bytes=40 * MIB),
        name="transport",
    )(table, xs, ys, x_mass, y_mass)


def pair_tables(pair_lists, tgt_block, per_block, slots, counts):
    width = pair_lists.shape[1]
    flat = pair_lists.reshape(-1)
    chosen = flat // per_block == tgt_block
    targets = flat % per_block
    sources = jnp.arange(flat.shape[0], dtype=jnp.int32) // width
    places = jnp.arange(slots, dtype=jnp.int32)
    rank = jnp.cumsum(chosen.astype(jnp.int32)) - 1
    matches = (rank[None, :] == places[:, None]) & chosen[None, :]
    row_src = jnp.sum(jnp.where(matches, sources[None, :], 0), axis=1)
    row_tgt = jnp.sum(jnp.where(matches, targets[None, :], 0), axis=1)
    live = places < jnp.sum(chosen.astype(jnp.int32))
    before = (row_tgt[None, :] < row_tgt[:, None]) | (
        (row_tgt[None, :] == row_tgt[:, None]) & (places[None, :] < places[:, None]))
    order = jnp.where(live, jnp.sum((before & live[None, :]).astype(jnp.int32), axis=1), places)
    moves = order[None, :] == places[:, None]
    col_src = jnp.sum(jnp.where(moves, row_src[None, :], 0), axis=1)
    col_tgt = jnp.sum(jnp.where(moves, row_tgt[None, :], 0), axis=1)

    def ends(kept):
        same = jnp.concatenate([jnp.zeros((1,), jnp.int32), (kept[1:] == kept[:-1]).astype(jnp.int32)])
        found = (kept[None, :] == places[:, None]) & live[None, :]
        last = jnp.max(jnp.where(found, places[None, :], -1), axis=1)
        return same, jnp.where(last < 0, slots, last)

    row_keep, row_last = ends(row_src)
    col_keep, col_last = ends(col_tgt)
    return jnp.concatenate([row_tgt, row_src, row_keep, row_last, col_src, col_tgt, col_keep, col_last] + counts)


def shards(source_cells, target_cells, source_mass, target_mass, source_count, target_count, pair_lists):
    n_src, n_tgt = lax.axis_size("src"), lax.axis_size("tgt")
    slots = 2 * pair_lists.size // n_tgt
    table = pair_tables(
        pair_lists, lax.axis_index("tgt"), target_count.shape[0], slots, [source_count, target_count])
    xs, ys = (
        jnp.transpose(cells.reshape(cells.shape[0], -1, TILE), (1, 0, 2)) for cells in (source_cells, target_cells))
    u, v, x_norm, y_norm, mapped = transport(
        n_src, n_tgt, slots, table, xs, ys,
        source_mass.reshape(-1, TILE // 2), target_mass.reshape(-1, TILE // 2))
    source_pot = jnp.where(u > 0.5 * EMPTY, 0.5 * u + x_norm, 0.0)
    target_pot = jnp.where(v > 0.5 * EMPTY, 0.5 * v + y_norm, 0.0)
    return source_pot.reshape(-1), target_pot.reshape(-1), mapped


def solution(mesh):
    return jax.shard_map(
        shards,
        mesh=mesh,
        in_specs=(P(None, "src"), P(None, "tgt"), P("src"), P("tgt"), P("src"), P("tgt"), P("src", None)),
        out_specs=(P("src"), P("tgt"), P(None, ("src", "tgt"))),
        check_vma=False,
    )
```

```python
import functools
import math

import jax
import jax.numpy as jnp
from jax import lax
from jax.experimental import pallas as pl
from jax.experimental.pallas import tpu as pltpu
from jax.sharding import PartitionSpec as P

MESH = pl.DeviceIdType.MESH
EMPTY = -1e30
TILE = 256
SUB = 8
AUX = 16
CHUNKS = 8
CODE = 32752.0
NY = 2
MIB = 1 << 20
ROW_SUB, ROW_LANE, ROW_KEEP, ROW_LAST, COL_SUB, COL_LANE, COL_KEEP, COL_LAST, SRC_COUNT, TGT_COUNT = range(10)


def split3(row):
    high = row.astype(jnp.bfloat16).astype(jnp.float32)
    rest = row - high
    mid = rest.astype(jnp.bfloat16).astype(jnp.float32)
    low = rest - mid
    return high, mid, low


def cluster_row(ref, cluster):
    return ref[pl.ds(cluster, 1), :]


def halves_row(ref, cluster):
    first = ref[pl.ds(2 * cluster, 1), :]
    second = ref[pl.ds(2 * cluster + 1, 1), :]
    return jnp.concatenate([first, second], axis=1)


def put_halves(ref, cluster, row):
    ref[pl.ds(2 * cluster, 1), :] = row[:, :128]
    ref[pl.ds(2 * cluster + 1, 1), :] = row[:, 128:]


def squared_norm(cells):
    wide = cells.astype(jnp.float32)
    return jnp.sum(wide * wide, axis=0, keepdims=True)


def far_offset(axis, j, n):
    if axis == "tgt":
        return n // 2 + lax.div(j + 1, 2) * (1 - 2 * lax.rem(j, 2))
    i = lax.div(j, 2)
    near = n // 4 + lax.div(i + 1, 2) * (2 * lax.rem(i, 2) - 1)
    return near + lax.rem(j, 2) * (n - 2 * near)


def aux_rows(row, offset, other):
    at = lax.broadcasted_iota(jnp.int32, (AUX, TILE), 0)
    high, mid, low = split3(row)
    out = jnp.where((at >= other) & (at < other + 3), 1.0, 0.0)
    out = jnp.where(at == offset, high, out)
    out = jnp.where(at == offset + 1, mid, out)
    out = jnp.where(at == offset + 2, low, out)
    return out.astype(jnp.bfloat16)


def kernel(
    sizes, table, xs, ys, x_mass, y_mass, u_out, v_out, x_norm_out, y_norm_out, out,
    masses, u0, v0, u1, v1, u2, v2, parts, helds, slot_m, slot_s, slot_n, slot_d, send_a, send_y, den, held_d,
    first_y, ring_a, ring_b, last_y, kept, local, *sems,
):
    n_src, n_tgt, slots = sizes
    step = math.gcd(slots, 32)
    clusters, features = xs.shape[:2]
    me_src, me_tgt = lax.axis_index("src"), lax.axis_index("tgt")
    barrier = pltpu.get_barrier_semaphore()
    for axis, me, n in (("tgt", me_tgt, n_tgt), ("src", me_src, n_src)):
        for k in range(1, n):
            pl.semaphore_signal(barrier, inc=1, device_id={axis: lax.rem(me + k, n)}, device_id_type=MESH)

    fetches = []
    for i, (mass, me, n) in enumerate(((x_mass, me_tgt, n_tgt), (y_mass, me_src, n_src))):
        rows = 2 * clusters // n
        fetch = pltpu.make_async_copy(
            mass.at[pl.ds(pl.multiple_of(me * rows, rows), rows)], masses.at[i], local.at[i])
        fetch.start()
        fetches.append(fetch)
    slot_m[slots] = jnp.full((SUB, TILE), EMPTY, jnp.float32)
    slot_s[slots] = jnp.zeros((SUB, TILE), jnp.float32)
    slot_n[slots] = jnp.zeros((features, TILE), jnp.float32)
    slot_d[pl.ds(slots, SUB), :] = jnp.zeros((SUB, TILE), jnp.float32)

    def entry(which, p):
        return table[which * slots + p]

    def scaled(cells, ref):
        return cells * jnp.bfloat16(4.0) if ref is xs else cells

    def sweep(kind, first, sub_cells, lane_cells, sub_pot, lane_pot):
        def tile(p, carry):
            a, b, keep = entry(first, p), entry(first + 1, p), entry(first + 2, p)
            sub, lane = sub_cells[a], lane_cells[b]
            left = jnp.concatenate([scaled(sub, sub_cells), aux_rows(cluster_row(sub_pot, a), 0, 3)], axis=0)
            right = jnp.concatenate([scaled(lane, lane_cells), aux_rows(cluster_row(lane_pot, b), 3, 0)], axis=0)
            score = lax.dot_general(left, right, (((0,), (0,)), ((), ())), preferred_element_type=jnp.float32)
            hold = keep.astype(jnp.float32)
            if kind == "max":
                score = score.reshape(CHUNKS, TILE // SUB // CHUNKS, SUB, TILE)
                best = [jnp.max(score[q], axis=0) for q in range(CHUNKS)]
                old = carry[0] * hold + (1.0 - hold) * EMPTY
                new = functools.reduce(jnp.maximum, best, old)
                total = carry[1] * hold * jnp.exp(old - new)
                for q in range(CHUNKS):
                    total = total + jnp.sum(jnp.exp(score[q] - best[q][None]), axis=0) * jnp.exp(best[q] - new)
                slot_m[p] = new
                slot_s[p] = total
                return new, total
            weight = jnp.exp(score)
            if kind == "sum":
                total = carry[0] * hold + jnp.sum(weight.reshape(TILE // SUB, SUB, TILE), axis=0)
                slot_s[p] = total
                return (total,)
            high = weight.astype(jnp.bfloat16)
            low = (weight - high.astype(jnp.float32)).astype(jnp.bfloat16)
            ones = jnp.where(lax.broadcasted_iota(jnp.int32, (AUX, TILE), 0) == 0, 1.0, 0.0).astype(jnp.bfloat16)
            cells = jnp.concatenate([sub, ones], axis=0)
            moved = jnp.dot(cells, high, preferred_element_type=jnp.float32)
            moved = moved + jnp.dot(cells, low, preferred_element_type=jnp.float32)
            total = carry[0] * hold + moved[:features]
            weights = carry[1] * hold + moved[features:features + 1]
            slot_n[p] = total
            slot_d[pl.ds(p, 1), :] = weights
            return total, weights

        def group(g, carry):
            for r in range(step):
                carry = tile(g * step + r, carry)
            return carry

        empty = jnp.zeros((SUB, TILE), jnp.float32)
        if kind == "max":
            start = (empty + EMPTY, empty)
        elif kind == "sum":
            start = (empty,)
        else:
            start = (jnp.zeros((features, TILE), jnp.float32), jnp.zeros((1, TILE), jnp.float32))
        lax.fori_loop(0, slots // step, group, start)

    def reduce(kind, which, axis, me, n, last, old, new, meanwhile):
        part, held = parts.at[which], helds.at[which]
        per = clusters // n
        lanes = lax.broadcasted_iota(jnp.int32, (1, TILE), 1)

        def shard(peer):
            return pl.ds(pl.multiple_of(peer * per, per), per)

        def finish(peer):
            rows = []
            for r in range(per):
                at = entry(last, peer * per + r)
                if kind == "max":
                    best = jnp.max(slot_m[at], axis=0, keepdims=True)
                    row = jnp.sum(slot_s[at] * jnp.exp(slot_m[at] - best), axis=0, keepdims=True)
                    rows.append(best + jnp.log(jnp.where(row > 0.0, row, 1.0)))
                else:
                    rows.append(jnp.sum(slot_s[at], axis=0, keepdims=True))
            part[shard(peer), :] = jnp.concatenate(rows, axis=0)

        def copy(j, phase):
            k = far_offset(axis, j, n)
            peer = lax.rem(me + k, n)
            mine = shard(me)
            src_ref, dst_ref = (part.at[shard(peer)], held.at[k]) if phase == 0 else (new.at[mine], new.at[mine])
            return pltpu.make_async_remote_copy(
                src_ref=src_ref, dst_ref=dst_ref,
                send_sem=sems[2 * phase].at[which, k], recv_sem=sems[2 * phase + 1].at[which, k],
                device_id={axis: peer}, device_id_type=MESH)

        if which == 0:
            pl.semaphore_wait(barrier, n_src + n_tgt - 2)

        @pl.loop(0, n - 1)
        def _(j):
            finish(lax.rem(me + far_offset(axis, j, n), n))
            copy(j, 0).start()

        finish(me)
        meanwhile()
        if which < 2:
            fetches[which].wait()
        mass = masses.at[which % 2]
        count = (SRC_COUNT, TGT_COUNT)[which % 2]
        rows = []
        for r in range(per):
            rows.append(jnp.where(lanes < entry(count, me * per + r), jnp.log(halves_row(mass, r)), EMPTY))
        logmass = jnp.concatenate(rows, axis=0)

        @pl.loop(0, n - 1)
        def _(j):
            copy(j, 0).wait_recv()

        mine = shard(me)
        own = part[mine, :]
        if kind == "max":
            best = own
            for k in range(1, n):
                best = jnp.maximum(best, held[k])
            total = jnp.exp(own - best)
            for k in range(1, n):
                total = total + jnp.exp(held[k] - best)
            lse = best + jnp.log(total)
        else:
            total = own
            for k in range(1, n):
                total = total + held[k]
            lse = jnp.log(jnp.where(total > 0.0, total, 1.0))
        new[mine, :] = jnp.where(logmass > 0.5 * EMPTY, old[mine, :] + logmass - lse, EMPTY)

        @pl.loop(0, n - 1)
        def _(j):
            copy(j, 1).start()

        @pl.loop(0, n - 1)
        def _(j):
            copy(j, 0).wait_send()

        @pl.loop(0, n - 1)
        def _(j):
            copy(j, 1).wait()

    lane = lax.broadcasted_iota(jnp.int32, (1, TILE), 1)
    u0[...] = jnp.zeros(u0.shape, jnp.float32)

    @pl.loop(0, clusters // SUB)
    def _(g):
        rows = []
        for r in range(SUB):
            c = g * SUB + r
            rows.append(jnp.where(lane < entry(TGT_COUNT, c), -2.0 * squared_norm(ys[c]), EMPTY))
        v0[pl.ds(pl.multiple_of(g * SUB, SUB), SUB), :] = jnp.concatenate(rows, axis=0)

    def norms(part):
        groups = clusters // SUB // 2

        @pl.loop(part * groups, part * groups + groups)
        def _(g):
            for r in range(SUB):
                c = g * SUB + r
                put_halves(x_norm_out, c, squared_norm(xs[c]))
                put_halves(y_norm_out, c, -0.5 * cluster_row(v0, c))

    def nothing():
        pass

    def write_u():
        @pl.loop(0, clusters // SUB)
        def _(g):
            for r in range(SUB):
                put_halves(u_out, g * SUB + r, cluster_row(u2, g * SUB + r))

    sweep("max", ROW_SUB, ys, xs, v0, u0)
    reduce("max", 0, "tgt", me_tgt, n_tgt, ROW_LAST, u0, u1, lambda: norms(0))
    sweep("max", COL_SUB, xs, ys, u1, v0)
    reduce("max", 1, "src", me_src, n_src, COL_LAST, v0, v1, lambda: norms(1))
    sweep("sum", ROW_SUB, ys, xs, v1, u1)
    reduce("sum", 2, "tgt", me_tgt, n_tgt, ROW_LAST, u1, u2, nothing)
    sweep("sum", COL_SUB, xs, ys, u2, v1)
    reduce("sum", 3, "src", me_src, n_src, COL_LAST, v1, v2, write_u)
    sweep("map", ROW_SUB, ys, xs, v2, u2)

    n, nz = n_tgt, n_tgt // NY
    z, y = me_tgt // NY, lax.rem(me_tgt, NY)
    other = NY - 1 - y
    sides = (other, y)
    per = out.shape[1] // TILE
    half = per // 2
    sign = (1, -1)
    far = nz // 2
    hops = ((far, nz - 1 - far), (nz - 1 - far, far))
    partner = z * NY + other

    def toward(d):
        return lax.rem(z + sign[d] + nz, nz) * NY + y

    def block(g, d, hop):
        return lax.rem(z + sign[d] * (hops[g][d] - hop) + nz, nz)

    def own(at, side, g, c):
        return slot_n[entry(ROW_LAST, (at * NY + side) * per + g * half + c)]

    def copy(src, dst, sem, k, peer):
        made = pltpu.make_async_remote_copy(
            src_ref=src, dst_ref=dst, send_sem=sems[2 * sem].at[k], recv_sem=sems[2 * sem + 1].at[k],
            device_id={"tgt": peer}, device_id_type=MESH)
        made.start()
        return made

    def encode(ref, values):
        exponents = []
        for c in range(half):
            value = values(c)
            largest = jnp.max(jnp.abs(value), axis=0, keepdims=True)
            exponent = jnp.ceil(jnp.log2(jnp.maximum(largest, 1e-30)))
            code = jnp.floor(value * (jnp.exp2(-exponent) * CODE) + 0.5)
            ref[c * features:(c + 1) * features, :] = code.astype(jnp.int32).astype(jnp.int16)
            exponents.append(exponent)
        exponents.append(jnp.zeros((AUX - half, TILE), jnp.float32))
        block = jnp.concatenate(exponents, axis=0)
        ref[half * features:half * features + AUX, :] = block.astype(jnp.int32).astype(jnp.int16)

    def decoder(ref):
        exponents = ref[half * features:half * features + AUX, :].astype(jnp.int32).astype(jnp.float32)
        scale = jnp.exp2(exponents) * (1.0 / CODE)
        return lambda c: (
            ref[c * features:(c + 1) * features, :].astype(jnp.int32).astype(jnp.float32) * scale[c:c + 1])

    pieces = [(d, hop) for hop in range(far) for d in range(2) if hop < hops[1][d]]
    over_y = {}
    over_a = {}
    over_b = {}

    def send_piece(i, at):
        encode(send_y.at[i], lambda c: own(at, other, 1, c))
        over_y[i] = copy(send_y.at[i], first_y.at[i], 2, i, partner)

    for i in range(2):
        d, hop = pieces[i]
        send_piece(i, block(1, d, hop))
        for s in range(NY):
            encode(send_a.at[i, s], lambda c: own(block(0, i, 0), sides[s], 0, c))
            over_a[i, s, 0] = copy(send_a.at[i, s], ring_a.at[i, 0, s], 3, (i * NY + s) * far, toward(i))
    for i in range(2, nz - 1):
        d, hop = pieces[i]
        send_piece(i, block(1, d, hop))
    send_piece(nz - 1, z)

    def gather(t):
        for c in range(per):
            den[t, pl.ds(c, 1), :] = slot_d[pl.ds(entry(ROW_LAST, t * per + c), 1), :]

    pl.loop(0, n)(gather)
    others = []
    for k in range(1, n):
        peer = lax.rem(me_tgt + k, n)
        others.append(copy(den.at[peer], held_d.at[k], 6, k, peer))

    def step_b(d, hop):
        i = pieces.index((d, hop))
        over_y[i].wait_recv()
        parts_of = [decoder(first_y.at[i])]
        if hop > 0:
            over_b[d, hop - 1].wait_recv()
            parts_of.append(decoder(ring_b.at[d, hop - 1]))
        at = block(1, d, hop)
        encode(first_y.at[i], lambda c: sum((part(c) for part in parts_of), own(at, y, 1, c)))
        over_b[d, hop] = copy(first_y.at[i], ring_b.at[d, hop], 4, d * far + hop, toward(d))

    def step_a(d, s, hop):
        over_a[d, s, hop - 1].wait_recv()
        held = ring_a.at[d, hop - 1, s]
        arrived = decoder(held)
        at = block(0, d, hop)
        encode(held, lambda c: arrived(c) + own(at, sides[s], 0, c))
        over_a[d, s, hop] = copy(held, ring_a.at[d, hop, s], 3, (d * NY + s) * far + hop, toward(d))

    for hop in range(far):
        for d in range(2):
            if hop < hops[1][d]:
                step_b(d, hop)
        for s in range(NY):
            for d in range(2):
                if 0 < hop < hops[0][d]:
                    step_a(d, s, hop)

    def arrived_a(s):
        both = []
        for d in range(2):
            over_a[d, s, hops[0][d] - 1].wait_recv()
            both.append(decoder(ring_a.at[d, hops[0][d] - 1, s]))
        return lambda c: both[0](c) + both[1](c) + own(z, sides[s], 0, c)

    encode(kept, arrived_a(0))
    over_last = copy(kept, last_y, 5, 0, partner)

    @pl.loop(0, clusters // SUB)
    def _(g):
        for r in range(SUB):
            put_halves(v_out, g * SUB + r, cluster_row(v2, g * SUB + r))

    for made in others:
        made.wait_recv()
    total = den[me_tgt]
    for k in range(1, n):
        total = total + held_d[k]
    total = jnp.where(total > 0.0, total, 1.0)

    def put(c, value):
        out[:, c * TILE:(c + 1) * TILE] = value / total[c:c + 1]

    over_y[nz - 1].wait_recv()
    parts_b = [decoder(first_y.at[nz - 1])]
    for d in range(2):
        over_b[d, hops[1][d] - 1].wait_recv()
        parts_b.append(decoder(ring_b.at[d, hops[1][d] - 1]))
    for c in range(half):
        put(half + c, sum((part(c) for part in parts_b), own(z, y, 1, c)))
    mine = arrived_a(1)
    over_last.wait_recv()
    last = decoder(last_y)
    for c in range(half):
        put(c, mine(c) + last(c))
    for made in others + [over_last] + list(over_y.values()) + list(over_a.values()) + list(over_b.values()):
        made.wait_send()


def transport(n_src, n_tgt, slots, table, xs, ys, x_mass, y_mass):
    clusters, features = xs.shape[:2]
    per, nz = clusters // n_tgt, n_tgt // NY
    far = nz // 2
    f32 = jnp.float32
    vmem = pl.BlockSpec(memory_space=pltpu.VMEM)
    smem = pl.BlockSpec(memory_space=pltpu.SMEM)
    hbm = pl.BlockSpec(memory_space=pl.ANY)
    dma = pltpu.SemaphoreType.DMA
    most = max(n_src, n_tgt)
    sems = [dma((4, most))] * 4
    for many in (nz, 2 * NY * far, 2 * far, 1, n_tgt):
        sems += [dma((many,))] * 2
    flat = jax.ShapeDtypeStruct((2 * clusters, TILE // 2), f32)
    row = pltpu.VMEM((clusters, TILE), f32)
    coded = (per // 2 * features + AUX, TILE)

    def codes(*many):
        return pltpu.VMEM(many + coded, jnp.int16)

    scratch = [pltpu.VMEM((2, 2 * clusters // n_tgt, TILE // 2), f32)] + [row] * 6 + [
        pltpu.VMEM((4, clusters, TILE), f32),
        pltpu.VMEM((4, most, clusters // min(n_src, n_tgt), TILE), f32),
        pltpu.VMEM((slots + 1, SUB, TILE), f32),
        pltpu.VMEM((slots + 1, SUB, TILE), f32),
        pltpu.VMEM((slots + 1, features, TILE), f32),
        pltpu.VMEM((slots + SUB, TILE), f32),
        codes(2, NY),
        codes(nz),
        pltpu.VMEM((n_tgt, per, TILE), f32),
        pltpu.VMEM((n_tgt, per, TILE), f32),
        codes(nz),
        codes(2, far, NY),
        codes(2, far),
        codes(),
        codes(),
        dma((2,)),
    ]
    return pl.pallas_call(
        functools.partial(kernel, (n_src, n_tgt, slots)),
        out_shape=(flat,) * 4 + (jax.ShapeDtypeStruct((features, per * TILE), f32),),
        in_specs=[smem, vmem, vmem, hbm, hbm],
        out_specs=(vmem,) * 5,
        scratch_shapes=scratch + sems,
        compiler_params=pltpu.CompilerParams(collective_id=0, has_side_effects=True, vmem_limit_bytes=40 * MIB),
        name="transport",
    )(table, xs, ys, x_mass, y_mass)


def pair_tables(pair_lists, tgt_block, per_block, slots, counts):
    width = pair_lists.shape[1]
    flat = pair_lists.reshape(-1)
    chosen = flat // per_block == tgt_block
    targets = flat % per_block
    sources = jnp.arange(flat.shape[0], dtype=jnp.int32) // width
    places = jnp.arange(slots, dtype=jnp.int32)
    rank = jnp.cumsum(chosen.astype(jnp.int32)) - 1
    matches = (rank[None, :] == places[:, None]) & chosen[None, :]
    row_src = jnp.sum(jnp.where(matches, sources[None, :], 0), axis=1)
    row_tgt = jnp.sum(jnp.where(matches, targets[None, :], 0), axis=1)
    live = places < jnp.sum(chosen.astype(jnp.int32))
    before = (row_tgt[None, :] < row_tgt[:, None]) | (
        (row_tgt[None, :] == row_tgt[:, None]) & (places[None, :] < places[:, None]))
    order = jnp.where(live, jnp.sum((before & live[None, :]).astype(jnp.int32), axis=1), places)
    moves = order[None, :] == places[:, None]
    col_src = jnp.sum(jnp.where(moves, row_src[None, :], 0), axis=1)
    col_tgt = jnp.sum(jnp.where(moves, row_tgt[None, :], 0), axis=1)

    def ends(kept):
        same = jnp.concatenate([jnp.zeros((1,), jnp.int32), (kept[1:] == kept[:-1]).astype(jnp.int32)])
        found = (kept[None, :] == places[:, None]) & live[None, :]
        last = jnp.max(jnp.where(found, places[None, :], -1), axis=1)
        return same, jnp.where(last < 0, slots, last)

    row_keep, row_last = ends(row_src)
    col_keep, col_last = ends(col_tgt)
    return jnp.concatenate([row_tgt, row_src, row_keep, row_last, col_src, col_tgt, col_keep, col_last] + counts)


def shards(source_cells, target_cells, source_mass, target_mass, source_count, target_count, pair_lists):
    n_src, n_tgt = lax.axis_size("src"), lax.axis_size("tgt")
    slots = 2 * pair_lists.size // n_tgt
    table = pair_tables(
        pair_lists, lax.axis_index("tgt"), target_count.shape[0], slots, [source_count, target_count])
    xs, ys = (
        jnp.transpose(cells.reshape(cells.shape[0], -1, TILE), (1, 0, 2)) for cells in (source_cells, target_cells))
    u, v, x_norm, y_norm, mapped = transport(
        n_src, n_tgt, slots, table, xs, ys,
        source_mass.reshape(-1, TILE // 2), target_mass.reshape(-1, TILE // 2))
    source_pot = jnp.where(u > 0.5 * EMPTY, 0.5 * u + x_norm, 0.0)
    target_pot = jnp.where(v > 0.5 * EMPTY, 0.5 * v + y_norm, 0.0)
    return source_pot.reshape(-1), target_pot.reshape(-1), mapped


def solution(mesh):
    return jax.shard_map(
        shards,
        mesh=mesh,
        in_specs=(P(None, "src"), P(None, "tgt"), P("src"), P("tgt"), P("src"), P("tgt"), P("src", None)),
        out_specs=(P("src"), P("tgt"), P(None, ("src", "tgt"))),
        check_vma=False,
    )
```

```python
import functools
import math

import jax
import jax.numpy as jnp
from jax import lax
from jax.experimental import pallas as pl
from jax.experimental.pallas import tpu as pltpu
from jax.sharding import PartitionSpec as P

MESH = pl.DeviceIdType.MESH
EMPTY = -1e30
TILE = 256
SUB = 8
AUX = 16
CHUNKS = 8
CODE = 32752.0
NY = 2
MIB = 1 << 20
ROW_SUB, ROW_LANE, ROW_KEEP, ROW_LAST, COL_SUB, COL_LANE, COL_KEEP, COL_LAST, SRC_COUNT, TGT_COUNT = range(10)


def split3(row):
    high = row.astype(jnp.bfloat16).astype(jnp.float32)
    rest = row - high
    mid = rest.astype(jnp.bfloat16).astype(jnp.float32)
    low = rest - mid
    return high, mid, low


def cluster_row(ref, cluster):
    return ref[pl.ds(cluster, 1), :]


def halves_row(ref, cluster):
    first = ref[pl.ds(2 * cluster, 1), :]
    second = ref[pl.ds(2 * cluster + 1, 1), :]
    return jnp.concatenate([first, second], axis=1)


def put_halves(ref, cluster, row):
    ref[pl.ds(2 * cluster, 1), :] = row[:, :128]
    ref[pl.ds(2 * cluster + 1, 1), :] = row[:, 128:]


def squared_norm(cells):
    wide = cells.astype(jnp.float32)
    return jnp.sum(wide * wide, axis=0, keepdims=True)


def far_offset(axis, j, n):
    if axis == "tgt":
        return n // 2 + (j + 1) // 2 * (1 - 2 * (j % 2))
    i = j // 2
    near = n // 4 + (i + 1) // 2 * (2 * (i % 2) - 1)
    return n - near if j % 2 else near


def aux_rows(row, offset, other):
    at = lax.broadcasted_iota(jnp.int32, (AUX, TILE), 0)
    high, mid, low = split3(row)
    out = jnp.where((at >= other) & (at < other + 3), 1.0, 0.0)
    out = jnp.where(at == offset, high, out)
    out = jnp.where(at == offset + 1, mid, out)
    out = jnp.where(at == offset + 2, low, out)
    return out.astype(jnp.bfloat16)


def kernel(
    sizes, table, xs, ys, x_mass, y_mass, u_out, v_out, x_norm_out, y_norm_out, out,
    masses, u0, v0, u1, v1, u2, v2, parts, helds, slot_m, slot_s, slot_n, slot_d, send_a, send_y, den, held_d,
    first_y, ring_a, ring_b, last_y, kept, local, *sems,
):
    n_src, n_tgt, slots = sizes
    step = math.gcd(slots, 32)
    clusters, features = xs.shape[:2]
    me_src, me_tgt = lax.axis_index("src"), lax.axis_index("tgt")
    barrier = pltpu.get_barrier_semaphore()
    for axis, me, n in (("tgt", me_tgt, n_tgt), ("src", me_src, n_src)):
        for k in range(1, n):
            pl.semaphore_signal(barrier, inc=1, device_id={axis: lax.rem(me + k, n)}, device_id_type=MESH)

    fetches = []
    for i, (mass, me, n) in enumerate(((x_mass, me_tgt, n_tgt), (y_mass, me_src, n_src))):
        rows = 2 * clusters // n
        fetch = pltpu.make_async_copy(
            mass.at[pl.ds(pl.multiple_of(me * rows, rows), rows)], masses.at[i], local.at[i])
        fetch.start()
        fetches.append(fetch)
    slot_m[slots] = jnp.full((SUB, TILE), EMPTY, jnp.float32)
    slot_s[slots] = jnp.zeros((SUB, TILE), jnp.float32)
    slot_n[slots] = jnp.zeros((features, TILE), jnp.float32)
    slot_d[pl.ds(slots, SUB), :] = jnp.zeros((SUB, TILE), jnp.float32)

    def entry(which, p):
        return table[which * slots + p]

    def scaled(cells, ref):
        return cells * jnp.bfloat16(4.0) if ref is xs else cells

    def sweep(kind, first, sub_cells, lane_cells, sub_pot, lane_pot):
        def tile(p, carry):
            a, b, keep = entry(first, p), entry(first + 1, p), entry(first + 2, p)
            sub, lane = sub_cells[a], lane_cells[b]
            left = jnp.concatenate([scaled(sub, sub_cells), aux_rows(cluster_row(sub_pot, a), 0, 3)], axis=0)
            right = jnp.concatenate([scaled(lane, lane_cells), aux_rows(cluster_row(lane_pot, b), 3, 0)], axis=0)
            score = lax.dot_general(left, right, (((0,), (0,)), ((), ())), preferred_element_type=jnp.float32)
            hold = keep.astype(jnp.float32)
            if kind == "max":
                score = score.reshape(CHUNKS, TILE // SUB // CHUNKS, SUB, TILE)
                best = [jnp.max(score[q], axis=0) for q in range(CHUNKS)]
                old = carry[0] * hold + (1.0 - hold) * EMPTY
                new = functools.reduce(jnp.maximum, best, old)
                total = carry[1] * hold * jnp.exp(old - new)
                for q in range(CHUNKS):
                    total = total + jnp.sum(jnp.exp(score[q] - best[q][None]), axis=0) * jnp.exp(best[q] - new)
                slot_m[p] = new
                slot_s[p] = total
                return new, total
            weight = jnp.exp(score)
            if kind == "sum":
                total = carry[0] * hold + jnp.sum(weight.reshape(TILE // SUB, SUB, TILE), axis=0)
                slot_s[p] = total
                return (total,)
            high = weight.astype(jnp.bfloat16)
            low = (weight - high.astype(jnp.float32)).astype(jnp.bfloat16)
            ones = jnp.where(lax.broadcasted_iota(jnp.int32, (AUX, TILE), 0) == 0, 1.0, 0.0).astype(jnp.bfloat16)
            cells = jnp.concatenate([sub, ones], axis=0)
            moved = jnp.dot(cells, high, preferred_element_type=jnp.float32)
            moved = moved + jnp.dot(cells, low, preferred_element_type=jnp.float32)
            total = carry[0] * hold + moved[:features]
            weights = carry[1] * hold + moved[features:features + 1]
            slot_n[p] = total
            slot_d[pl.ds(p, 1), :] = weights
            return total, weights

        def group(g, carry):
            for r in range(step):
                carry = tile(g * step + r, carry)
            return carry

        empty = jnp.zeros((SUB, TILE), jnp.float32)
        if kind == "max":
            start = (empty + EMPTY, empty)
        elif kind == "sum":
            start = (empty,)
        else:
            start = (jnp.zeros((features, TILE), jnp.float32), jnp.zeros((1, TILE), jnp.float32))
        lax.fori_loop(0, slots // step, group, start)

    def reduce(kind, which, axis, me, n, last, old, new, meanwhile):
        part, held = parts.at[which], helds.at[which]
        per = clusters // n
        lanes = lax.broadcasted_iota(jnp.int32, (1, TILE), 1)

        def shard(peer):
            return pl.ds(pl.multiple_of(peer * per, per), per)

        def finish(peer):
            rows = []
            for r in range(per):
                at = entry(last, peer * per + r)
                if kind == "max":
                    best = jnp.max(slot_m[at], axis=0, keepdims=True)
                    row = jnp.sum(slot_s[at] * jnp.exp(slot_m[at] - best), axis=0, keepdims=True)
                    rows.append(best + jnp.log(jnp.where(row > 0.0, row, 1.0)))
                else:
                    rows.append(jnp.sum(slot_s[at], axis=0, keepdims=True))
            part[shard(peer), :] = jnp.concatenate(rows, axis=0)

        def copy(j, phase):
            k = far_offset(axis, j, n)
            peer = lax.rem(me + k, n)
            mine = shard(me)
            src_ref, dst_ref = (part.at[shard(peer)], held.at[k]) if phase == 0 else (new.at[mine], new.at[mine])
            return pltpu.make_async_remote_copy(
                src_ref=src_ref, dst_ref=dst_ref,
                send_sem=sems[2 * phase].at[which, k], recv_sem=sems[2 * phase + 1].at[which, k],
                device_id={axis: peer}, device_id_type=MESH)

        if which == 0:
            pl.semaphore_wait(barrier, n_src + n_tgt - 2)

        made = []
        for j in range(n - 1):
            finish(lax.rem(me + far_offset(axis, j, n), n))
            made.append(copy(j, 0))
            made[-1].start()

        finish(me)
        meanwhile()
        if which < 2:
            fetches[which].wait()
        mass = masses.at[which % 2]
        count = (SRC_COUNT, TGT_COUNT)[which % 2]
        rows = []
        for r in range(per):
            rows.append(jnp.where(lanes < entry(count, me * per + r), jnp.log(halves_row(mass, r)), EMPTY))
        logmass = jnp.concatenate(rows, axis=0)

        for each in made:
            each.wait_recv()

        mine = shard(me)
        own = part[mine, :]
        if kind == "max":
            best = own
            for k in range(1, n):
                best = jnp.maximum(best, held[k])
            total = jnp.exp(own - best)
            for k in range(1, n):
                total = total + jnp.exp(held[k] - best)
            lse = best + jnp.log(total)
        else:
            total = own
            for k in range(1, n):
                total = total + held[k]
            lse = jnp.log(jnp.where(total > 0.0, total, 1.0))
        new[mine, :] = jnp.where(logmass > 0.5 * EMPTY, old[mine, :] + logmass - lse, EMPTY)

        sent = [copy(j, 1) for j in range(n - 1)]
        for each in sent:
            each.start()
        for each in made:
            each.wait_send()
        for each in sent:
            each.wait()

    lane = lax.broadcasted_iota(jnp.int32, (1, TILE), 1)
    u0[...] = jnp.zeros(u0.shape, jnp.float32)

    @pl.loop(0, clusters // SUB)
    def _(g):
        rows = []
        for r in range(SUB):
            c = g * SUB + r
            rows.append(jnp.where(lane < entry(TGT_COUNT, c), -2.0 * squared_norm(ys[c]), EMPTY))
        v0[pl.ds(pl.multiple_of(g * SUB, SUB), SUB), :] = jnp.concatenate(rows, axis=0)

    def norms(part):
        groups = clusters // SUB // 2

        @pl.loop(part * groups, part * groups + groups)
        def _(g):
            for r in range(SUB):
                c = g * SUB + r
                put_halves(x_norm_out, c, squared_norm(xs[c]))
                put_halves(y_norm_out, c, -0.5 * cluster_row(v0, c))

    def nothing():
        pass

    def write_u():
        @pl.loop(0, clusters // SUB)
        def _(g):
            for r in range(SUB):
                put_halves(u_out, g * SUB + r, cluster_row(u2, g * SUB + r))

    sweep("max", ROW_SUB, ys, xs, v0, u0)
    reduce("max", 0, "tgt", me_tgt, n_tgt, ROW_LAST, u0, u1, lambda: norms(0))
    sweep("max", COL_SUB, xs, ys, u1, v0)
    reduce("max", 1, "src", me_src, n_src, COL_LAST, v0, v1, lambda: norms(1))
    sweep("sum", ROW_SUB, ys, xs, v1, u1)
    reduce("sum", 2, "tgt", me_tgt, n_tgt, ROW_LAST, u1, u2, nothing)
    sweep("sum", COL_SUB, xs, ys, u2, v1)
    reduce("sum", 3, "src", me_src, n_src, COL_LAST, v1, v2, write_u)
    sweep("map", ROW_SUB, ys, xs, v2, u2)

    n, nz = n_tgt, n_tgt // NY
    z, y = me_tgt // NY, lax.rem(me_tgt, NY)
    other = NY - 1 - y
    sides = (other, y)
    per = out.shape[1] // TILE
    half = per // 2
    sign = (1, -1)
    far = nz // 2
    hops = ((far, nz - 1 - far), (nz - 1 - far, far))
    partner = z * NY + other

    def toward(d):
        return lax.rem(z + sign[d] + nz, nz) * NY + y

    def block(g, d, hop):
        return lax.rem(z + sign[d] * (hops[g][d] - hop) + nz, nz)

    def own(at, side, g, c):
        return slot_n[entry(ROW_LAST, (at * NY + side) * per + g * half + c)]

    def copy(src, dst, sem, k, peer):
        made = pltpu.make_async_remote_copy(
            src_ref=src, dst_ref=dst, send_sem=sems[2 * sem].at[k], recv_sem=sems[2 * sem + 1].at[k],
            device_id={"tgt": peer}, device_id_type=MESH)
        made.start()
        return made

    def encode(ref, values):
        exponents = []
        for c in range(half):
            value = values(c)
            largest = jnp.max(jnp.abs(value), axis=0, keepdims=True)
            exponent = jnp.ceil(jnp.log2(jnp.maximum(largest, 1e-30)))
            code = jnp.floor(value * (jnp.exp2(-exponent) * CODE) + 0.5)
            ref[c * features:(c + 1) * features, :] = code.astype(jnp.int32).astype(jnp.int16)
            exponents.append(exponent)
        exponents.append(jnp.zeros((AUX - half, TILE), jnp.float32))
        block = jnp.concatenate(exponents, axis=0)
        ref[half * features:half * features + AUX, :] = block.astype(jnp.int32).astype(jnp.int16)

    def decoder(ref):
        exponents = ref[half * features:half * features + AUX, :].astype(jnp.int32).astype(jnp.float32)
        scale = jnp.exp2(exponents) * (1.0 / CODE)
        return lambda c: (
            ref[c * features:(c + 1) * features, :].astype(jnp.int32).astype(jnp.float32) * scale[c:c + 1])

    pieces = [(d, hop) for hop in range(far) for d in range(2) if hop < hops[1][d]]
    over_y = {}
    over_a = {}
    over_b = {}

    def send_piece(i, at):
        encode(send_y.at[i], lambda c: own(at, other, 1, c))
        over_y[i] = copy(send_y.at[i], first_y.at[i], 2, i, partner)

    for i in range(2):
        d, hop = pieces[i]
        send_piece(i, block(1, d, hop))
        for s in range(NY):
            encode(send_a.at[i, s], lambda c: own(block(0, i, 0), sides[s], 0, c))
            over_a[i, s, 0] = copy(send_a.at[i, s], ring_a.at[i, 0, s], 3, (i * NY + s) * far, toward(i))
    for i in range(2, nz - 1):
        d, hop = pieces[i]
        send_piece(i, block(1, d, hop))
    send_piece(nz - 1, z)

    def gather(t):
        for c in range(per):
            den[t, pl.ds(c, 1), :] = slot_d[pl.ds(entry(ROW_LAST, t * per + c), 1), :]

    pl.loop(0, n)(gather)
    others = []
    for k in range(1, n):
        peer = lax.rem(me_tgt + k, n)
        others.append(copy(den.at[peer], held_d.at[k], 6, k, peer))

    def step_b(d, hop):
        i = pieces.index((d, hop))
        over_y[i].wait_recv()
        parts_of = [decoder(first_y.at[i])]
        if hop > 0:
            over_b[d, hop - 1].wait_recv()
            parts_of.append(decoder(ring_b.at[d, hop - 1]))
        at = block(1, d, hop)
        encode(first_y.at[i], lambda c: sum((part(c) for part in parts_of), own(at, y, 1, c)))
        over_b[d, hop] = copy(first_y.at[i], ring_b.at[d, hop], 4, d * far + hop, toward(d))

    def step_a(d, s, hop):
        over_a[d, s, hop - 1].wait_recv()
        held = ring_a.at[d, hop - 1, s]
        arrived = decoder(held)
        at = block(0, d, hop)
        encode(held, lambda c: arrived(c) + own(at, sides[s], 0, c))
        over_a[d, s, hop] = copy(held, ring_a.at[d, hop, s], 3, (d * NY + s) * far + hop, toward(d))

    for hop in range(far):
        for d in range(2):
            if hop < hops[1][d]:
                step_b(d, hop)
        for s in range(NY):
            for d in range(2):
                if 0 < hop < hops[0][d]:
                    step_a(d, s, hop)

    def arrived_a(s):
        both = []
        for d in range(2):
            over_a[d, s, hops[0][d] - 1].wait_recv()
            both.append(decoder(ring_a.at[d, hops[0][d] - 1, s]))
        return lambda c: both[0](c) + both[1](c) + own(z, sides[s], 0, c)

    encode(kept, arrived_a(0))
    over_last = copy(kept, last_y, 5, 0, partner)

    @pl.loop(0, clusters // SUB)
    def _(g):
        for r in range(SUB):
            put_halves(v_out, g * SUB + r, cluster_row(v2, g * SUB + r))

    for made in others:
        made.wait_recv()
    total = den[me_tgt]
    for k in range(1, n):
        total = total + held_d[k]
    total = jnp.where(total > 0.0, total, 1.0)

    def put(c, value):
        out[:, c * TILE:(c + 1) * TILE] = value / total[c:c + 1]

    over_y[nz - 1].wait_recv()
    parts_b = [decoder(first_y.at[nz - 1])]
    for d in range(2):
        over_b[d, hops[1][d] - 1].wait_recv()
        parts_b.append(decoder(ring_b.at[d, hops[1][d] - 1]))
    for c in range(half):
        put(half + c, sum((part(c) for part in parts_b), own(z, y, 1, c)))
    mine = arrived_a(1)
    over_last.wait_recv()
    last = decoder(last_y)
    for c in range(half):
        put(c, mine(c) + last(c))
    for made in others + [over_last] + list(over_y.values()) + list(over_a.values()) + list(over_b.values()):
        made.wait_send()


def transport(n_src, n_tgt, slots, table, xs, ys, x_mass, y_mass):
    clusters, features = xs.shape[:2]
    per, nz = clusters // n_tgt, n_tgt // NY
    far = nz // 2
    f32 = jnp.float32
    vmem = pl.BlockSpec(memory_space=pltpu.VMEM)
    smem = pl.BlockSpec(memory_space=pltpu.SMEM)
    hbm = pl.BlockSpec(memory_space=pl.ANY)
    dma = pltpu.SemaphoreType.DMA
    most = max(n_src, n_tgt)
    sems = [dma((4, most))] * 4
    for many in (nz, 2 * NY * far, 2 * far, 1, n_tgt):
        sems += [dma((many,))] * 2
    flat = jax.ShapeDtypeStruct((2 * clusters, TILE // 2), f32)
    row = pltpu.VMEM((clusters, TILE), f32)
    coded = (per // 2 * features + AUX, TILE)

    def codes(*many):
        return pltpu.VMEM(many + coded, jnp.int16)

    scratch = [pltpu.VMEM((2, 2 * clusters // n_tgt, TILE // 2), f32)] + [row] * 6 + [
        pltpu.VMEM((4, clusters, TILE), f32),
        pltpu.VMEM((4, most, clusters // min(n_src, n_tgt), TILE), f32),
        pltpu.VMEM((slots + 1, SUB, TILE), f32),
        pltpu.VMEM((slots + 1, SUB, TILE), f32),
        pltpu.VMEM((slots + 1, features, TILE), f32),
        pltpu.VMEM((slots + SUB, TILE), f32),
        codes(2, NY),
        codes(nz),
        pltpu.VMEM((n_tgt, per, TILE), f32),
        pltpu.VMEM((n_tgt, per, TILE), f32),
        codes(nz),
        codes(2, far, NY),
        codes(2, far),
        codes(),
        codes(),
        dma((2,)),
    ]
    return pl.pallas_call(
        functools.partial(kernel, (n_src, n_tgt, slots)),
        out_shape=(flat,) * 4 + (jax.ShapeDtypeStruct((features, per * TILE), f32),),
        in_specs=[smem, vmem, vmem, hbm, hbm],
        out_specs=(vmem,) * 5,
        scratch_shapes=scratch + sems,
        compiler_params=pltpu.CompilerParams(collective_id=0, has_side_effects=True, vmem_limit_bytes=40 * MIB),
        name="transport",
    )(table, xs, ys, x_mass, y_mass)


def pair_tables(pair_lists, tgt_block, per_block, slots, counts):
    lists = pair_lists.T
    chosen = lists // per_block == tgt_block
    targets = lists % per_block
    sources = lax.broadcasted_iota(jnp.int32, lists.shape, 1)
    places = jnp.arange(slots, dtype=jnp.int32)

    def counted(which):
        upto = jnp.sum((chosen[None] & (which[None] <= places[:, None, None])).astype(jnp.int32), axis=(1, 2))
        equal = jnp.sum((chosen[None] & (which[None] == places[:, None, None])).astype(jnp.int32), axis=(1, 2))
        return upto, equal

    def kept(upto, equal):
        cluster = jnp.sum((upto[None, :] <= places[:, None]).astype(jnp.int32), axis=1)
        before = jnp.sum((upto[None, :] < places[:, None]).astype(jnp.int32), axis=1)
        cluster = jnp.minimum(cluster, per_block - 1)
        return cluster, (cluster == before).astype(jnp.int32), jnp.where(equal > 0, upto - 1, slots)

    upto, equal = counted(sources)
    row_src, row_keep, row_last = kept(upto, equal)
    col_upto, col_equal = counted(targets)
    col_tgt, col_keep, col_last = kept(col_upto, col_equal)
    within = jnp.cumsum(chosen.astype(jnp.int32), axis=0)
    rank = jnp.where(chosen, (upto - equal)[None, :] + within - 1, -1)
    row_tgt = jnp.sum(jnp.where(rank[None] == places[:, None, None], targets[None], 0), axis=(1, 2))
    live = places < upto[-1]
    before = (row_tgt[None, :] < row_tgt[:, None]) | (
        (row_tgt[None, :] == row_tgt[:, None]) & (places[None, :] < places[:, None]))
    order = jnp.where(live, jnp.sum((before & live[None, :]).astype(jnp.int32), axis=1), -1)
    col_src = jnp.sum(jnp.where(order[None, :] == places[:, None], row_src[None, :], 0), axis=1)
    return jnp.concatenate([row_tgt, row_src, row_keep, row_last, col_src, col_tgt, col_keep, col_last] + counts)


def shards(source_cells, target_cells, source_mass, target_mass, source_count, target_count, pair_lists):
    n_src, n_tgt = lax.axis_size("src"), lax.axis_size("tgt")
    slots = 2 * pair_lists.size // n_tgt
    table = pair_tables(
        pair_lists, lax.axis_index("tgt"), target_count.shape[0], slots, [source_count, target_count])
    xs, ys = (
        jnp.transpose(cells.reshape(cells.shape[0], -1, TILE), (1, 0, 2)) for cells in (source_cells, target_cells))
    u, v, x_norm, y_norm, mapped = transport(
        n_src, n_tgt, slots, table, xs, ys,
        source_mass.reshape(-1, TILE // 2), target_mass.reshape(-1, TILE // 2))
    source_pot = jnp.where(u > 0.5 * EMPTY, 0.5 * u + x_norm, 0.0)
    target_pot = jnp.where(v > 0.5 * EMPTY, 0.5 * v + y_norm, 0.0)
    return source_pot.reshape(-1), target_pot.reshape(-1), mapped


def solution(mesh):
    return jax.shard_map(
        shards,
        mesh=mesh,
        in_specs=(P(None, "src"), P(None, "tgt"), P("src"), P("tgt"), P("src"), P("tgt"), P("src", None)),
        out_specs=(P("src"), P("tgt"), P(None, ("src", "tgt"))),
        check_vma=False,
    )
```

```python
import functools
import math

import jax
import jax.numpy as jnp
from jax import lax
from jax.experimental import pallas as pl
from jax.experimental.pallas import tpu as pltpu
from jax.sharding import PartitionSpec as P

MESH = pl.DeviceIdType.MESH
EMPTY = -1e30
TILE = 256
SUB = 8
AUX = 16
CHUNKS = 8
CODE = 32752.0
NY = 2
MIB = 1 << 20
ROW_SUB, ROW_LANE, ROW_KEEP, ROW_LAST, COL_SUB, COL_LANE, COL_KEEP, COL_LAST, SRC_COUNT, TGT_COUNT = range(10)


def split3(row):
    high = row.astype(jnp.bfloat16).astype(jnp.float32)
    rest = row - high
    mid = rest.astype(jnp.bfloat16).astype(jnp.float32)
    low = rest - mid
    return high, mid, low


def cluster_row(ref, cluster):
    return ref[pl.ds(cluster, 1), :]


def halves_row(ref, cluster):
    first = ref[pl.ds(2 * cluster, 1), :]
    second = ref[pl.ds(2 * cluster + 1, 1), :]
    return jnp.concatenate([first, second], axis=1)


def put_halves(ref, cluster, row):
    ref[pl.ds(2 * cluster, 1), :] = row[:, :128]
    ref[pl.ds(2 * cluster + 1, 1), :] = row[:, 128:]


def squared_norm(cells):
    wide = cells.astype(jnp.float32)
    return jnp.sum(wide * wide, axis=0, keepdims=True)


def far_offset(axis, j, n):
    if axis == "tgt":
        return n // 2 + lax.div(j + 1, 2) * (1 - 2 * lax.rem(j, 2))
    i = lax.div(j, 2)
    near = n // 4 + lax.div(i + 1, 2) * (2 * lax.rem(i, 2) - 1)
    return near + lax.rem(j, 2) * (n - 2 * near)


def aux_rows(row, offset, other):
    at = lax.broadcasted_iota(jnp.int32, (AUX, TILE), 0)
    high, mid, low = split3(row)
    out = jnp.where((at >= other) & (at < other + 3), 1.0, 0.0)
    out = jnp.where(at == offset, high, out)
    out = jnp.where(at == offset + 1, mid, out)
    out = jnp.where(at == offset + 2, low, out)
    return out.astype(jnp.bfloat16)


def kernel(
    sizes, table, xs, ys, x_mass, y_mass, u_out, v_out, x_norm_out, y_norm_out, out,
    masses, u0, v0, u1, v1, u2, v2, parts, helds, slot_m, slot_s, slot_n, slot_d, send_a, send_y,
    first_y, ring_a, ring_b, last_y, kept, local, *sems,
):
    n_src, n_tgt, slots = sizes
    step = math.gcd(slots, 32)
    clusters, features = xs.shape[:2]
    me_src, me_tgt = lax.axis_index("src"), lax.axis_index("tgt")
    barrier = pltpu.get_barrier_semaphore()
    for axis, me, n in (("tgt", me_tgt, n_tgt), ("src", me_src, n_src)):
        for k in range(1, n):
            pl.semaphore_signal(barrier, inc=1, device_id={axis: lax.rem(me + k, n)}, device_id_type=MESH)

    fetches = []
    for i, (mass, me, n) in enumerate(((x_mass, me_tgt, n_tgt), (y_mass, me_src, n_src))):
        rows = 2 * clusters // n
        fetch = pltpu.make_async_copy(
            mass.at[pl.ds(pl.multiple_of(me * rows, rows), rows)], masses.at[i], local.at[i])
        fetch.start()
        fetches.append(fetch)
    slot_m[slots] = jnp.full((SUB, TILE), EMPTY, jnp.float32)
    slot_s[slots] = jnp.zeros((SUB, TILE), jnp.float32)
    slot_n[slots] = jnp.zeros((features, TILE), jnp.float32)
    slot_d[pl.ds(slots, SUB), :] = jnp.zeros((SUB, TILE), jnp.float32)

    def entry(which, p):
        return table[which * slots + p]

    def scaled(cells, ref):
        return cells * jnp.bfloat16(4.0) if ref is xs else cells

    def sweep(kind, first, sub_cells, lane_cells, sub_pot, lane_pot):
        def tile(p, carry):
            a, b, keep = entry(first, p), entry(first + 1, p), entry(first + 2, p)
            sub, lane = sub_cells[a], lane_cells[b]
            left = jnp.concatenate([scaled(sub, sub_cells), aux_rows(cluster_row(sub_pot, a), 0, 3)], axis=0)
            right = jnp.concatenate([scaled(lane, lane_cells), aux_rows(cluster_row(lane_pot, b), 3, 0)], axis=0)
            score = lax.dot_general(left, right, (((0,), (0,)), ((), ())), preferred_element_type=jnp.float32)
            hold = keep.astype(jnp.float32)
            if kind == "max":
                score = score.reshape(CHUNKS, TILE // SUB // CHUNKS, SUB, TILE)
                best = [jnp.max(score[q], axis=0) for q in range(CHUNKS)]
                old = carry[0] * hold + (1.0 - hold) * EMPTY
                new = functools.reduce(jnp.maximum, best, old)
                total = carry[1] * hold * jnp.exp(old - new)
                for q in range(CHUNKS):
                    total = total + jnp.sum(jnp.exp(score[q] - best[q][None]), axis=0) * jnp.exp(best[q] - new)
                slot_m[p] = new
                slot_s[p] = total
                return new, total
            weight = jnp.exp(score)
            if kind == "sum":
                total = carry[0] * hold + jnp.sum(weight.reshape(TILE // SUB, SUB, TILE), axis=0)
                slot_s[p] = total
                return (total,)
            high = weight.astype(jnp.bfloat16)
            low = (weight - high.astype(jnp.float32)).astype(jnp.bfloat16)
            ones = jnp.where(lax.broadcasted_iota(jnp.int32, (AUX, TILE), 0) == 0, 1.0, 0.0).astype(jnp.bfloat16)
            cells = jnp.concatenate([sub, ones], axis=0)
            moved = jnp.dot(cells, high, preferred_element_type=jnp.float32)
            moved = moved + jnp.dot(cells, low, preferred_element_type=jnp.float32)
            total = carry[0] * hold + moved[:features]
            weights = carry[1] * hold + moved[features:features + 1]
            slot_n[p] = total
            slot_d[pl.ds(p, 1), :] = weights
            return total, weights

        def group(g, carry):
            for r in range(step):
                carry = tile(g * step + r, carry)
            return carry

        empty = jnp.zeros((SUB, TILE), jnp.float32)
        if kind == "max":
            start = (empty + EMPTY, empty)
        elif kind == "sum":
            start = (empty,)
        else:
            start = (jnp.zeros((features, TILE), jnp.float32), jnp.zeros((1, TILE), jnp.float32))
        lax.fori_loop(0, slots // step, group, start)

    def reduce(kind, which, axis, me, n, last, old, new, meanwhile):
        part, held = parts.at[which], helds.at[which]
        per = clusters // n
        lanes = lax.broadcasted_iota(jnp.int32, (1, TILE), 1)

        def shard(peer):
            return pl.ds(pl.multiple_of(peer * per, per), per)

        def finish(peer):
            rows = []
            for r in range(per):
                at = entry(last, peer * per + r)
                if kind == "max":
                    best = jnp.max(slot_m[at], axis=0, keepdims=True)
                    row = jnp.sum(slot_s[at] * jnp.exp(slot_m[at] - best), axis=0, keepdims=True)
                    rows.append(best + jnp.log(jnp.where(row > 0.0, row, 1.0)))
                else:
                    rows.append(jnp.sum(slot_s[at], axis=0, keepdims=True))
            part[shard(peer), :] = jnp.concatenate(rows, axis=0)

        def copy(j, phase):
            k = far_offset(axis, j, n)
            peer = lax.rem(me + k, n)
            mine = shard(me)
            src_ref, dst_ref = (part.at[shard(peer)], held.at[k]) if phase == 0 else (new.at[mine], new.at[mine])
            return pltpu.make_async_remote_copy(
                src_ref=src_ref, dst_ref=dst_ref,
                send_sem=sems[2 * phase].at[which, k], recv_sem=sems[2 * phase + 1].at[which, k],
                device_id={axis: peer}, device_id_type=MESH)

        if which == 0:
            pl.semaphore_wait(barrier, n_src + n_tgt - 2)

        @pl.loop(0, n - 1)
        def _(j):
            finish(lax.rem(me + far_offset(axis, j, n), n))
            copy(j, 0).start()

        finish(me)
        meanwhile()
        if which < 2:
            fetches[which].wait()
        mass = masses.at[which % 2]
        count = (SRC_COUNT, TGT_COUNT)[which % 2]
        rows = []
        for r in range(per):
            rows.append(jnp.where(lanes < entry(count, me * per + r), jnp.log(halves_row(mass, r)), EMPTY))
        logmass = jnp.concatenate(rows, axis=0)

        @pl.loop(0, n - 1)
        def _(j):
            copy(j, 0).wait_recv()

        mine = shard(me)
        own = part[mine, :]
        if kind == "max":
            best = own
            for k in range(1, n):
                best = jnp.maximum(best, held[k])
            total = jnp.exp(own - best)
            for k in range(1, n):
                total = total + jnp.exp(held[k] - best)
            lse = best + jnp.log(total)
        else:
            total = own
            for k in range(1, n):
                total = total + held[k]
            lse = jnp.log(jnp.where(total > 0.0, total, 1.0))
        new[mine, :] = jnp.where(logmass > 0.5 * EMPTY, old[mine, :] + logmass - lse, EMPTY)

        @pl.loop(0, n - 1)
        def _(j):
            copy(j, 1).start()

        @pl.loop(0, n - 1)
        def _(j):
            copy(j, 0).wait_send()

        @pl.loop(0, n - 1)
        def _(j):
            copy(j, 1).wait()

    lane = lax.broadcasted_iota(jnp.int32, (1, TILE), 1)
    u0[...] = jnp.zeros(u0.shape, jnp.float32)

    @pl.loop(0, clusters // SUB)
    def _(g):
        rows = []
        for r in range(SUB):
            c = g * SUB + r
            rows.append(jnp.where(lane < entry(TGT_COUNT, c), -2.0 * squared_norm(ys[c]), EMPTY))
        v0[pl.ds(pl.multiple_of(g * SUB, SUB), SUB), :] = jnp.concatenate(rows, axis=0)

    def norms(part):
        groups = clusters // SUB // 2

        @pl.loop(part * groups, part * groups + groups)
        def _(g):
            for r in range(SUB):
                c = g * SUB + r
                put_halves(x_norm_out, c, squared_norm(xs[c]))
                put_halves(y_norm_out, c, -0.5 * cluster_row(v0, c))

    def nothing():
        pass

    def write_u():
        @pl.loop(0, clusters // SUB)
        def _(g):
            for r in range(SUB):
                put_halves(u_out, g * SUB + r, cluster_row(u2, g * SUB + r))

    sweep("max", ROW_SUB, ys, xs, v0, u0)
    reduce("max", 0, "tgt", me_tgt, n_tgt, ROW_LAST, u0, u1, lambda: norms(0))
    sweep("max", COL_SUB, xs, ys, u1, v0)
    reduce("max", 1, "src", me_src, n_src, COL_LAST, v0, v1, lambda: norms(1))
    sweep("sum", ROW_SUB, ys, xs, v1, u1)
    reduce("sum", 2, "tgt", me_tgt, n_tgt, ROW_LAST, u1, u2, nothing)
    sweep("sum", COL_SUB, xs, ys, u2, v1)
    reduce("sum", 3, "src", me_src, n_src, COL_LAST, v1, v2, write_u)
    sweep("map", ROW_SUB, ys, xs, v2, u2)

    n, nz = n_tgt, n_tgt // NY
    z, y = me_tgt // NY, lax.rem(me_tgt, NY)
    other = NY - 1 - y
    sides = (other, y)
    per = out.shape[1] // TILE
    half = per // 2
    sign = (1, -1)
    far = nz // 2
    hops = ((far, nz - 1 - far), (nz - 1 - far, far))
    partner = z * NY + other

    def toward(d):
        return lax.rem(z + sign[d] + nz, nz) * NY + y

    def block(g, d, hop):
        return lax.rem(z + sign[d] * (hops[g][d] - hop) + nz, nz)

    def own(at, side, g, c):
        slot = entry(ROW_LAST, (at * NY + side) * per + g * half + c)
        return slot_n[slot], slot_d[pl.ds(slot, 1), :]

    def plus(*terms):
        return tuple(functools.reduce(jnp.add, term) for term in zip(*terms))

    def copy(src, dst, sem, k, peer):
        made = pltpu.make_async_remote_copy(
            src_ref=src, dst_ref=dst, send_sem=sems[2 * sem].at[k], recv_sem=sems[2 * sem + 1].at[k],
            device_id={"tgt": peer}, device_id_type=MESH)
        made.start()
        return made

    def exponent_of(value):
        return jnp.ceil(jnp.log2(jnp.maximum(value, 1e-30)))

    def coded(value, exponent):
        return jnp.floor(value * (jnp.exp2(-exponent) * CODE) + 0.5)

    def encode(ref, values):
        rows = [[], [], []]
        for c in range(half):
            value, weight = values(c)
            exponent = exponent_of(jnp.max(jnp.abs(value), axis=0, keepdims=True))
            code = coded(value, exponent)
            ref[c * features:(c + 1) * features, :] = code.astype(jnp.int32).astype(jnp.int16)
            at = exponent_of(weight)
            for row, item in zip(rows, (exponent, at, coded(weight, at))):
                row.append(item)
        spare = [jnp.zeros((AUX - 3 * half, TILE), jnp.float32)]
        block = jnp.concatenate(rows[0] + rows[1] + rows[2] + spare, axis=0)
        ref[half * features:half * features + AUX, :] = block.astype(jnp.int32).astype(jnp.int16)

    def decoder(ref):
        block = ref[half * features:half * features + AUX, :].astype(jnp.int32).astype(jnp.float32)
        scale = jnp.exp2(block[:2 * half]) * (1.0 / CODE)

        def decode(c):
            code = ref[c * features:(c + 1) * features, :].astype(jnp.int32).astype(jnp.float32)
            weight = block[2 * half + c:2 * half + c + 1] * scale[half + c:half + c + 1]
            return code * scale[c:c + 1], weight

        return decode

    pieces = [(d, hop) for hop in range(far) for d in range(2) if hop < hops[1][d]]
    over_y = {}
    over_a = {}
    over_b = {}

    def send_piece(i, at):
        encode(send_y.at[i], lambda c: own(at, other, 1, c))
        over_y[i] = copy(send_y.at[i], first_y.at[i], 2, i, partner)

    for i in range(2):
        d, hop = pieces[i]
        send_piece(i, block(1, d, hop))
        for s in range(NY):
            encode(send_a.at[i, s], lambda c: own(block(0, i, 0), sides[s], 0, c))
            over_a[i, s, 0] = copy(send_a.at[i, s], ring_a.at[i, 0, s], 3, (i * NY + s) * far, toward(i))
    for i in range(2, nz - 1):
        d, hop = pieces[i]
        send_piece(i, block(1, d, hop))
    send_piece(nz - 1, z)

    def step_b(d, hop):
        i = pieces.index((d, hop))
        over_y[i].wait_recv()
        parts_of = [decoder(first_y.at[i])]
        if hop > 0:
            over_b[d, hop - 1].wait_recv()
            parts_of.append(decoder(ring_b.at[d, hop - 1]))
        at = block(1, d, hop)
        encode(first_y.at[i], lambda c: plus(own(at, y, 1, c), *(part(c) for part in parts_of)))
        over_b[d, hop] = copy(first_y.at[i], ring_b.at[d, hop], 4, d * far + hop, toward(d))

    def step_a(d, s, hop):
        over_a[d, s, hop - 1].wait_recv()
        held = ring_a.at[d, hop - 1, s]
        arrived = decoder(held)
        at = block(0, d, hop)
        encode(held, lambda c: plus(arrived(c), own(at, sides[s], 0, c)))
        over_a[d, s, hop] = copy(held, ring_a.at[d, hop, s], 3, (d * NY + s) * far + hop, toward(d))

    for hop in range(far):
        for d in range(2):
            if hop < hops[1][d]:
                step_b(d, hop)
        for s in range(NY):
            for d in range(2):
                if 0 < hop < hops[0][d]:
                    step_a(d, s, hop)

    def arrived_a(s):
        both = []
        for d in range(2):
            over_a[d, s, hops[0][d] - 1].wait_recv()
            both.append(decoder(ring_a.at[d, hops[0][d] - 1, s]))
        return lambda c: plus(both[0](c), both[1](c), own(z, sides[s], 0, c))

    encode(kept, arrived_a(0))
    over_last = copy(kept, last_y, 5, 0, partner)

    @pl.loop(0, clusters // SUB)
    def _(g):
        for r in range(SUB):
            put_halves(v_out, g * SUB + r, cluster_row(v2, g * SUB + r))

    def put(c, sums):
        value, weight = sums
        out[:, c * TILE:(c + 1) * TILE] = value / jnp.where(weight > 0.0, weight, 1.0)

    over_y[nz - 1].wait_recv()
    parts_b = [decoder(first_y.at[nz - 1])]
    for d in range(2):
        over_b[d, hops[1][d] - 1].wait_recv()
        parts_b.append(decoder(ring_b.at[d, hops[1][d] - 1]))
    for c in range(half):
        put(half + c, plus(own(z, y, 1, c), *(part(c) for part in parts_b)))
    mine = arrived_a(1)
    over_last.wait_recv()
    last = decoder(last_y)
    for c in range(half):
        put(c, plus(mine(c), last(c)))
    for made in [over_last] + list(over_y.values()) + list(over_a.values()) + list(over_b.values()):
        made.wait_send()


def transport(n_src, n_tgt, slots, table, xs, ys, x_mass, y_mass):
    clusters, features = xs.shape[:2]
    per, nz = clusters // n_tgt, n_tgt // NY
    far = nz // 2
    f32 = jnp.float32
    vmem = pl.BlockSpec(memory_space=pltpu.VMEM)
    smem = pl.BlockSpec(memory_space=pltpu.SMEM)
    hbm = pl.BlockSpec(memory_space=pl.ANY)
    dma = pltpu.SemaphoreType.DMA
    most = max(n_src, n_tgt)
    sems = [dma((4, most))] * 4
    for many in (nz, 2 * NY * far, 2 * far, 1):
        sems += [dma((many,))] * 2
    flat = jax.ShapeDtypeStruct((2 * clusters, TILE // 2), f32)
    row = pltpu.VMEM((clusters, TILE), f32)
    coded = (per // 2 * features + AUX, TILE)

    def codes(*many):
        return pltpu.VMEM(many + coded, jnp.int16)

    scratch = [pltpu.VMEM((2, 2 * clusters // n_tgt, TILE // 2), f32)] + [row] * 6 + [
        pltpu.VMEM((4, clusters, TILE), f32),
        pltpu.VMEM((4, most, clusters // min(n_src, n_tgt), TILE), f32),
        pltpu.VMEM((slots + 1, SUB, TILE), f32),
        pltpu.VMEM((slots + 1, SUB, TILE), f32),
        pltpu.VMEM((slots + 1, features, TILE), f32),
        pltpu.VMEM((slots + SUB, TILE), f32),
        codes(2, NY),
        codes(nz),
        codes(nz),
        codes(2, far, NY),
        codes(2, far),
        codes(),
        codes(),
        dma((2,)),
    ]
    return pl.pallas_call(
        functools.partial(kernel, (n_src, n_tgt, slots)),
        out_shape=(flat,) * 4 + (jax.ShapeDtypeStruct((features, per * TILE), f32),),
        in_specs=[smem, vmem, vmem, hbm, hbm],
        out_specs=(vmem,) * 5,
        scratch_shapes=scratch + sems,
        compiler_params=pltpu.CompilerParams(collective_id=0, has_side_effects=True, vmem_limit_bytes=40 * MIB),
        name="transport",
    )(table, xs, ys, x_mass, y_mass)


def pair_tables(pair_lists, tgt_block, per_block, slots, counts):
    width = pair_lists.shape[1]
    flat = pair_lists.reshape(-1)
    chosen = flat // per_block == tgt_block
    targets = flat % per_block
    sources = jnp.arange(flat.shape[0], dtype=jnp.int32) // width
    places = jnp.arange(slots, dtype=jnp.int32)
    rank = jnp.cumsum(chosen.astype(jnp.int32)) - 1
    matches = (rank[None, :] == places[:, None]) & chosen[None, :]
    row_src = jnp.sum(jnp.where(matches, sources[None, :], 0), axis=1)
    row_tgt = jnp.sum(jnp.where(matches, targets[None, :], 0), axis=1)
    live = jnp.sum(matches.astype(jnp.int32), axis=1) > 0
    before = (row_tgt[None, :] < row_tgt[:, None]) | (
        (row_tgt[None, :] == row_tgt[:, None]) & (places[None, :] < places[:, None]))
    order = jnp.where(live, jnp.sum((before & live[None, :]).astype(jnp.int32), axis=1), places)
    moves = order[None, :] == places[:, None]
    col_src = jnp.sum(jnp.where(moves, row_src[None, :], 0), axis=1)
    col_tgt = jnp.sum(jnp.where(moves, row_tgt[None, :], 0), axis=1)

    def ends(kept):
        same = jnp.concatenate([jnp.zeros((1,), jnp.int32), (kept[1:] == kept[:-1]).astype(jnp.int32)])
        found = (kept[None, :] == places[:, None]) & live[None, :]
        last = jnp.max(jnp.where(found, places[None, :], -1), axis=1)
        return same, jnp.where(last < 0, slots, last)

    row_keep, row_last = ends(row_src)
    col_keep, col_last = ends(col_tgt)
    return jnp.concatenate([row_tgt, row_src, row_keep, row_last, col_src, col_tgt, col_keep, col_last] + counts)


def shards(source_cells, target_cells, source_mass, target_mass, source_count, target_count, pair_lists):
    n_src, n_tgt = lax.axis_size("src"), lax.axis_size("tgt")
    slots = 2 * pair_lists.size // n_tgt
    table = pair_tables(
        pair_lists, lax.axis_index("tgt"), target_count.shape[0], slots, [source_count, target_count])
    xs, ys = (
        jnp.transpose(cells.reshape(cells.shape[0], -1, TILE), (1, 0, 2)) for cells in (source_cells, target_cells))
    u, v, x_norm, y_norm, mapped = transport(
        n_src, n_tgt, slots, table, xs, ys,
        source_mass.reshape(-1, TILE // 2), target_mass.reshape(-1, TILE // 2))
    source_pot = jnp.where(u > 0.5 * EMPTY, 0.5 * u + x_norm, 0.0)
    target_pot = jnp.where(v > 0.5 * EMPTY, 0.5 * v + y_norm, 0.0)
    return source_pot.reshape(-1), target_pot.reshape(-1), mapped


def solution(mesh):
    return jax.shard_map(
        shards,
        mesh=mesh,
        in_specs=(P(None, "src"), P(None, "tgt"), P("src"), P("tgt"), P("src"), P("tgt"), P("src", None)),
        out_specs=(P("src"), P("tgt"), P(None, ("src", "tgt"))),
        check_vma=False,
    )
```

```python
import functools
import math

import jax
import jax.numpy as jnp
from jax import lax
from jax.experimental import pallas as pl
from jax.experimental.pallas import tpu as pltpu
from jax.sharding import PartitionSpec as P

MESH = pl.DeviceIdType.MESH
EMPTY = -1e30
TILE = 256
SUB = 8
AUX = 16
CHUNKS = 8
CODE = 32752.0
NY = 2
MIB = 1 << 20
ROW_SUB, ROW_LANE, ROW_KEEP, ROW_LAST, COL_SUB, COL_LANE, COL_KEEP, COL_LAST, SRC_COUNT, TGT_COUNT = range(10)


def split3(row):
    high = row.astype(jnp.bfloat16).astype(jnp.float32)
    rest = row - high
    mid = rest.astype(jnp.bfloat16).astype(jnp.float32)
    low = rest - mid
    return high, mid, low


def cluster_row(ref, cluster):
    return ref[pl.ds(cluster, 1), :]


def halves_row(ref, cluster):
    first = ref[pl.ds(2 * cluster, 1), :]
    second = ref[pl.ds(2 * cluster + 1, 1), :]
    return jnp.concatenate([first, second], axis=1)


def put_halves(ref, cluster, row):
    ref[pl.ds(2 * cluster, 1), :] = row[:, :128]
    ref[pl.ds(2 * cluster + 1, 1), :] = row[:, 128:]


def squared_norm(cells):
    wide = cells.astype(jnp.float32)
    return jnp.sum(wide * wide, axis=0, keepdims=True)


def far_offset(axis, j, n):
    if axis == "tgt":
        return n // 2 + lax.div(j + 1, 2) * (1 - 2 * lax.rem(j, 2))
    i = lax.div(j, 2)
    near = n // 4 + lax.div(i + 1, 2) * (2 * lax.rem(i, 2) - 1)
    return near + lax.rem(j, 2) * (n - 2 * near)


def aux_rows(row, offset, other):
    at = lax.broadcasted_iota(jnp.int32, (AUX, TILE), 0)
    high, mid, low = split3(row)
    out = jnp.where((at >= other) & (at < other + 3), 1.0, 0.0)
    out = jnp.where(at == offset, high, out)
    out = jnp.where(at == offset + 1, mid, out)
    out = jnp.where(at == offset + 2, low, out)
    return out.astype(jnp.bfloat16)


def kernel(
    sizes, table, xs, ys, x_mass, y_mass, u_out, v_out, x_norm_out, y_norm_out, out,
    masses, u0, v0, u1, v1, u2, v2, parts, helds, slot_m, slot_s, slot_n, slot_d, send_a, send_y,
    first_y, ring_a, ring_b, last_y, kept, local, *sems,
):
    n_src, n_tgt, slots = sizes
    step = math.gcd(slots, 64)
    clusters, features = xs.shape[:2]
    me_src, me_tgt = lax.axis_index("src"), lax.axis_index("tgt")
    barrier = pltpu.get_barrier_semaphore()
    for axis, me, n in (("tgt", me_tgt, n_tgt), ("src", me_src, n_src)):
        for k in range(1, n):
            pl.semaphore_signal(barrier, inc=1, device_id={axis: lax.rem(me + k, n)}, device_id_type=MESH)

    fetches = []
    for i, (mass, me, n) in enumerate(((x_mass, me_tgt, n_tgt), (y_mass, me_src, n_src))):
        rows = 2 * clusters // n
        fetch = pltpu.make_async_copy(
            mass.at[pl.ds(pl.multiple_of(me * rows, rows), rows)], masses.at[i], local.at[i])
        fetch.start()
        fetches.append(fetch)
    slot_m[slots] = jnp.full((SUB, TILE), EMPTY, jnp.float32)
    slot_s[slots] = jnp.zeros((SUB, TILE), jnp.float32)
    slot_n[slots] = jnp.zeros((features, TILE), jnp.float32)
    slot_d[pl.ds(slots, SUB), :] = jnp.zeros((SUB, TILE), jnp.float32)

    def entry(which, p):
        return table[which * slots + p]

    def scaled(cells, ref):
        return cells * jnp.bfloat16(4.0) if ref is xs else cells

    def sweep(kind, first, sub_cells, lane_cells, sub_pot, lane_pot):
        def tile(p, carry):
            a, b, keep = entry(first, p), entry(first + 1, p), entry(first + 2, p)
            sub, lane = sub_cells[a], lane_cells[b]
            left = jnp.concatenate([scaled(sub, sub_cells), aux_rows(cluster_row(sub_pot, a), 0, 3)], axis=0)
            right = jnp.concatenate([scaled(lane, lane_cells), aux_rows(cluster_row(lane_pot, b), 3, 0)], axis=0)
            score = lax.dot_general(left, right, (((0,), (0,)), ((), ())), preferred_element_type=jnp.float32)
            hold = keep.astype(jnp.float32)
            if kind == "max":
                score = score.reshape(CHUNKS, TILE // SUB // CHUNKS, SUB, TILE)
                best = [jnp.max(score[q], axis=0) for q in range(CHUNKS)]
                old = carry[0] * hold + (1.0 - hold) * EMPTY
                new = functools.reduce(jnp.maximum, best, old)
                total = carry[1] * hold * jnp.exp(old - new)
                for q in range(CHUNKS):
                    total = total + jnp.sum(jnp.exp(score[q] - best[q][None]), axis=0) * jnp.exp(best[q] - new)
                slot_m[p] = new
                slot_s[p] = total
                return new, total
            weight = jnp.exp(score)
            if kind == "sum":
                total = carry[0] * hold + jnp.sum(weight.reshape(TILE // SUB, SUB, TILE), axis=0)
                slot_s[p] = total
                return (total,)
            high = weight.astype(jnp.bfloat16)
            low = (weight - high.astype(jnp.float32)).astype(jnp.bfloat16)
            ones = jnp.where(lax.broadcasted_iota(jnp.int32, (AUX, TILE), 0) == 0, 1.0, 0.0).astype(jnp.bfloat16)
            cells = jnp.concatenate([sub, ones], axis=0)
            moved = jnp.dot(cells, high, preferred_element_type=jnp.float32)
            moved = moved + jnp.dot(cells, low, preferred_element_type=jnp.float32)
            total = carry[0] * hold + moved[:features]
            weights = carry[1] * hold + moved[features:features + 1]
            slot_n[p] = total
            slot_d[pl.ds(p, 1), :] = weights
            return total, weights

        def group(g, carry):
            for r in range(step):
                carry = tile(g * step + r, carry)
            return carry

        empty = jnp.zeros((SUB, TILE), jnp.float32)
        if kind == "max":
            start = (empty + EMPTY, empty)
        elif kind == "sum":
            start = (empty,)
        else:
            start = (jnp.zeros((features, TILE), jnp.float32), jnp.zeros((1, TILE), jnp.float32))
        lax.fori_loop(0, slots // step, group, start)

    def reduce(kind, which, axis, me, n, last, old, new, meanwhile):
        part, held = parts.at[which], helds.at[which]
        per = clusters // n
        lanes = lax.broadcasted_iota(jnp.int32, (1, TILE), 1)

        def shard(peer):
            return pl.ds(pl.multiple_of(peer * per, per), per)

        def finish(peer):
            rows = []
            for r in range(per):
                at = entry(last, peer * per + r)
                if kind == "max":
                    best = jnp.max(slot_m[at], axis=0, keepdims=True)
                    row = jnp.sum(slot_s[at] * jnp.exp(slot_m[at] - best), axis=0, keepdims=True)
                    rows.append(best + jnp.log(jnp.where(row > 0.0, row, 1.0)))
                else:
                    rows.append(jnp.sum(slot_s[at], axis=0, keepdims=True))
            part[shard(peer), :] = jnp.concatenate(rows, axis=0)

        def copy(j, phase):
            k = far_offset(axis, j, n)
            peer = lax.rem(me + k, n)
            mine = shard(me)
            src_ref, dst_ref = (part.at[shard(peer)], held.at[k]) if phase == 0 else (new.at[mine], new.at[mine])
            return pltpu.make_async_remote_copy(
                src_ref=src_ref, dst_ref=dst_ref,
                send_sem=sems[2 * phase].at[which, k], recv_sem=sems[2 * phase + 1].at[which, k],
                device_id={axis: peer}, device_id_type=MESH)

        if which == 0:
            pl.semaphore_wait(barrier, n_src + n_tgt - 2)

        @pl.loop(0, n - 1)
        def _(j):
            finish(lax.rem(me + far_offset(axis, j, n), n))
            copy(j, 0).start()

        finish(me)
        meanwhile()
        if which < 2:
            fetches[which].wait()
        mass = masses.at[which % 2]
        count = (SRC_COUNT, TGT_COUNT)[which % 2]
        rows = []
        for r in range(per):
            rows.append(jnp.where(lanes < entry(count, me * per + r), jnp.log(halves_row(mass, r)), EMPTY))
        logmass = jnp.concatenate(rows, axis=0)

        @pl.loop(0, n - 1)
        def _(j):
            copy(j, 0).wait_recv()

        mine = shard(me)
        own = part[mine, :]
        if kind == "max":
            best = own
            for k in range(1, n):
                best = jnp.maximum(best, held[k])
            total = jnp.exp(own - best)
            for k in range(1, n):
                total = total + jnp.exp(held[k] - best)
            lse = best + jnp.log(total)
        else:
            total = own
            for k in range(1, n):
                total = total + held[k]
            lse = jnp.log(jnp.where(total > 0.0, total, 1.0))
        new[mine, :] = jnp.where(logmass > 0.5 * EMPTY, old[mine, :] + logmass - lse, EMPTY)

        @pl.loop(0, n - 1)
        def _(j):
            copy(j, 1).start()

        @pl.loop(0, n - 1)
        def _(j):
            copy(j, 0).wait_send()

        @pl.loop(0, n - 1)
        def _(j):
            copy(j, 1).wait()

    lane = lax.broadcasted_iota(jnp.int32, (1, TILE), 1)
    u0[...] = jnp.zeros(u0.shape, jnp.float32)

    @pl.loop(0, clusters // SUB)
    def _(g):
        rows = []
        for r in range(SUB):
            c = g * SUB + r
            rows.append(jnp.where(lane < entry(TGT_COUNT, c), -2.0 * squared_norm(ys[c]), EMPTY))
        v0[pl.ds(pl.multiple_of(g * SUB, SUB), SUB), :] = jnp.concatenate(rows, axis=0)

    def norms(part):
        groups = clusters // SUB // 2

        @pl.loop(part * groups, part * groups + groups)
        def _(g):
            for r in range(SUB):
                c = g * SUB + r
                put_halves(x_norm_out, c, squared_norm(xs[c]))
                put_halves(y_norm_out, c, -0.5 * cluster_row(v0, c))

    def nothing():
        pass

    def write_u():
        @pl.loop(0, clusters // SUB)
        def _(g):
            for r in range(SUB):
                put_halves(u_out, g * SUB + r, cluster_row(u2, g * SUB + r))

    sweep("max", ROW_SUB, ys, xs, v0, u0)
    reduce("max", 0, "tgt", me_tgt, n_tgt, ROW_LAST, u0, u1, lambda: norms(0))
    sweep("max", COL_SUB, xs, ys, u1, v0)
    reduce("max", 1, "src", me_src, n_src, COL_LAST, v0, v1, lambda: norms(1))
    sweep("sum", ROW_SUB, ys, xs, v1, u1)
    reduce("sum", 2, "tgt", me_tgt, n_tgt, ROW_LAST, u1, u2, nothing)
    sweep("sum", COL_SUB, xs, ys, u2, v1)
    reduce("sum", 3, "src", me_src, n_src, COL_LAST, v1, v2, write_u)
    sweep("map", ROW_SUB, ys, xs, v2, u2)

    n, nz = n_tgt, n_tgt // NY
    z, y = me_tgt // NY, lax.rem(me_tgt, NY)
    other = NY - 1 - y
    sides = (other, y)
    per = out.shape[1] // TILE
    half = per // 2
    sign = (1, -1)
    far = nz // 2
    hops = ((far, nz - 1 - far), (nz - 1 - far, far))
    partner = z * NY + other

    def toward(d):
        return lax.rem(z + sign[d] + nz, nz) * NY + y

    def block(g, d, hop):
        return lax.rem(z + sign[d] * (hops[g][d] - hop) + nz, nz)

    def own(at, side, g, c):
        slot = entry(ROW_LAST, (at * NY + side) * per + g * half + c)
        return slot_n[slot], slot_d[pl.ds(slot, 1), :]

    def plus(*terms):
        return tuple(functools.reduce(jnp.add, term) for term in zip(*terms))

    def copy(src, dst, sem, k, peer):
        made = pltpu.make_async_remote_copy(
            src_ref=src, dst_ref=dst, send_sem=sems[2 * sem].at[k], recv_sem=sems[2 * sem + 1].at[k],
            device_id={"tgt": peer}, device_id_type=MESH)
        made.start()
        return made

    def exponent_of(value):
        return jnp.ceil(jnp.log2(jnp.maximum(value, 1e-30)))

    def coded(value, exponent):
        return jnp.floor(value * (jnp.exp2(-exponent) * CODE) + 0.5)

    def encode(ref, values):
        rows = [[], [], []]
        for c in range(half):
            value, weight = values(c)
            exponent = exponent_of(jnp.max(jnp.abs(value), axis=0, keepdims=True))
            code = coded(value, exponent)
            ref[c * features:(c + 1) * features, :] = code.astype(jnp.int32).astype(jnp.int16)
            at = exponent_of(weight)
            for row, item in zip(rows, (exponent, at, coded(weight, at))):
                row.append(item)
        spare = [jnp.zeros((AUX - 3 * half, TILE), jnp.float32)]
        block = jnp.concatenate(rows[0] + rows[1] + rows[2] + spare, axis=0)
        ref[half * features:half * features + AUX, :] = block.astype(jnp.int32).astype(jnp.int16)

    def decoder(ref):
        block = ref[half * features:half * features + AUX, :].astype(jnp.int32).astype(jnp.float32)
        scale = jnp.exp2(block[:2 * half]) * (1.0 / CODE)

        def decode(c):
            code = ref[c * features:(c + 1) * features, :].astype(jnp.int32).astype(jnp.float32)
            weight = block[2 * half + c:2 * half + c + 1] * scale[half + c:half + c + 1]
            return code * scale[c:c + 1], weight

        return decode

    pieces = [(d, hop) for hop in range(far) for d in range(2) if hop < hops[1][d]]
    over_y = {}
    over_a = {}
    over_b = {}

    def send_piece(i, at):
        encode(send_y.at[i], lambda c: own(at, other, 1, c))
        over_y[i] = copy(send_y.at[i], first_y.at[i], 2, i, partner)

    def start_a(d, s):
        encode(send_a.at[d, s], lambda c: own(block(0, d, 0), sides[s], 0, c))
        over_a[d, s, 0] = copy(send_a.at[d, s], ring_a.at[d, 0, s], 3, (d * NY + s) * far, toward(d))

    for d in range(2):
        start_a(d, 0)
    for i in range(2):
        send_piece(i, block(1, *pieces[i]))
    for d in range(2):
        start_a(d, 1)
    for i in range(2, nz - 1):
        send_piece(i, block(1, *pieces[i]))
    send_piece(nz - 1, z)

    def step_b(d, hop):
        i = pieces.index((d, hop))
        over_y[i].wait_recv()
        parts_of = [decoder(first_y.at[i])]
        if hop > 0:
            over_b[d, hop - 1].wait_recv()
            parts_of.append(decoder(ring_b.at[d, hop - 1]))
        at = block(1, d, hop)
        encode(first_y.at[i], lambda c: plus(own(at, y, 1, c), *(part(c) for part in parts_of)))
        over_b[d, hop] = copy(first_y.at[i], ring_b.at[d, hop], 4, d * far + hop, toward(d))

    def step_a(d, s, hop):
        over_a[d, s, hop - 1].wait_recv()
        held = ring_a.at[d, hop - 1, s]
        arrived = decoder(held)
        at = block(0, d, hop)
        encode(held, lambda c: plus(arrived(c), own(at, sides[s], 0, c)))
        over_a[d, s, hop] = copy(held, ring_a.at[d, hop, s], 3, (d * NY + s) * far + hop, toward(d))

    def arrived_a(s):
        both = []
        for d in range(2):
            over_a[d, s, hops[0][d] - 1].wait_recv()
            both.append(decoder(ring_a.at[d, hops[0][d] - 1, s]))
        return lambda c: plus(both[0](c), both[1](c), own(z, sides[s], 0, c))

    for hop in range(1, far + 1):
        for d in range(2):
            if hop < hops[0][d]:
                step_a(d, 0, hop)
        if hop == far:
            encode(kept, arrived_a(0))
            over_last = copy(kept, last_y, 5, 0, partner)
        for d in range(2):
            if hop - 1 < hops[1][d]:
                step_b(d, hop - 1)
        for d in range(2):
            if hop < hops[0][d]:
                step_a(d, 1, hop)

    @pl.loop(0, clusters // SUB)
    def _(g):
        for r in range(SUB):
            put_halves(v_out, g * SUB + r, cluster_row(v2, g * SUB + r))

    def put(c, sums):
        value, weight = sums
        out[:, c * TILE:(c + 1) * TILE] = value / jnp.where(weight > 0.0, weight, 1.0)

    over_y[nz - 1].wait_recv()
    parts_b = [decoder(first_y.at[nz - 1])]
    for d in range(2):
        over_b[d, hops[1][d] - 1].wait_recv()
        parts_b.append(decoder(ring_b.at[d, hops[1][d] - 1]))
    for c in range(half):
        put(half + c, plus(own(z, y, 1, c), *(part(c) for part in parts_b)))
    mine = arrived_a(1)
    over_last.wait_recv()
    last = decoder(last_y)
    for c in range(half):
        put(c, plus(mine(c), last(c)))
    for made in [over_last] + list(over_y.values()) + list(over_a.values()) + list(over_b.values()):
        made.wait_send()


def transport(n_src, n_tgt, slots, table, xs, ys, x_mass, y_mass):
    clusters, features = xs.shape[:2]
    per, nz = clusters // n_tgt, n_tgt // NY
    far = nz // 2
    f32 = jnp.float32
    vmem = pl.BlockSpec(memory_space=pltpu.VMEM)
    smem = pl.BlockSpec(memory_space=pltpu.SMEM)
    hbm = pl.BlockSpec(memory_space=pl.ANY)
    dma = pltpu.SemaphoreType.DMA
    most = max(n_src, n_tgt)
    sems = [dma((4, most))] * 4
    for many in (nz, 2 * NY * far, 2 * far, 1):
        sems += [dma((many,))] * 2
    flat = jax.ShapeDtypeStruct((2 * clusters, TILE // 2), f32)
    row = pltpu.VMEM((clusters, TILE), f32)
    coded = (per // 2 * features + AUX, TILE)

    def codes(*many):
        return pltpu.VMEM(many + coded, jnp.int16)

    scratch = [pltpu.VMEM((2, 2 * clusters // n_tgt, TILE // 2), f32)] + [row] * 6 + [
        pltpu.VMEM((4, clusters, TILE), f32),
        pltpu.VMEM((4, most, clusters // min(n_src, n_tgt), TILE), f32),
        pltpu.VMEM((slots + 1, SUB, TILE), f32),
        pltpu.VMEM((slots + 1, SUB, TILE), f32),
        pltpu.VMEM((slots + 1, features, TILE), f32),
        pltpu.VMEM((slots + SUB, TILE), f32),
        codes(2, NY),
        codes(nz),
        codes(nz),
        codes(2, far, NY),
        codes(2, far),
        codes(),
        codes(),
        dma((2,)),
    ]
    return pl.pallas_call(
        functools.partial(kernel, (n_src, n_tgt, slots)),
        out_shape=(flat,) * 4 + (jax.ShapeDtypeStruct((features, per * TILE), f32),),
        in_specs=[smem, vmem, vmem, hbm, hbm],
        out_specs=(vmem,) * 5,
        scratch_shapes=scratch + sems,
        compiler_params=pltpu.CompilerParams(collective_id=0, has_side_effects=True, vmem_limit_bytes=40 * MIB),
        name="transport",
    )(table, xs, ys, x_mass, y_mass)


def pair_tables(pair_lists, tgt_block, per_block, slots, counts):
    width = pair_lists.shape[1]
    flat = pair_lists.reshape(-1)
    chosen = flat // per_block == tgt_block
    targets = flat % per_block
    sources = jnp.arange(flat.shape[0], dtype=jnp.int32) // width
    places = jnp.arange(slots, dtype=jnp.int32)
    rank = jnp.cumsum(chosen.astype(jnp.int32)) - 1
    matches = (rank[None, :] == places[:, None]) & chosen[None, :]
    row_src = jnp.sum(jnp.where(matches, sources[None, :], 0), axis=1)
    row_tgt = jnp.sum(jnp.where(matches, targets[None, :], 0), axis=1)
    live = jnp.sum(matches.astype(jnp.int32), axis=1) > 0
    before = (row_tgt[None, :] < row_tgt[:, None]) | (
        (row_tgt[None, :] == row_tgt[:, None]) & (places[None, :] < places[:, None]))
    order = jnp.where(live, jnp.sum((before & live[None, :]).astype(jnp.int32), axis=1), places)
    moves = order[None, :] == places[:, None]
    col_src = jnp.sum(jnp.where(moves, row_src[None, :], 0), axis=1)
    col_tgt = jnp.sum(jnp.where(moves, row_tgt[None, :], 0), axis=1)

    def ends(kept):
        same = jnp.concatenate([jnp.zeros((1,), jnp.int32), (kept[1:] == kept[:-1]).astype(jnp.int32)])
        found = (kept[None, :] == places[:, None]) & live[None, :]
        last = jnp.max(jnp.where(found, places[None, :], -1), axis=1)
        return same, jnp.where(last < 0, slots, last)

    row_keep, row_last = ends(row_src)
    col_keep, col_last = ends(col_tgt)
    return jnp.concatenate([row_tgt, row_src, row_keep, row_last, col_src, col_tgt, col_keep, col_last] + counts)


def shards(source_cells, target_cells, source_mass, target_mass, source_count, target_count, pair_lists):
    n_src, n_tgt = lax.axis_size("src"), lax.axis_size("tgt")
    slots = 2 * pair_lists.size // n_tgt
    table = pair_tables(
        pair_lists, lax.axis_index("tgt"), target_count.shape[0], slots, [source_count, target_count])
    xs, ys = (
        jnp.transpose(cells.reshape(cells.shape[0], -1, TILE), (1, 0, 2)) for cells in (source_cells, target_cells))
    u, v, x_norm, y_norm, mapped = transport(
        n_src, n_tgt, slots, table, xs, ys,
        source_mass.reshape(-1, TILE // 2), target_mass.reshape(-1, TILE // 2))
    source_pot = jnp.where(u > 0.5 * EMPTY, 0.5 * u + x_norm, 0.0)
    target_pot = jnp.where(v > 0.5 * EMPTY, 0.5 * v + y_norm, 0.0)
    return source_pot.reshape(-1), target_pot.reshape(-1), mapped


def solution(mesh):
    return jax.shard_map(
        shards,
        mesh=mesh,
        in_specs=(P(None, "src"), P(None, "tgt"), P("src"), P("tgt"), P("src"), P("tgt"), P("src", None)),
        out_specs=(P("src"), P("tgt"), P(None, ("src", "tgt"))),
        check_vma=False,
    )
```

```python
import functools
import math

import jax
import jax.numpy as jnp
from jax import lax
from jax.experimental import pallas as pl
from jax.experimental.pallas import tpu as pltpu
from jax.sharding import PartitionSpec as P

MESH = pl.DeviceIdType.MESH
EMPTY = -1e30
TILE = 256
SUB = 8
AUX = 16
CHUNKS = 8
CODE = 32752.0
EARLY = 64
NY = 2
MIB = 1 << 20
ROW_SUB, ROW_LANE, ROW_KEEP, ROW_LAST, COL_SUB, COL_LANE, COL_KEEP, COL_LAST, SRC_COUNT, TGT_COUNT = range(10)


def split3(row):
    high = row.astype(jnp.bfloat16).astype(jnp.float32)
    rest = row - high
    mid = rest.astype(jnp.bfloat16).astype(jnp.float32)
    low = rest - mid
    return high, mid, low


def cluster_row(ref, cluster):
    return ref[pl.ds(cluster, 1), :]


def halves_row(ref, cluster):
    first = ref[pl.ds(2 * cluster, 1), :]
    second = ref[pl.ds(2 * cluster + 1, 1), :]
    return jnp.concatenate([first, second], axis=1)


def put_halves(ref, cluster, row):
    ref[pl.ds(2 * cluster, 1), :] = row[:, :128]
    ref[pl.ds(2 * cluster + 1, 1), :] = row[:, 128:]


def squared_norm(cells):
    wide = cells.astype(jnp.float32)
    return jnp.sum(wide * wide, axis=0, keepdims=True)


def far_offset(axis, j, n):
    if axis == "tgt":
        return n // 2 + lax.div(j + 1, 2) * (1 - 2 * lax.rem(j, 2))
    i = lax.div(j, 2)
    near = n // 4 + lax.div(i + 1, 2) * (2 * lax.rem(i, 2) - 1)
    return near + lax.rem(j, 2) * (n - 2 * near)


def aux_rows(row, offset, other):
    at = lax.broadcasted_iota(jnp.int32, (AUX, TILE), 0)
    high, mid, low = split3(row)
    out = jnp.where((at >= other) & (at < other + 3), 1.0, 0.0)
    out = jnp.where(at == offset, high, out)
    out = jnp.where(at == offset + 1, mid, out)
    out = jnp.where(at == offset + 2, low, out)
    return out.astype(jnp.bfloat16)


def kernel(
    sizes, table, xs, ys, x_mass, y_mass, u_out, v_out, x_norm_out, y_norm_out, out,
    masses, u0, v0, u1, v1, u2, v2, parts, helds, slot_m, slot_s, slot_n, slot_d, send_a, send_y,
    first_y, ring_a, ring_b, last_y, kept, ahead, local, *sems,
):
    n_src, n_tgt, slots = sizes
    step = math.gcd(slots, 64)
    clusters, features = xs.shape[:2]
    me_src, me_tgt = lax.axis_index("src"), lax.axis_index("tgt")
    barrier = pltpu.get_barrier_semaphore()
    for axis, me, n in (("tgt", me_tgt, n_tgt), ("src", me_src, n_src)):
        for k in range(1, n):
            pl.semaphore_signal(barrier, inc=1, device_id={axis: lax.rem(me + k, n)}, device_id_type=MESH)

    fetches = []
    for i, (mass, me, n) in enumerate(((x_mass, me_tgt, n_tgt), (y_mass, me_src, n_src))):
        rows = 2 * clusters // n
        fetch = pltpu.make_async_copy(
            mass.at[pl.ds(pl.multiple_of(me * rows, rows), rows)], masses.at[i], local.at[i])
        fetch.start()
        fetches.append(fetch)
    slot_m[slots] = jnp.full((SUB, TILE), EMPTY, jnp.float32)
    slot_s[slots] = jnp.zeros((SUB, TILE), jnp.float32)
    slot_n[slots] = jnp.zeros((features, TILE), jnp.float32)
    slot_d[pl.ds(slots, SUB), :] = jnp.zeros((SUB, TILE), jnp.float32)

    def entry(which, p):
        return table[which * slots + p]

    def scaled(cells, ref):
        return cells * jnp.bfloat16(4.0) if ref is xs else cells

    def scores(a, b, sub_cells, lane_cells, sub_pot, lane_pot):
        sub, lane = sub_cells[a], lane_cells[b]
        left = jnp.concatenate([scaled(sub, sub_cells), aux_rows(cluster_row(sub_pot, a), 0, 3)], axis=0)
        right = jnp.concatenate([scaled(lane, lane_cells), aux_rows(cluster_row(lane_pot, b), 3, 0)], axis=0)
        return lax.dot_general(left, right, (((0,), (0,)), ((), ())), preferred_element_type=jnp.float32)

    def two_parts(value):
        high = value.astype(jnp.bfloat16)
        return high, (value - high.astype(jnp.float32)).astype(jnp.bfloat16)

    def with_weights(cells, row):
        at = lax.broadcasted_iota(jnp.int32, (AUX, TILE), 0)
        return jnp.concatenate([cells, jnp.where(at == 0, row, 0.0).astype(cells.dtype)], axis=0)

    def early(first):
        for p in range(first, first + EARLY // 2):
            weight = jnp.exp(scores(entry(ROW_SUB, p), entry(ROW_LANE, p), ys, xs, v1, u2))
            ahead[p, :TILE], ahead[p, TILE:] = two_parts(weight)

    def sweep(kind, first, sub_cells, lane_cells, sub_pot, lane_pot):
        def store(p, carry, moved, keep):
            hold = keep.astype(jnp.float32)
            total = carry[0] * hold + moved[:features]
            weights = carry[1] * hold + moved[features:features + 1]
            slot_n[p] = total
            slot_d[pl.ds(p, 1), :] = weights
            return total, weights

        def kept_tile(p, carry):
            a, keep = entry(first, p), entry(first + 2, p)
            change = jnp.exp(cluster_row(sub_pot, a) - cluster_row(v1, a))
            high, low = two_parts(with_weights(sub_cells[a].astype(jnp.float32) * change, change))
            left = jnp.concatenate([high, low], axis=0)
            moved = jnp.dot(left, ahead[p, :TILE], preferred_element_type=jnp.float32)
            moved = moved + jnp.dot(left, ahead[p, TILE:], preferred_element_type=jnp.float32)
            return store(p, carry, moved[:features + AUX] + moved[features + AUX:], keep)

        def tile(p, carry):
            a, b, keep = entry(first, p), entry(first + 1, p), entry(first + 2, p)
            score = scores(a, b, sub_cells, lane_cells, sub_pot, lane_pot)
            hold = keep.astype(jnp.float32)
            if kind == "max":
                score = score.reshape(CHUNKS, TILE // SUB // CHUNKS, SUB, TILE)
                best = [jnp.max(score[q], axis=0) for q in range(CHUNKS)]
                old = carry[0] * hold + (1.0 - hold) * EMPTY
                new = functools.reduce(jnp.maximum, best, old)
                total = carry[1] * hold * jnp.exp(old - new)
                for q in range(CHUNKS):
                    total = total + jnp.sum(jnp.exp(score[q] - best[q][None]), axis=0) * jnp.exp(best[q] - new)
                slot_m[p] = new
                slot_s[p] = total
                return new, total
            weight = jnp.exp(score)
            if kind == "sum":
                total = carry[0] * hold + jnp.sum(weight.reshape(TILE // SUB, SUB, TILE), axis=0)
                slot_s[p] = total
                return (total,)
            high, low = two_parts(weight)
            cells = with_weights(sub_cells[a], 1.0)
            moved = jnp.dot(cells, high, preferred_element_type=jnp.float32)
            moved = moved + jnp.dot(cells, low, preferred_element_type=jnp.float32)
            return store(p, carry, moved, keep)

        def group(g, carry):
            for r in range(step):
                carry = tile(g * step + r, carry)
            return carry

        empty = jnp.zeros((SUB, TILE), jnp.float32)
        if kind == "max":
            start = (empty + EMPTY, empty)
        elif kind == "sum":
            start = (empty,)
        else:
            start = (jnp.zeros((features, TILE), jnp.float32), jnp.zeros((1, TILE), jnp.float32))
        done = 0
        if kind == "map":
            for p in range(EARLY):
                start = kept_tile(p, start)
            done = EARLY // step
        lax.fori_loop(done, slots // step, group, start)

    def reduce(kind, which, axis, me, n, last, old, new, meanwhile, later):
        part, held = parts.at[which], helds.at[which]
        per = clusters // n
        lanes = lax.broadcasted_iota(jnp.int32, (1, TILE), 1)

        def shard(peer):
            return pl.ds(pl.multiple_of(peer * per, per), per)

        def finish(peer):
            rows = []
            for r in range(per):
                at = entry(last, peer * per + r)
                if kind == "max":
                    best = jnp.max(slot_m[at], axis=0, keepdims=True)
                    row = jnp.sum(slot_s[at] * jnp.exp(slot_m[at] - best), axis=0, keepdims=True)
                    rows.append(best + jnp.log(jnp.where(row > 0.0, row, 1.0)))
                else:
                    rows.append(jnp.sum(slot_s[at], axis=0, keepdims=True))
            part[shard(peer), :] = jnp.concatenate(rows, axis=0)

        def copy(j, phase):
            k = far_offset(axis, j, n)
            peer = lax.rem(me + k, n)
            mine = shard(me)
            src_ref, dst_ref = (part.at[shard(peer)], held.at[k]) if phase == 0 else (new.at[mine], new.at[mine])
            return pltpu.make_async_remote_copy(
                src_ref=src_ref, dst_ref=dst_ref,
                send_sem=sems[2 * phase].at[which, k], recv_sem=sems[2 * phase + 1].at[which, k],
                device_id={axis: peer}, device_id_type=MESH)

        if which == 0:
            pl.semaphore_wait(barrier, n_src + n_tgt - 2)

        @pl.loop(0, n - 1)
        def _(j):
            finish(lax.rem(me + far_offset(axis, j, n), n))
            copy(j, 0).start()

        finish(me)
        meanwhile()
        if which < 2:
            fetches[which].wait()
        mass = masses.at[which % 2]
        count = (SRC_COUNT, TGT_COUNT)[which % 2]
        rows = []
        for r in range(per):
            rows.append(jnp.where(lanes < entry(count, me * per + r), jnp.log(halves_row(mass, r)), EMPTY))
        logmass = jnp.concatenate(rows, axis=0)

        @pl.loop(0, n - 1)
        def _(j):
            copy(j, 0).wait_recv()

        mine = shard(me)
        own = part[mine, :]
        if kind == "max":
            best = own
            for k in range(1, n):
                best = jnp.maximum(best, held[k])
            total = jnp.exp(own - best)
            for k in range(1, n):
                total = total + jnp.exp(held[k] - best)
            lse = best + jnp.log(total)
        else:
            total = own
            for k in range(1, n):
                total = total + held[k]
            lse = jnp.log(jnp.where(total > 0.0, total, 1.0))
        new[mine, :] = jnp.where(logmass > 0.5 * EMPTY, old[mine, :] + logmass - lse, EMPTY)

        @pl.loop(0, n - 1)
        def _(j):
            copy(j, 1).start()

        later()

        @pl.loop(0, n - 1)
        def _(j):
            copy(j, 0).wait_send()

        @pl.loop(0, n - 1)
        def _(j):
            copy(j, 1).wait()

    lane = lax.broadcasted_iota(jnp.int32, (1, TILE), 1)
    u0[...] = jnp.zeros(u0.shape, jnp.float32)

    @pl.loop(0, clusters // SUB)
    def _(g):
        rows = []
        for r in range(SUB):
            c = g * SUB + r
            rows.append(jnp.where(lane < entry(TGT_COUNT, c), -2.0 * squared_norm(ys[c]), EMPTY))
        v0[pl.ds(pl.multiple_of(g * SUB, SUB), SUB), :] = jnp.concatenate(rows, axis=0)

    def norms(part):
        groups = clusters // SUB // 2

        @pl.loop(part * groups, part * groups + groups)
        def _(g):
            for r in range(SUB):
                c = g * SUB + r
                put_halves(x_norm_out, c, squared_norm(xs[c]))
                put_halves(y_norm_out, c, -0.5 * cluster_row(v0, c))

    def nothing():
        pass

    sweep("max", ROW_SUB, ys, xs, v0, u0)
    reduce("max", 0, "tgt", me_tgt, n_tgt, ROW_LAST, u0, u1, lambda: norms(0), nothing)
    sweep("max", COL_SUB, xs, ys, u1, v0)
    reduce("max", 1, "src", me_src, n_src, COL_LAST, v0, v1, lambda: norms(1), nothing)
    sweep("sum", ROW_SUB, ys, xs, v1, u1)
    reduce("sum", 2, "tgt", me_tgt, n_tgt, ROW_LAST, u1, u2, nothing, nothing)
    sweep("sum", COL_SUB, xs, ys, u2, v1)
    reduce("sum", 3, "src", me_src, n_src, COL_LAST, v1, v2, lambda: early(0), lambda: early(EARLY // 2))
    sweep("map", ROW_SUB, ys, xs, v2, u2)

    n, nz = n_tgt, n_tgt // NY
    z, y = me_tgt // NY, lax.rem(me_tgt, NY)
    other = NY - 1 - y
    sides = (other, y)
    per = out.shape[1] // TILE
    half = per // 2
    sign = (1, -1)
    far = nz // 2
    hops = ((far, nz - 1 - far), (nz - 1 - far, far))
    partner = z * NY + other

    def toward(d):
        return lax.rem(z + sign[d] + nz, nz) * NY + y

    def block(g, d, hop):
        return lax.rem(z + sign[d] * (hops[g][d] - hop) + nz, nz)

    def own(at, side, g, c):
        slot = entry(ROW_LAST, (at * NY + side) * per + g * half + c)
        return slot_n[slot], slot_d[pl.ds(slot, 1), :]

    def plus(*terms):
        return tuple(functools.reduce(jnp.add, term) for term in zip(*terms))

    def copy(src, dst, sem, k, peer):
        made = pltpu.make_async_remote_copy(
            src_ref=src, dst_ref=dst, send_sem=sems[2 * sem].at[k], recv_sem=sems[2 * sem + 1].at[k],
            device_id={"tgt": peer}, device_id_type=MESH)
        made.start()
        return made

    def exponent_of(value):
        return jnp.ceil(jnp.log2(jnp.maximum(value, 1e-30)))

    def coded(value, exponent):
        return jnp.floor(value * (jnp.exp2(-exponent) * CODE) + 0.5)

    def encode(ref, values):
        rows = [[], [], []]
        for c in range(half):
            value, weight = values(c)
            exponent = exponent_of(jnp.max(jnp.abs(value), axis=0, keepdims=True))
            code = coded(value, exponent)
            ref[c * features:(c + 1) * features, :] = code.astype(jnp.int32).astype(jnp.int16)
            at = exponent_of(weight)
            for row, item in zip(rows, (exponent, at, coded(weight, at))):
                row.append(item)
        spare = [jnp.zeros((AUX - 3 * half, TILE), jnp.float32)]
        block = jnp.concatenate(rows[0] + rows[1] + rows[2] + spare, axis=0)
        ref[half * features:half * features + AUX, :] = block.astype(jnp.int32).astype(jnp.int16)

    def decoder(ref):
        block = ref[half * features:half * features + AUX, :].astype(jnp.int32).astype(jnp.float32)
        scale = jnp.exp2(block[:2 * half]) * (1.0 / CODE)

        def decode(c):
            code = ref[c * features:(c + 1) * features, :].astype(jnp.int32).astype(jnp.float32)
            weight = block[2 * half + c:2 * half + c + 1] * scale[half + c:half + c + 1]
            return code * scale[c:c + 1], weight

        return decode

    pieces = [(d, hop) for hop in range(far) for d in range(2) if hop < hops[1][d]]
    over_y = {}
    over_a = {}
    over_b = {}

    def send_piece(i, at):
        encode(send_y.at[i], lambda c: own(at, other, 1, c))
        over_y[i] = copy(send_y.at[i], first_y.at[i], 2, i, partner)

    def start_a(d, s):
        encode(send_a.at[d, s], lambda c: own(block(0, d, 0), sides[s], 0, c))
        over_a[d, s, 0] = copy(send_a.at[d, s], ring_a.at[d, 0, s], 3, (d * NY + s) * far, toward(d))

    for d in range(2):
        start_a(d, 0)
    for i in range(2):
        send_piece(i, block(1, *pieces[i]))
    for d in range(2):
        start_a(d, 1)
    for i in range(2, nz - 1):
        send_piece(i, block(1, *pieces[i]))
    send_piece(nz - 1, z)

    def step_b(d, hop):
        i = pieces.index((d, hop))
        over_y[i].wait_recv()
        parts_of = [decoder(first_y.at[i])]
        if hop > 0:
            over_b[d, hop - 1].wait_recv()
            parts_of.append(decoder(ring_b.at[d, hop - 1]))
        at = block(1, d, hop)
        encode(first_y.at[i], lambda c: plus(own(at, y, 1, c), *(part(c) for part in parts_of)))
        over_b[d, hop] = copy(first_y.at[i], ring_b.at[d, hop], 4, d * far + hop, toward(d))

    def step_a(d, s, hop):
        over_a[d, s, hop - 1].wait_recv()
        held = ring_a.at[d, hop - 1, s]
        arrived = decoder(held)
        at = block(0, d, hop)
        encode(held, lambda c: plus(arrived(c), own(at, sides[s], 0, c)))
        over_a[d, s, hop] = copy(held, ring_a.at[d, hop, s], 3, (d * NY + s) * far + hop, toward(d))

    def arrived_a(s):
        both = []
        for d in range(2):
            over_a[d, s, hops[0][d] - 1].wait_recv()
            both.append(decoder(ring_a.at[d, hops[0][d] - 1, s]))
        return lambda c: plus(both[0](c), both[1](c), own(z, sides[s], 0, c))

    for hop in range(1, far + 1):
        for d in range(2):
            if hop < hops[0][d]:
                step_a(d, 0, hop)
        if hop == far:
            encode(kept, arrived_a(0))
            over_last = copy(kept, last_y, 5, 0, partner)
        for d in range(2):
            if hop - 1 < hops[1][d]:
                step_b(d, hop - 1)
        for d in range(2):
            if hop < hops[0][d]:
                step_a(d, 1, hop)

    @pl.loop(0, clusters // SUB)
    def _(g):
        for r in range(SUB):
            put_halves(u_out, g * SUB + r, cluster_row(u2, g * SUB + r))
            put_halves(v_out, g * SUB + r, cluster_row(v2, g * SUB + r))

    def put(c, sums):
        value, weight = sums
        out[:, c * TILE:(c + 1) * TILE] = value / jnp.where(weight > 0.0, weight, 1.0)

    over_y[nz - 1].wait_recv()
    parts_b = [decoder(first_y.at[nz - 1])]
    for d in range(2):
        over_b[d, hops[1][d] - 1].wait_recv()
        parts_b.append(decoder(ring_b.at[d, hops[1][d] - 1]))
    for c in range(half):
        put(half + c, plus(own(z, y, 1, c), *(part(c) for part in parts_b)))
    mine = arrived_a(1)
    over_last.wait_recv()
    last = decoder(last_y)
    for c in range(half):
        put(c, plus(mine(c), last(c)))
    for made in [over_last] + list(over_y.values()) + list(over_a.values()) + list(over_b.values()):
        made.wait_send()


def transport(n_src, n_tgt, slots, table, xs, ys, x_mass, y_mass):
    clusters, features = xs.shape[:2]
    per, nz = clusters // n_tgt, n_tgt // NY
    far = nz // 2
    f32 = jnp.float32
    vmem = pl.BlockSpec(memory_space=pltpu.VMEM)
    smem = pl.BlockSpec(memory_space=pltpu.SMEM)
    hbm = pl.BlockSpec(memory_space=pl.ANY)
    dma = pltpu.SemaphoreType.DMA
    most = max(n_src, n_tgt)
    sems = [dma((4, most))] * 4
    for many in (nz, 2 * NY * far, 2 * far, 1):
        sems += [dma((many,))] * 2
    flat = jax.ShapeDtypeStruct((2 * clusters, TILE // 2), f32)
    row = pltpu.VMEM((clusters, TILE), f32)
    coded = (per // 2 * features + AUX, TILE)

    def codes(*many):
        return pltpu.VMEM(many + coded, jnp.int16)

    scratch = [pltpu.VMEM((2, 2 * clusters // n_tgt, TILE // 2), f32)] + [row] * 6 + [
        pltpu.VMEM((4, clusters, TILE), f32),
        pltpu.VMEM((4, most, clusters // min(n_src, n_tgt), TILE), f32),
        pltpu.VMEM((slots + 1, SUB, TILE), f32),
        pltpu.VMEM((slots + 1, SUB, TILE), f32),
        pltpu.VMEM((slots + 1, features, TILE), f32),
        pltpu.VMEM((slots + SUB, TILE), f32),
        codes(2, NY),
        codes(nz),
        codes(nz),
        codes(2, far, NY),
        codes(2, far),
        codes(),
        codes(),
        pltpu.VMEM((EARLY, 2 * TILE, TILE), jnp.bfloat16),
        dma((2,)),
    ]
    return pl.pallas_call(
        functools.partial(kernel, (n_src, n_tgt, slots)),
        out_shape=(flat,) * 4 + (jax.ShapeDtypeStruct((features, per * TILE), f32),),
        in_specs=[smem, vmem, vmem, hbm, hbm],
        out_specs=(vmem,) * 5,
        scratch_shapes=scratch + sems,
        compiler_params=pltpu.CompilerParams(collective_id=0, has_side_effects=True, vmem_limit_bytes=48 * MIB),
        name="transport",
    )(table, xs, ys, x_mass, y_mass)


def pair_tables(pair_lists, tgt_block, per_block, slots, counts):
    width = pair_lists.shape[1]
    flat = pair_lists.reshape(-1)
    chosen = flat // per_block == tgt_block
    targets = flat % per_block
    sources = jnp.arange(flat.shape[0], dtype=jnp.int32) // width
    places = jnp.arange(slots, dtype=jnp.int32)
    rank = jnp.cumsum(chosen.astype(jnp.int32)) - 1
    matches = (rank[None, :] == places[:, None]) & chosen[None, :]
    row_src = jnp.sum(jnp.where(matches, sources[None, :], 0), axis=1)
    row_tgt = jnp.sum(jnp.where(matches, targets[None, :], 0), axis=1)
    live = jnp.sum(matches.astype(jnp.int32), axis=1) > 0
    before = (row_tgt[None, :] < row_tgt[:, None]) | (
        (row_tgt[None, :] == row_tgt[:, None]) & (places[None, :] < places[:, None]))
    order = jnp.where(live, jnp.sum((before & live[None, :]).astype(jnp.int32), axis=1), places)
    moves = order[None, :] == places[:, None]
    col_src = jnp.sum(jnp.where(moves, row_src[None, :], 0), axis=1)
    col_tgt = jnp.sum(jnp.where(moves, row_tgt[None, :], 0), axis=1)

    def ends(kept):
        same = jnp.concatenate([jnp.zeros((1,), jnp.int32), (kept[1:] == kept[:-1]).astype(jnp.int32)])
        found = (kept[None, :] == places[:, None]) & live[None, :]
        last = jnp.max(jnp.where(found, places[None, :], -1), axis=1)
        return same, jnp.where(last < 0, slots, last)

    row_keep, row_last = ends(row_src)
    col_keep, col_last = ends(col_tgt)
    return jnp.concatenate([row_tgt, row_src, row_keep, row_last, col_src, col_tgt, col_keep, col_last] + counts)


def shards(source_cells, target_cells, source_mass, target_mass, source_count, target_count, pair_lists):
    n_src, n_tgt = lax.axis_size("src"), lax.axis_size("tgt")
    slots = 2 * pair_lists.size // n_tgt
    table = pair_tables(
        pair_lists, lax.axis_index("tgt"), target_count.shape[0], slots, [source_count, target_count])
    xs, ys = (
        jnp.transpose(cells.reshape(cells.shape[0], -1, TILE), (1, 0, 2)) for cells in (source_cells, target_cells))
    u, v, x_norm, y_norm, mapped = transport(
        n_src, n_tgt, slots, table, xs, ys,
        source_mass.reshape(-1, TILE // 2), target_mass.reshape(-1, TILE // 2))
    source_pot = jnp.where(u > 0.5 * EMPTY, 0.5 * u + x_norm, 0.0)
    target_pot = jnp.where(v > 0.5 * EMPTY, 0.5 * v + y_norm, 0.0)
    return source_pot.reshape(-1), target_pot.reshape(-1), mapped


def solution(mesh):
    return jax.shard_map(
        shards,
        mesh=mesh,
        in_specs=(P(None, "src"), P(None, "tgt"), P("src"), P("tgt"), P("src"), P("tgt"), P("src", None)),
        out_specs=(P("src"), P("tgt"), P(None, ("src", "tgt"))),
        check_vma=False,
    )
```

```python
import functools
import math

import jax
import jax.numpy as jnp
from jax import lax
from jax.experimental import pallas as pl
from jax.experimental.pallas import tpu as pltpu
from jax.sharding import PartitionSpec as P

MESH = pl.DeviceIdType.MESH
EMPTY = -1e30
TILE = 256
SUB = 8
AUX = 16
CHUNKS = 8
CODE = 32752.0
NY = 2
MIB = 1 << 20
ROW_SUB, ROW_LANE, ROW_KEEP, ROW_LAST, COL_SUB, COL_LANE, COL_KEEP, COL_LAST, SRC_COUNT, TGT_COUNT = range(10)


def split3(row):
    high = row.astype(jnp.bfloat16).astype(jnp.float32)
    rest = row - high
    mid = rest.astype(jnp.bfloat16).astype(jnp.float32)
    low = rest - mid
    return high, mid, low


def cluster_row(ref, cluster):
    return ref[pl.ds(cluster, 1), :]


def halves_row(ref, cluster):
    first = ref[pl.ds(2 * cluster, 1), :]
    second = ref[pl.ds(2 * cluster + 1, 1), :]
    return jnp.concatenate([first, second], axis=1)


def put_halves(ref, cluster, row):
    ref[pl.ds(2 * cluster, 1), :] = row[:, :128]
    ref[pl.ds(2 * cluster + 1, 1), :] = row[:, 128:]


def squared_norm(cells):
    wide = cells.astype(jnp.float32)
    return jnp.sum(wide * wide, axis=0, keepdims=True)


def far_offset(axis, j, n):
    if axis == "tgt":
        return n // 2 + lax.div(j + 1, 2) * (1 - 2 * lax.rem(j, 2))
    i = lax.div(j, 2)
    near = n // 4 + lax.div(i + 1, 2) * (2 * lax.rem(i, 2) - 1)
    return near + lax.rem(j, 2) * (n - 2 * near)


def aux_rows(row, offset, other):
    at = lax.broadcasted_iota(jnp.int32, (AUX, TILE), 0)
    high, mid, low = split3(row)
    out = jnp.where((at >= other) & (at < other + 3), 1.0, 0.0)
    out = jnp.where(at == offset, high, out)
    out = jnp.where(at == offset + 1, mid, out)
    out = jnp.where(at == offset + 2, low, out)
    return out.astype(jnp.bfloat16)


def kernel(
    sizes, table, xs, ys, x_mass, y_mass, u_out, v_out, x_norm_out, y_norm_out, out,
    masses, u0, v0, u1, v1, u2, v2, parts, helds, slot_m, slot_s, slot_n, slot_d, send_a, send_y,
    first_y, ring_a, ring_b, last_y, kept, local, *sems,
):
    n_src, n_tgt, slots = sizes
    step = math.gcd(slots, 128)
    clusters, features = xs.shape[:2]
    me_src, me_tgt = lax.axis_index("src"), lax.axis_index("tgt")
    barrier = pltpu.get_barrier_semaphore()
    for axis, me, n in (("tgt", me_tgt, n_tgt), ("src", me_src, n_src)):
        for k in range(1, n):
            pl.semaphore_signal(barrier, inc=1, device_id={axis: lax.rem(me + k, n)}, device_id_type=MESH)

    fetches = []
    for i, (mass, me, n) in enumerate(((x_mass, me_tgt, n_tgt), (y_mass, me_src, n_src))):
        rows = 2 * clusters // n
        fetch = pltpu.make_async_copy(
            mass.at[pl.ds(pl.multiple_of(me * rows, rows), rows)], masses.at[i], local.at[i])
        fetch.start()
        fetches.append(fetch)
    slot_m[slots] = jnp.full((SUB, TILE), EMPTY, jnp.float32)
    slot_s[slots] = jnp.zeros((SUB, TILE), jnp.float32)
    slot_n[slots] = jnp.zeros((features, TILE), jnp.float32)
    slot_d[pl.ds(slots, SUB), :] = jnp.zeros((SUB, TILE), jnp.float32)

    def entry(which, p):
        return table[which * slots + p]

    def scaled(cells, ref):
        return cells * jnp.bfloat16(4.0) if ref is xs else cells

    def sweep(kind, first, sub_cells, lane_cells, sub_pot, lane_pot):
        def tile(p, carry):
            a, b, keep = entry(first, p), entry(first + 1, p), entry(first + 2, p)
            sub, lane = sub_cells[a], lane_cells[b]
            left = jnp.concatenate([scaled(sub, sub_cells), aux_rows(cluster_row(sub_pot, a), 0, 3)], axis=0)
            right = jnp.concatenate([scaled(lane, lane_cells), aux_rows(cluster_row(lane_pot, b), 3, 0)], axis=0)
            score = lax.dot_general(left, right, (((0,), (0,)), ((), ())), preferred_element_type=jnp.float32)
            hold = keep.astype(jnp.float32)
            if kind == "max":
                score = score.reshape(CHUNKS, TILE // SUB // CHUNKS, SUB, TILE)
                best = [jnp.max(score[q], axis=0) for q in range(CHUNKS)]
                old = carry[0] * hold + (1.0 - hold) * EMPTY
                new = functools.reduce(jnp.maximum, best, old)
                total = carry[1] * hold * jnp.exp(old - new)
                for q in range(CHUNKS):
                    total = total + jnp.sum(jnp.exp(score[q] - best[q][None]), axis=0) * jnp.exp(best[q] - new)
                slot_m[p] = new
                slot_s[p] = total
                return new, total
            weight = jnp.exp(score)
            if kind == "sum":
                total = carry[0] * hold + jnp.sum(weight.reshape(TILE // SUB, SUB, TILE), axis=0)
                slot_s[p] = total
                return (total,)
            high = weight.astype(jnp.bfloat16)
            low = (weight - high.astype(jnp.float32)).astype(jnp.bfloat16)
            ones = jnp.where(lax.broadcasted_iota(jnp.int32, (AUX, TILE), 0) == 0, 1.0, 0.0).astype(jnp.bfloat16)
            cells = jnp.concatenate([sub, ones], axis=0)
            moved = jnp.dot(cells, high, preferred_element_type=jnp.float32)
            moved = moved + jnp.dot(cells, low, preferred_element_type=jnp.float32)
            total = carry[0] * hold + moved[:features]
            weights = carry[1] * hold + moved[features:features + 1]
            slot_n[p] = total
            slot_d[pl.ds(p, 1), :] = weights
            return total, weights

        def group(g, carry):
            for r in range(step):
                carry = tile(g * step + r, carry)
            return carry

        empty = jnp.zeros((SUB, TILE), jnp.float32)
        if kind == "max":
            start = (empty + EMPTY, empty)
        elif kind == "sum":
            start = (empty,)
        else:
            start = (jnp.zeros((features, TILE), jnp.float32), jnp.zeros((1, TILE), jnp.float32))
        lax.fori_loop(0, slots // step, group, start)

    def reduce(kind, which, axis, me, n, last, old, new, meanwhile):
        part, held = parts.at[which], helds.at[which]
        per = clusters // n
        lanes = lax.broadcasted_iota(jnp.int32, (1, TILE), 1)

        def shard(peer):
            return pl.ds(pl.multiple_of(peer * per, per), per)

        def finish(peer):
            rows = []
            for r in range(per):
                at = entry(last, peer * per + r)
                if kind == "max":
                    best = jnp.max(slot_m[at], axis=0, keepdims=True)
                    row = jnp.sum(slot_s[at] * jnp.exp(slot_m[at] - best), axis=0, keepdims=True)
                    rows.append(best + jnp.log(jnp.where(row > 0.0, row, 1.0)))
                else:
                    rows.append(jnp.sum(slot_s[at], axis=0, keepdims=True))
            part[shard(peer), :] = jnp.concatenate(rows, axis=0)

        def copy(j, phase):
            k = far_offset(axis, j, n)
            peer = lax.rem(me + k, n)
            mine = shard(me)
            src_ref, dst_ref = (part.at[shard(peer)], held.at[k]) if phase == 0 else (new.at[mine], new.at[mine])
            return pltpu.make_async_remote_copy(
                src_ref=src_ref, dst_ref=dst_ref,
                send_sem=sems[2 * phase].at[which, k], recv_sem=sems[2 * phase + 1].at[which, k],
                device_id={axis: peer}, device_id_type=MESH)

        if which == 0:
            pl.semaphore_wait(barrier, n_src + n_tgt - 2)

        @pl.loop(0, n - 1)
        def _(j):
            finish(lax.rem(me + far_offset(axis, j, n), n))
            copy(j, 0).start()

        finish(me)
        meanwhile()
        if which < 2:
            fetches[which].wait()
        mass = masses.at[which % 2]
        count = (SRC_COUNT, TGT_COUNT)[which % 2]
        rows = []
        for r in range(per):
            rows.append(jnp.where(lanes < entry(count, me * per + r), jnp.log(halves_row(mass, r)), EMPTY))
        logmass = jnp.concatenate(rows, axis=0)

        @pl.loop(0, n - 1)
        def _(j):
            copy(j, 0).wait_recv()

        mine = shard(me)
        own = part[mine, :]
        if kind == "max":
            best = own
            for k in range(1, n):
                best = jnp.maximum(best, held[k])
            total = jnp.exp(own - best)
            for k in range(1, n):
                total = total + jnp.exp(held[k] - best)
            lse = best + jnp.log(total)
        else:
            total = own
            for k in range(1, n):
                total = total + held[k]
            lse = jnp.log(jnp.where(total > 0.0, total, 1.0))
        new[mine, :] = jnp.where(logmass > 0.5 * EMPTY, old[mine, :] + logmass - lse, EMPTY)

        @pl.loop(0, n - 1)
        def _(j):
            copy(j, 1).start()

        @pl.loop(0, n - 1)
        def _(j):
            copy(j, 0).wait_send()

        @pl.loop(0, n - 1)
        def _(j):
            copy(j, 1).wait()

    lane = lax.broadcasted_iota(jnp.int32, (1, TILE), 1)
    u0[...] = jnp.zeros(u0.shape, jnp.float32)

    @pl.loop(0, clusters // (2 * SUB))
    def _(g):
        rows = []
        for r in range(2 * SUB):
            c = g * 2 * SUB + r
            rows.append(jnp.where(lane < entry(TGT_COUNT, c), -2.0 * squared_norm(ys[c]), EMPTY))
        v0[pl.ds(pl.multiple_of(g * 2 * SUB, 2 * SUB), 2 * SUB), :] = jnp.concatenate(rows, axis=0)

    def norms(part):
        groups = clusters // SUB // 2

        @pl.loop(part * groups, part * groups + groups)
        def _(g):
            for r in range(SUB):
                c = g * SUB + r
                put_halves(x_norm_out, c, squared_norm(xs[c]))
                put_halves(y_norm_out, c, -0.5 * cluster_row(v0, c))

    def nothing():
        pass

    def write_u():
        @pl.loop(0, clusters // SUB)
        def _(g):
            for r in range(SUB):
                put_halves(u_out, g * SUB + r, cluster_row(u2, g * SUB + r))

    sweep("max", ROW_SUB, ys, xs, v0, u0)
    reduce("max", 0, "tgt", me_tgt, n_tgt, ROW_LAST, u0, u1, lambda: norms(0))
    sweep("max", COL_SUB, xs, ys, u1, v0)
    reduce("max", 1, "src", me_src, n_src, COL_LAST, v0, v1, lambda: norms(1))
    sweep("sum", ROW_SUB, ys, xs, v1, u1)
    reduce("sum", 2, "tgt", me_tgt, n_tgt, ROW_LAST, u1, u2, nothing)
    sweep("sum", COL_SUB, xs, ys, u2, v1)
    reduce("sum", 3, "src", me_src, n_src, COL_LAST, v1, v2, write_u)
    sweep("map", ROW_SUB, ys, xs, v2, u2)

    n, nz = n_tgt, n_tgt // NY
    z, y = me_tgt // NY, lax.rem(me_tgt, NY)
    other = NY - 1 - y
    sides = (other, y)
    per = out.shape[1] // TILE
    half = per // 2
    sign = (1, -1)
    far = nz // 2
    hops = ((far, nz - 1 - far), (nz - 1 - far, far))
    partner = z * NY + other

    def toward(d):
        return lax.rem(z + sign[d] + nz, nz) * NY + y

    def block(g, d, hop):
        return lax.rem(z + sign[d] * (hops[g][d] - hop) + nz, nz)

    def own(at, side, g, c):
        slot = entry(ROW_LAST, (at * NY + side) * per + g * half + c)
        return slot_n[slot], slot_d[pl.ds(slot, 1), :]

    def plus(*terms):
        return tuple(functools.reduce(jnp.add, term) for term in zip(*terms))

    def copy(src, dst, sem, k, peer):
        made = pltpu.make_async_remote_copy(
            src_ref=src, dst_ref=dst, send_sem=sems[2 * sem].at[k], recv_sem=sems[2 * sem + 1].at[k],
            device_id={"tgt": peer}, device_id_type=MESH)
        made.start()
        return made

    def exponent_of(value):
        return jnp.ceil(jnp.log2(jnp.maximum(value, 1e-30)))

    def coded(value, exponent):
        return jnp.floor(value * (jnp.exp2(-exponent) * CODE) + 0.5)

    def encode(ref, values):
        rows = [[], [], []]
        for c in range(half):
            value, weight = values(c)
            exponent = exponent_of(jnp.max(jnp.abs(value), axis=0, keepdims=True))
            code = coded(value, exponent)
            ref[c * features:(c + 1) * features, :] = code.astype(jnp.int32).astype(jnp.int16)
            at = exponent_of(weight)
            for row, item in zip(rows, (exponent, at, coded(weight, at))):
                row.append(item)
        spare = [jnp.zeros((AUX - 3 * half, TILE), jnp.float32)]
        block = jnp.concatenate(rows[0] + rows[1] + rows[2] + spare, axis=0)
        ref[half * features:half * features + AUX, :] = block.astype(jnp.int32).astype(jnp.int16)

    def decoder(ref):
        block = ref[half * features:half * features + AUX, :].astype(jnp.int32).astype(jnp.float32)
        scale = jnp.exp2(block[:2 * half]) * (1.0 / CODE)

        def decode(c):
            code = ref[c * features:(c + 1) * features, :].astype(jnp.int32).astype(jnp.float32)
            weight = block[2 * half + c:2 * half + c + 1] * scale[half + c:half + c + 1]
            return code * scale[c:c + 1], weight

        return decode

    pieces = [(d, hop) for hop in range(far) for d in range(2) if hop < hops[1][d]]
    over_y = {}
    over_a = {}
    over_b = {}

    def send_piece(i, at):
        encode(send_y.at[i], lambda c: own(at, other, 1, c))
        over_y[i] = copy(send_y.at[i], first_y.at[i], 2, i, partner)

    def start_a(d, s):
        encode(send_a.at[d, s], lambda c: own(block(0, d, 0), sides[s], 0, c))
        over_a[d, s, 0] = copy(send_a.at[d, s], ring_a.at[d, 0, s], 3, (d * NY + s) * far, toward(d))

    for d in range(2):
        start_a(d, 0)
    for i in range(2):
        send_piece(i, block(1, *pieces[i]))
    for d in range(2):
        start_a(d, 1)
    for i in range(2, nz - 1):
        send_piece(i, block(1, *pieces[i]))
    send_piece(nz - 1, z)

    def step_b(d, hop):
        i = pieces.index((d, hop))
        over_y[i].wait_recv()
        parts_of = [decoder(first_y.at[i])]
        if hop > 0:
            over_b[d, hop - 1].wait_recv()
            parts_of.append(decoder(ring_b.at[d, hop - 1]))
        at = block(1, d, hop)
        encode(first_y.at[i], lambda c: plus(own(at, y, 1, c), *(part(c) for part in parts_of)))
        over_b[d, hop] = copy(first_y.at[i], ring_b.at[d, hop], 4, d * far + hop, toward(d))

    def step_a(d, s, hop):
        over_a[d, s, hop - 1].wait_recv()
        held = ring_a.at[d, hop - 1, s]
        arrived = decoder(held)
        at = block(0, d, hop)
        encode(held, lambda c: plus(arrived(c), own(at, sides[s], 0, c)))
        over_a[d, s, hop] = copy(held, ring_a.at[d, hop, s], 3, (d * NY + s) * far + hop, toward(d))

    def arrived_a(s):
        both = []
        for d in range(2):
            over_a[d, s, hops[0][d] - 1].wait_recv()
            both.append(decoder(ring_a.at[d, hops[0][d] - 1, s]))
        return lambda c: plus(both[0](c), both[1](c), own(z, sides[s], 0, c))

    for hop in range(1, far + 1):
        for d in range(2):
            if hop < hops[0][d]:
                step_a(d, 0, hop)
        if hop == far:
            encode(kept, arrived_a(0))
            over_last = copy(kept, last_y, 5, 0, partner)
        for d in range(2):
            if hop - 1 < hops[1][d]:
                step_b(d, hop - 1)
        for d in range(2):
            if hop < hops[0][d]:
                step_a(d, 1, hop)

    @pl.loop(0, clusters // SUB)
    def _(g):
        for r in range(SUB):
            put_halves(v_out, g * SUB + r, cluster_row(v2, g * SUB + r))

    def put(c, sums):
        value, weight = sums
        out[:, c * TILE:(c + 1) * TILE] = value / jnp.where(weight > 0.0, weight, 1.0)

    over_y[nz - 1].wait_recv()
    parts_b = [decoder(first_y.at[nz - 1])]
    for d in range(2):
        over_b[d, hops[1][d] - 1].wait_recv()
        parts_b.append(decoder(ring_b.at[d, hops[1][d] - 1]))
    for c in range(half):
        put(half + c, plus(own(z, y, 1, c), *(part(c) for part in parts_b)))
    mine = arrived_a(1)
    over_last.wait_recv()
    last = decoder(last_y)
    for c in range(half):
        put(c, plus(mine(c), last(c)))
    for made in [over_last] + list(over_y.values()) + list(over_a.values()) + list(over_b.values()):
        made.wait_send()


def transport(n_src, n_tgt, slots, table, xs, ys, x_mass, y_mass):
    clusters, features = xs.shape[:2]
    per, nz = clusters // n_tgt, n_tgt // NY
    far = nz // 2
    f32 = jnp.float32
    vmem = pl.BlockSpec(memory_space=pltpu.VMEM)
    smem = pl.BlockSpec(memory_space=pltpu.SMEM)
    hbm = pl.BlockSpec(memory_space=pl.ANY)
    dma = pltpu.SemaphoreType.DMA
    most = max(n_src, n_tgt)
    sems = [dma((4, most))] * 4
    for many in (nz, 2 * NY * far, 2 * far, 1):
        sems += [dma((many,))] * 2
    flat = jax.ShapeDtypeStruct((2 * clusters, TILE // 2), f32)
    row = pltpu.VMEM((clusters, TILE), f32)
    coded = (per // 2 * features + AUX, TILE)

    def codes(*many):
        return pltpu.VMEM(many + coded, jnp.int16)

    scratch = [pltpu.VMEM((2, 2 * clusters // n_tgt, TILE // 2), f32)] + [row] * 6 + [
        pltpu.VMEM((4, clusters, TILE), f32),
        pltpu.VMEM((4, most, clusters // min(n_src, n_tgt), TILE), f32),
        pltpu.VMEM((slots + 1, SUB, TILE), f32),
        pltpu.VMEM((slots + 1, SUB, TILE), f32),
        pltpu.VMEM((slots + 1, features, TILE), f32),
        pltpu.VMEM((slots + SUB, TILE), f32),
        codes(2, NY),
        codes(nz),
        codes(nz),
        codes(2, far, NY),
        codes(2, far),
        codes(),
        codes(),
        dma((2,)),
    ]
    return pl.pallas_call(
        functools.partial(kernel, (n_src, n_tgt, slots)),
        out_shape=(flat,) * 4 + (jax.ShapeDtypeStruct((features, per * TILE), f32),),
        in_specs=[smem, vmem, vmem, hbm, hbm],
        out_specs=(vmem,) * 5,
        scratch_shapes=scratch + sems,
        compiler_params=pltpu.CompilerParams(collective_id=0, has_side_effects=True, vmem_limit_bytes=40 * MIB),
        name="transport",
    )(table, xs, ys, x_mass, y_mass)


def pair_tables(pair_lists, tgt_block, per_block, slots, counts):
    width = pair_lists.shape[1]
    flat = pair_lists.reshape(-1)
    chosen = flat // per_block == tgt_block
    targets = flat % per_block
    sources = jnp.arange(flat.shape[0], dtype=jnp.int32) // width
    places = jnp.arange(slots, dtype=jnp.int32)
    rank = jnp.cumsum(chosen.astype(jnp.int32)) - 1
    matches = (rank[None, :] == places[:, None]) & chosen[None, :]
    row_src = jnp.sum(jnp.where(matches, sources[None, :], 0), axis=1)
    row_tgt = jnp.sum(jnp.where(matches, targets[None, :], 0), axis=1)
    live = jnp.sum(matches.astype(jnp.int32), axis=1) > 0
    before = (row_tgt[None, :] < row_tgt[:, None]) | (
        (row_tgt[None, :] == row_tgt[:, None]) & (places[None, :] < places[:, None]))
    order = jnp.where(live, jnp.sum((before & live[None, :]).astype(jnp.int32), axis=1), places)
    moves = order[None, :] == places[:, None]
    col_src = jnp.sum(jnp.where(moves, row_src[None, :], 0), axis=1)
    col_tgt = jnp.sum(jnp.where(moves, row_tgt[None, :], 0), axis=1)

    def ends(kept):
        same = jnp.concatenate([jnp.zeros((1,), jnp.int32), (kept[1:] == kept[:-1]).astype(jnp.int32)])
        found = (kept[None, :] == places[:, None]) & live[None, :]
        last = jnp.max(jnp.where(found, places[None, :], -1), axis=1)
        return same, jnp.where(last < 0, slots, last)

    row_keep, row_last = ends(row_src)
    col_keep, col_last = ends(col_tgt)
    return jnp.concatenate([row_tgt, row_src, row_keep, row_last, col_src, col_tgt, col_keep, col_last] + counts)


def shards(source_cells, target_cells, source_mass, target_mass, source_count, target_count, pair_lists):
    n_src, n_tgt = lax.axis_size("src"), lax.axis_size("tgt")
    slots = 2 * pair_lists.size // n_tgt
    table = pair_tables(
        pair_lists, lax.axis_index("tgt"), target_count.shape[0], slots, [source_count, target_count])
    xs, ys = (
        jnp.transpose(cells.reshape(cells.shape[0], -1, TILE), (1, 0, 2)) for cells in (source_cells, target_cells))
    u, v, x_norm, y_norm, mapped = transport(
        n_src, n_tgt, slots, table, xs, ys,
        source_mass.reshape(-1, TILE // 2), target_mass.reshape(-1, TILE // 2))
    source_pot = jnp.where(u > 0.5 * EMPTY, 0.5 * u + x_norm, 0.0)
    target_pot = jnp.where(v > 0.5 * EMPTY, 0.5 * v + y_norm, 0.0)
    return source_pot.reshape(-1), target_pot.reshape(-1), mapped


def solution(mesh):
    return jax.shard_map(
        shards,
        mesh=mesh,
        in_specs=(P(None, "src"), P(None, "tgt"), P("src"), P("tgt"), P("src"), P("tgt"), P("src", None)),
        out_specs=(P("src"), P("tgt"), P(None, ("src", "tgt"))),
        check_vma=False,
    )
```
